32 devices in a mesh: filt: 2 (over core), row: 4 (over y, x), col: 4 (over z).
Axes of the slice: x: 2, y: 2, z: 4, core: 2. Of those that a mesh axis runs over, the one named last changes fastest.
Arguments:
- particles: bfloat16 [3072, 256], P(('filt', 'row', 'col')), parts along dimension 0, may hold values from -6 to 6
- cotangent: bfloat16 [3072, 256], P(('filt', 'row', 'col')), parts along dimension 0, may hold values from -3 to 3
- row_potential: bfloat16 [3072], P(('filt', 'row', 'col')), parts along dimension 0, may hold values from -0.099609375 to 0.099609375
- col_potential: bfloat16 [3072], P(('filt', 'row', 'col')), parts along dimension 0, may hold values from -0.099609375 to 0.099609375
- weights: bfloat16 [3072], P(('filt', 'row', 'col')), parts along dimension 0, may hold values from 0.5 to 18
Outputs:
- grad_particles: bfloat16 [3072, 256], P(('filt', 'row', 'col')), parts along dimension 0
- grad_weights: float32 [3072], P(('filt', 'row', 'col')), parts along dimension 0
The draws below stay inside these ranges and needn't reach their ends.
There are 2 independent parts, one for each index of `filt`. The reference program is written for one: setup_inputs(seed, part) draws one part's arguments, and reference() takes and returns one part's arrays. A program takes and returns all parts, laid end to end along the dimension named above; each array names one. Nothing has to cross between parts.
All inputs are finite; a program needn't handle non-finite values.
Results may differ from the reference program's by a relative error of at most 0.02.
Values may be sent and summed in bfloat16 or wider, within the bound.
A program may use at most 64 MiB of HBM per device.

```python
import math
import jax
import jax.numpy as jnp
from jax import lax

D = 256
ITERS = 4
PARTICLES = 1536


def draw_particles(key, part):
    groups = max(PARTICLES // 64, 1)
    key_member = jax.random.fold_in(key, 11)
    key_spot = jax.random.fold_in(key, 12)
    key_freq = jax.random.fold_in(key, 13)
    key_phase = jax.random.fold_in(key, 14)
    key_centre = jax.random.fold_in(key, 15)
    key_jitter = jax.random.fold_in(key, 16)
    member = jax.random.randint(key_member, (PARTICLES,), 0, groups)
    spot = jax.random.randint(key_spot, (PARTICLES,), 0, 32).astype(jnp.float32)
    freq = jax.random.uniform(key_freq, (groups, D), jnp.float32, 0.15, 0.42)
    phase = jax.random.uniform(key_phase, (groups, D), jnp.float32, -math.pi, math.pi)
    centre = jax.random.normal(key_centre, (groups, D), jnp.float32)
    jitter = jax.random.normal(key_jitter, (PARTICLES, D), jnp.float32)
    values = 0.8 * centre[member] + 1.2 * jnp.sin(freq[member] * spot[:, None] + phase[member]) + 0.15 * jitter
    return jnp.clip(values, -6.0, 6.0).astype(jnp.bfloat16)


def draw_weights(key, part):
    uniform_draw = jax.random.uniform(key, (PARTICLES,), jnp.float32, 0.0, 1.0)
    ramp = jnp.arange(PARTICLES, dtype=jnp.float32) / max(PARTICLES - 1, 1)
    values = jnp.exp(jnp.log(0.5) + uniform_draw * jnp.log(4.0)) * (1.0 + 2.0 * ramp)
    return values.astype(jnp.bfloat16)


def level_of(stream_key, extent, split, smallest, high):
    loudness = 1.0
    for axis_at, blocks in split:
        heights = jax.random.uniform(jax.random.fold_in(jax.random.fold_in(stream_key, 6), axis_at), (blocks,), jnp.float32, smallest / len(split), high / len(split))
        loudness = loudness * jnp.repeat(jnp.exp(heights), extent[axis_at] // blocks).reshape((-1,) + (1,) * (len(extent) - 1 - axis_at))
    return loudness


def normal_values(rng, dims, deviation, reach, split=(), kind=jnp.bfloat16):
    factor_of = level_of(rng, dims, split, -0.22, 0.18) if split else 1.0
    result = jax.random.normal(rng, dims, jnp.float32) * deviation * factor_of
    return jnp.minimum(jnp.maximum(result, -reach), reach).astype(kind)


def setup_inputs(seed: int = 0, part: int = 0) -> dict:
    streams_of = jax.random.split(jax.random.key(seed), 6)
    part_splits = jax.random.split(jax.random.fold_in(streams_of[5], part), 6)
    return {
        "particles": draw_particles(jax.random.fold_in(jax.random.fold_in(streams_of[5], part), 71), part),
        "cotangent": normal_values(part_splits[1], (PARTICLES, D), 0.5, 3.0, ((0, 16),)),
        "row_potential": jnp.clip(jax.random.uniform(part_splits[2], (PARTICLES,), jnp.float32, -0.099609375, 0.099609375) * level_of(part_splits[2], (PARTICLES,), ((0, 16),), -0.4, 0.0), -0.099609375, 0.099609375).astype(jnp.bfloat16),
        "col_potential": jnp.clip(jax.random.uniform(part_splits[3], (PARTICLES,), jnp.float32, -0.099609375, 0.099609375) * level_of(part_splits[3], (PARTICLES,), ((0, 16),), -0.4, 0.0), -0.099609375, 0.099609375).astype(jnp.bfloat16),
        "weights": draw_weights(jax.random.fold_in(jax.random.fold_in(streams_of[5], part), 71), part),
    }


EPS = 0.09


def plan_rows(part_blk, pot_blk, sq_blk, particles, sq_all, col_pot):
    cross = jnp.dot(part_blk, particles.T, preferred_element_type=jnp.float32)
    cost = (sq_blk[:, None] + sq_all[None, :] - 2.0 * cross) / (2.0 * D)
    return jnp.exp((pot_blk[:, None] + col_pot[None, :] - cost) / EPS)


def reference(particles, cotangent, row_potential, col_potential, weights):
    rsize = math.gcd(PARTICLES, 512)
    nblocks = PARTICLES // rsize
    pfloat = particles.astype(jnp.float32)
    sq_all = jnp.sum(pfloat * pfloat, axis=1)
    fpot = row_potential.astype(jnp.float32)
    gpot = col_potential.astype(jnp.float32)
    items = (particles.reshape(nblocks, rsize, D), fpot.reshape(nblocks, rsize), sq_all.reshape(nblocks, rsize))

    def first(carry, item):
        part_blk, pot_blk, sq_blk = item
        plan = plan_rows(part_blk, pot_blk, sq_blk, particles, sq_all, gpot)
        grads = jnp.dot(part_blk, cotangent.T, preferred_element_type=jnp.float32)
        weighted = plan * grads
        return (carry[0] + jnp.sum(plan, axis=0), carry[1] + jnp.sum(weighted, axis=0)), (jnp.sum(plan, axis=1), jnp.sum(weighted, axis=1))

    zeros_n = jnp.zeros((PARTICLES,), jnp.float32)
    (colmass, colph), (rowmass, rowph) = lax.scan(first, (zeros_n, zeros_n), items)
    psi = zeros_n
    phi = jnp.zeros((nblocks, rsize), jnp.float32)
    for step in range(ITERS):
        def sweep(acc, item):
            part_blk, pot_blk, sq_blk, mass_blk, ph_blk = item
            plan = plan_rows(part_blk, pot_blk, sq_blk, particles, sq_all, gpot)
            phi_blk = -(ph_blk + jnp.dot(plan, psi, precision=lax.Precision.HIGHEST)) / mass_blk
            return acc + jnp.dot(phi_blk, plan, precision=lax.Precision.HIGHEST), phi_blk

        accum, phi = lax.scan(sweep, zeros_n, items + (rowmass, rowph))
        psi = -(colph + accum) / colmass

    def last(acc, item):
        part_blk, pot_blk, sq_blk, phi_blk = item
        plan = plan_rows(part_blk, pot_blk, sq_blk, particles, sq_all, gpot)
        grads = jnp.dot(part_blk, cotangent.T, preferred_element_type=jnp.float32)
        mixed = plan * (grads + phi_blk[:, None] + psi[None, :])
        qrow = jnp.sum(mixed, axis=1)
        plan_bf = plan.astype(jnp.bfloat16)
        mixed_bf = mixed.astype(jnp.bfloat16)
        rowterm = jnp.dot(plan_bf, cotangent, preferred_element_type=jnp.float32)
        rowterm = rowterm + (jnp.dot(mixed_bf, particles, preferred_element_type=jnp.float32) - qrow[:, None] * part_blk.astype(jnp.float32)) / (D * EPS)
        return acc + jnp.dot(mixed_bf.T, part_blk, preferred_element_type=jnp.float32), rowterm

    colacc, rowterms = lax.scan(last, jnp.zeros((PARTICLES, D), jnp.float32), items + (phi,))
    grad_particles = (rowterms.reshape(PARTICLES, D) + colacc / (D * EPS)).astype(jnp.bfloat16)
    phi_flat = phi.reshape(PARTICLES)
    wfloat = weights.astype(jnp.float32)
    total = jnp.sum(wfloat)
    wphi = jnp.sum(wfloat * phi_flat)
    grad_weights = -(PARTICLES / total) * (phi_flat - wphi / total)
    return grad_particles, grad_weights
```

```python
import functools
import jax
import jax.numpy as jnp
from jax import lax
from jax.experimental import pallas as pl
from jax.experimental.pallas import tpu as pltpu
from jax.sharding import PartitionSpec as P

ITERS = 4


EPS = 0.09


def local_general(particles, cotangent, row_potential, col_potential, weights):
    row_parts, row_fpot, row_wts = (
        lax.all_gather(particles, "col", axis=0, tiled=True),
        lax.all_gather(row_potential, "col", axis=0, tiled=True),
        lax.all_gather(weights, "col", axis=0, tiled=True),
    )
    col_parts, col_grads, col_gpot = (
        lax.all_gather(particles, "row", axis=0, tiled=True),
        lax.all_gather(cotangent, "row", axis=0, tiled=True),
        lax.all_gather(col_potential, "row", axis=0, tiled=True),
    )
    own = particles.shape[0]
    width = particles.shape[1]
    rows = row_parts.shape[0]
    cols = col_parts.shape[0]
    blk = 512 if rows % 512 == 0 else rows
    count = rows // blk
    row_float = row_parts.astype(jnp.float32)
    row_sq = jnp.sum(row_float * row_float, axis=1)
    col_float = col_parts.astype(jnp.float32)
    col_sq = jnp.sum(col_float * col_float, axis=1)
    fpot = row_fpot.astype(jnp.float32)
    gpot = col_gpot.astype(jnp.float32)
    stacked = jnp.concatenate([col_parts, col_grads], axis=0)
    items = (
        row_parts.reshape(count, blk, width),
        fpot.reshape(count, blk),
        row_sq.reshape(count, blk),
    )

    def plan_from(cross, pot_blk, sq_blk):
        cost = (sq_blk[:, None] + col_sq[None, :] - 2.0 * cross) / (2.0 * width)
        return jnp.exp((pot_blk[:, None] + gpot[None, :] - cost) / EPS)

    def plan_only(part_blk, pot_blk, sq_blk):
        cross = jnp.einsum("rd,cd->rc", part_blk, col_parts, preferred_element_type=jnp.float32)
        return plan_from(cross, pot_blk, sq_blk)

    def first(carry, item):
        part_blk, pot_blk, sq_blk = item
        both = jnp.einsum("rd,cd->rc", part_blk, stacked, preferred_element_type=jnp.float32)
        plan = plan_from(both[:, :cols], pot_blk, sq_blk)
        weighted = plan * both[:, cols:]
        return (
            (carry[0] + jnp.sum(plan, axis=0), carry[1] + jnp.sum(weighted, axis=0)),
            (jnp.sum(plan, axis=1), jnp.sum(weighted, axis=1)),
        )

    zeros_c = jnp.zeros((cols,), jnp.float32)
    (colmass_part, colph_part), (rowmass_part, rowph_part) = lax.scan(
        first, (zeros_c, zeros_c), items
    )
    rowmass, rowph = lax.psum((rowmass_part.reshape(rows), rowph_part.reshape(rows)), "col")
    colmass, colph = lax.psum((colmass_part, colph_part), "row")
    psi = zeros_c
    phi = jnp.zeros((rows,), jnp.float32)
    for step in range(ITERS):

        def apply_rows(carry, item):
            plan = plan_only(item[0], item[1], item[2])
            return (carry, jnp.dot(plan, psi, precision=lax.Precision.HIGHEST))

        unused, row_apply = lax.scan(apply_rows, jnp.zeros((), jnp.float32), items)
        row_total = lax.psum(row_apply.reshape(rows), "col")
        phi = -(rowph + row_total) / rowmass

        def apply_cols(acc, item):
            plan = plan_only(item[0], item[1], item[2])
            return (acc + jnp.dot(item[3], plan, precision=lax.Precision.HIGHEST), None)

        col_apply, unused_out = lax.scan(apply_cols, zeros_c, items + (phi.reshape(count, blk),))
        col_total = lax.psum(col_apply, "row")
        psi = -(colph + col_total) / colmass

    def last(acc, item):
        part_blk, pot_blk, sq_blk, phi_blk = item
        both = jnp.einsum("rd,cd->rc", part_blk, stacked, preferred_element_type=jnp.float32)
        plan = plan_from(both[:, :cols], pot_blk, sq_blk)
        mixed = plan * (both[:, cols:] + phi_blk[:, None] + psi[None, :])
        qrow = jnp.sum(mixed, axis=1)
        plan_bf = plan.astype(jnp.bfloat16)
        mixed_bf = mixed.astype(jnp.bfloat16)
        rowterm = jnp.dot(plan_bf, col_grads, preferred_element_type=jnp.float32)
        rowterm = rowterm + (
            jnp.dot(mixed_bf, col_parts, preferred_element_type=jnp.float32)
            - qrow[:, None] * part_blk.astype(jnp.float32)
        ) / (width * EPS)
        return (
            acc + jnp.einsum("rc,rd->cd", mixed_bf, part_blk, preferred_element_type=jnp.float32),
            rowterm,
        )

    col_acc, row_terms = lax.scan(
        last, jnp.zeros((cols, width), jnp.float32), items + (phi.reshape(count, blk),)
    )
    row_terms = row_terms.reshape(rows, width)
    start = lax.axis_index("col") * own
    summed = lax.psum(row_terms.astype(jnp.bfloat16), "col").astype(jnp.float32)
    row_own = lax.dynamic_slice_in_dim(summed, start, own, 0)
    col_own = lax.psum_scatter(
        col_acc.astype(jnp.bfloat16), "row", scatter_dimension=0, tiled=True
    ).astype(jnp.float32)
    grad_particles = (row_own + col_own / (width * EPS)).astype(jnp.bfloat16)
    phi_own = lax.dynamic_slice_in_dim(phi, start, own, 0)
    own_wts = weights.astype(jnp.float32)
    total, wphi = lax.psum((jnp.sum(own_wts), jnp.sum(own_wts * phi_own)), ("row", "col"))
    count_all = rows * lax.axis_size("row")
    grad_weights = -(count_all / total) * (phi_own - wphi / total)
    return (grad_particles, grad_weights)


LANES = 128
SUBL = 8
CHUNK = 256
PLAN_BYTES = 24 * 1024 * 1024


def fold(block):
    return jnp.sum(block.reshape(block.shape[0] // SUBL, SUBL, block.shape[1]), axis=0)


def wide(column):
    return jnp.broadcast_to(column, (column.shape[0], LANES))


def fused_kernel(
    ncol, x_ref, gy_ref, pot_ref, gp_ref, gw_ref,
    x_all, gy_all, pots, plan, a_col, f_b, w_col, r_col, hr_col, phi_col, a_lane,
    zs, zr, xs, xr, ps, pr,
):
    nrow = 4
    own = x_ref.shape[0]
    half = own // 2
    width = x_ref.shape[1]
    blocks = nrow * ncol
    total = own * blocks
    tiles = total // LANES
    me_r = lax.axis_index("row")
    me_c = lax.axis_index("col")
    me = me_r * ncol + me_c
    xn = me_r + 1 - 2 * (me_r % 2)
    yn = (me_r + 2) % nrow
    dn = (xn + 2) % nrow
    peers = [(dr, dc) for dr in range(nrow) for dc in range(ncol) if dr or dc]

    def at(row, col, part=None):
        base = (row * ncol + col) * own
        if part is None:
            return pl.ds(pl.multiple_of(base, 32), own)
        return pl.ds(pl.multiple_of(base + part * half, 16), half)

    def dev(row, col):
        return {"row": row, "col": col}

    barrier = pltpu.get_barrier_semaphore()
    for dr, dc in peers:
        pl.semaphore_signal(
            barrier, inc=1, device_id=dev((me_r + dr) % nrow, (me_c + dc) % ncol),
            device_id_type=pl.DeviceIdType.MESH,
        )
    x_all[at(me_r, me_c), :] = x_ref[...]
    gy_all[at(me_r, me_c), :] = gy_ref[...]
    pots[pl.ds(pl.multiple_of(me * 16, 16), 16), :] = pot_ref[...]
    pl.semaphore_wait(barrier, len(peers))

    def copy(src, dst, ssem, rsem, row, col):
        c = pltpu.make_async_remote_copy(
            src_ref=src, dst_ref=dst, send_sem=ssem, recv_sem=rsem,
            device_id=dev(row, col), device_id_type=pl.DeviceIdType.MESH,
        )
        c.start()
        return c

    pending = []

    def send_z(buf, ref, n):
        out = []
        for dc in range(1, ncol):
            k = n * (ncol - 1) + dc - 1
            out.append(copy(ref, buf.at[at(me_r, me_c)], zs.at[k], zr.at[k], me_r, (me_c + dc) % ncol))
        return out

    def send_xy(buf, n, k):
        col = (me_c + ncol - k) % ncol
        s = (n * ncol + k) * 4
        here = buf.at[at(me_r, col)]
        return (
            copy(here, here, xs.at[s], xr.at[s], xn, me_c),
            copy(here, here, xs.at[s + 1], xr.at[s + 1], yn, me_c),
        )

    def forward(buf, n, k, first, second):
        col = (me_c + ncol - k) % ncol
        s = (n * ncol + k) * 4
        first.wait_recv()
        src = buf.at[at(xn, col, 0)]
        one = copy(src, src, xs.at[s + 2], xr.at[s + 2], yn, me_c)
        second.wait_recv()
        src = buf.at[at(yn, col, 1)]
        two = copy(src, src, xs.at[s + 3], xr.at[s + 3], xn, me_c)
        return (one, two)

    zx = send_z(x_all, x_ref, 0)
    xy_x = [send_xy(x_all, 0, 0)]
    pot_copies = []
    for k, (dr, dc) in enumerate(peers):
        pot_copies.append(
            copy(
                pot_ref, pots.at[pl.ds(pl.multiple_of(me * 16, 16), 16)], ps.at[k], pr.at[k],
                (me_r + dr) % nrow, (me_c + dc) % ncol,
            )
        )
    for k in range(1, ncol):
        zx[k - 1].wait_recv()
        xy_x.append(send_xy(x_all, 0, k))
    zg = send_z(gy_all, gy_ref, 1)
    fw_x = [forward(x_all, 0, k, *xy_x[k]) for k in range(ncol)]
    xy_g = [send_xy(gy_all, 1, 0)]
    for c in pot_copies:
        c.wait_recv()

    scale = 1.0 / (width * EPS)
    eye = (
        lax.broadcasted_iota(jnp.int32, (own, LANES), 0)
        == lax.broadcasted_iota(jnp.int32, (own, LANES), 1)
    )

    def spread(b, carry):
        rows = pl.ds(pl.multiple_of(b * own, 32), own)
        pot = pots[pl.ds(pl.multiple_of(b * 16, 16), 16), :].astype(jnp.float32)
        for at_row, dst in ((0, a_col), (1, f_b), (2, w_col)):
            line = jnp.broadcast_to(pot[at_row : at_row + 1, :], (own, LANES))
            dst[rows, :] = wide(jnp.sum(jnp.where(eye, line, 0.0), axis=1, keepdims=True))
        return carry

    lax.fori_loop(0, blocks, spread, 0)
    for k in range(1, ncol):
        zg[k - 1].wait_recv()
        xy_g.append(send_xy(gy_all, 1, k))
    for one, two in fw_x:
        one.wait_recv()
        two.wait_recv()

    eye_l = (
        lax.broadcasted_iota(jnp.int32, (LANES, LANES), 0)
        == lax.broadcasted_iota(jnp.int32, (LANES, LANES), 1)
    )

    def to_lanes(column):
        return jnp.sum(jnp.where(eye_l, column, 0.0), axis=0, keepdims=True)

    b_parts = []
    for t in range(tiles):
        rows = pl.ds(t * LANES, LANES)
        xf = x_all[rows, :].astype(jnp.float32)
        sq = jnp.sum(xf * xf, axis=1, keepdims=True) * (1.0 / (2.0 * width))
        a = (a_col[rows, :] - sq) * (1.0 / EPS)
        b = (f_b[rows, :] - sq) * (1.0 / EPS)
        a_col[rows, :] = a
        f_b[rows, :] = b
        b_parts.append(to_lanes(b))
        a_lane[0:1, pl.ds(t * LANES, LANES)] = to_lanes(a)
    b_lane = jnp.concatenate(b_parts, axis=1)

    def nt(left, right):
        return lax.dot_general(
            left, right, (((1,), (1,)), ((), ())), preferred_element_type=jnp.float32
        )

    def cut(value, t):
        return value[:, t * LANES : (t + 1) * LANES]

    def make_plan(i, acc):
        rows = pl.ds(pl.multiple_of(i * CHUNK, CHUNK), CHUNK)
        cross = nt(x_all[rows, :], x_all[...])
        a = a_col[rows, :]
        sums = jnp.zeros((CHUNK, LANES), jnp.float32)
        cols = []
        for t in range(tiles):
            p = jnp.exp(cut(cross, t) * scale + (a + cut(b_lane, t)))
            plan[rows, pl.ds(t * LANES, LANES)] = p
            sums = sums + p
            cols.append(fold(p))
        r_col[rows, :] = wide(jnp.sum(sums, axis=1, keepdims=True))
        return acc + jnp.concatenate(cols, axis=1)

    zeros = jnp.zeros((SUBL, total), jnp.float32)
    count = total // CHUNK
    c_acc = lax.fori_loop(0, count // 2, make_plan, zeros)
    fw_g = [forward(gy_all, 1, k, *xy_g[k]) for k in range(ncol)]
    c_acc = lax.fori_loop(count // 2, count, make_plan, c_acc)
    for one, two in fw_g:
        one.wait_recv()
        two.wait_recv()
    c_lane = jnp.sum(c_acc, axis=0, keepdims=True)

    def first(i, carry):
        hc, acc = carry
        rows = pl.ds(pl.multiple_of(i * CHUNK, CHUNK), CHUNK)
        h = nt(x_all[rows, :], gy_all[...])
        sums = jnp.zeros((CHUNK, LANES), jnp.float32)
        cols = []
        for t in range(tiles):
            v = plan[rows, pl.ds(t * LANES, LANES)] * cut(h, t)
            sums = sums + v
            cols.append(fold(v))
        hr = wide(jnp.sum(sums, axis=1, keepdims=True))
        hr_col[rows, :] = hr
        phi = -hr / r_col[rows, :]
        more = [fold(plan[rows, pl.ds(t * LANES, LANES)] * phi) for t in range(tiles)]
        return hc + jnp.concatenate(cols, axis=1), acc + jnp.concatenate(more, axis=1)

    hc_acc, acc = lax.fori_loop(0, count, first, (zeros, zeros))
    hc_lane = jnp.sum(hc_acc, axis=0, keepdims=True)
    psi = -(hc_lane + jnp.sum(acc, axis=0, keepdims=True)) / c_lane

    for step in range(1, ITERS):

        def sweep(i, acc):
            rows = pl.ds(pl.multiple_of(i * CHUNK, CHUNK), CHUNK)
            sums = jnp.zeros((CHUNK, LANES), jnp.float32)
            for t in range(tiles):
                sums = sums + plan[rows, pl.ds(t * LANES, LANES)] * cut(psi, t)
            phi = -(hr_col[rows, :] + wide(jnp.sum(sums, axis=1, keepdims=True))) / r_col[rows, :]
            phi_col[rows, :] = phi
            more = [fold(plan[rows, pl.ds(t * LANES, LANES)] * phi) for t in range(tiles)]
            return acc + jnp.concatenate(more, axis=1)

        acc = lax.fori_loop(0, count, sweep, zeros)
        psi = -(hc_lane + jnp.sum(acc, axis=0, keepdims=True)) / c_lane

    mine = at(me_r, me_c)
    phi_lane = jnp.concatenate([to_lanes(phi_col[pl.ds(t * LANES, LANES), :]) for t in range(tiles)], axis=1)
    phi_own = phi_col[mine, :]
    x_own = x_ref[...]
    gy_own = gy_ref[...]
    p_own = plan[mine, :]
    q_own = p_own * (nt(x_own, gy_all[...]) + (phi_own[:, :1] + psi))
    q_sum = jnp.sum(q_own, axis=1, keepdims=True)
    rowterm = jnp.dot(p_own.astype(jnp.bfloat16), gy_all[...], preferred_element_type=jnp.float32)
    mix = jnp.dot(q_own.astype(jnp.bfloat16), x_all[...], preferred_element_type=jnp.float32)

    pick = lax.broadcasted_iota(jnp.int32, (own, total), 1) == (
        lax.broadcasted_iota(jnp.int32, (own, total), 0) + me * own
    )
    psi_own = jnp.sum(jnp.where(pick, psi, 0.0), axis=1, keepdims=True)
    p_t = jnp.exp(nt(x_own, x_all[...]) * scale + (f_b[mine, :][:, :1] + a_lane[...]))
    q_t = p_t * (nt(gy_own, x_all[...]) + (psi_own + phi_lane))
    mix = mix + jnp.dot(q_t.astype(jnp.bfloat16), x_all[...], preferred_element_type=jnp.float32)
    gp_ref[...] = (rowterm + (mix - q_sum * x_own.astype(jnp.float32)) * scale).astype(jnp.bfloat16)

    w_all = w_col[...]
    w_sum = jnp.sum(fold(w_all), axis=0, keepdims=True)
    w_phi = jnp.sum(fold(w_all * phi_col[...]), axis=0, keepdims=True)
    phi_row = jnp.sum(jnp.where(eye, phi_own, 0.0), axis=0, keepdims=True)
    gw_ref[...] = (-(total / w_sum) * (phi_row - w_phi / w_sum))[:, :own]

    for c in zx + zg + pot_copies:
        c.wait_send()
    for group in (xy_x, fw_x, xy_g, fw_g):
        for one, two in group:
            one.wait_send()
            two.wait_send()


def local_fused(ncol, particles, cotangent, row_potential, col_potential, weights):
    own, width = particles.shape
    total = own * ncol * 4
    pot = jnp.pad(
        jnp.stack([row_potential, col_potential, weights]), ((0, 13), (0, LANES - own))
    )
    column = pltpu.VMEM((total, LANES), jnp.float32)
    dma = pltpu.SemaphoreType.DMA
    peers = 4 * ncol - 1
    gp, gw = pl.pallas_call(
        functools.partial(fused_kernel, ncol),
        out_shape=(
            jax.ShapeDtypeStruct((own, width), jnp.bfloat16),
            jax.ShapeDtypeStruct((1, own), jnp.float32),
        ),
        in_specs=[pl.BlockSpec(memory_space=pltpu.VMEM)] * 3,
        out_specs=[pl.BlockSpec(memory_space=pltpu.VMEM)] * 2,
        scratch_shapes=[
            pltpu.VMEM((total, width), jnp.bfloat16),
            pltpu.VMEM((total, width), jnp.bfloat16),
            pltpu.VMEM((16 * 4 * ncol, LANES), jnp.bfloat16),
            pltpu.VMEM((total, total), jnp.float32),
            column, column, column, column, column, column,
            pltpu.VMEM((1, total), jnp.float32),
            dma((2 * (ncol - 1),)), dma((2 * (ncol - 1),)),
            dma((8 * ncol,)), dma((8 * ncol,)),
            dma((peers,)), dma((peers,)),
        ],
        compiler_params=pltpu.CompilerParams(
            collective_id=0, has_side_effects=True, vmem_limit_bytes=48 * 1024 * 1024
        ),
        cost_estimate=pl.CostEstimate(flops=5 * total * total * width, bytes_accessed=4 * own * width, transcendentals=total * total),
    )(particles, cotangent, pot)
    return gp, gw.reshape(own)


def solution(mesh):
    nrow, ncol = mesh.shape["row"], mesh.shape["col"]

    def local(particles, cotangent, row_potential, col_potential, weights):
        args = (particles, cotangent, row_potential, col_potential, weights)
        own = particles.shape[0]
        total = own * nrow * ncol
        if nrow == 4 and ncol > 1 and own % 32 == 0 and own <= LANES and total % CHUNK == 0 and 4 * total * total <= PLAN_BYTES:
            return local_fused(ncol, *args)
        return local_general(*args)

    return jax.shard_map(
        local,
        mesh=mesh,
        in_specs=(
            P(("filt", "row", "col"), None),
            P(("filt", "row", "col"), None),
            P(("filt", "row", "col")),
            P(("filt", "row", "col")),
            P(("filt", "row", "col")),
        ),
        out_specs=(P(("filt", "row", "col"), None), P(("filt", "row", "col"))),
        check_vma=False,
    )
```

```python
import functools
import jax
import jax.numpy as jnp
from jax import lax
from jax.experimental import pallas as pl
from jax.experimental.pallas import tpu as pltpu
from jax.sharding import PartitionSpec as P

ITERS = 4


EPS = 0.09


def local_general(particles, cotangent, row_potential, col_potential, weights):
    row_parts, row_fpot, row_wts = (
        lax.all_gather(particles, "col", axis=0, tiled=True),
        lax.all_gather(row_potential, "col", axis=0, tiled=True),
        lax.all_gather(weights, "col", axis=0, tiled=True),
    )
    col_parts, col_grads, col_gpot = (
        lax.all_gather(particles, "row", axis=0, tiled=True),
        lax.all_gather(cotangent, "row", axis=0, tiled=True),
        lax.all_gather(col_potential, "row", axis=0, tiled=True),
    )
    own = particles.shape[0]
    width = particles.shape[1]
    rows = row_parts.shape[0]
    cols = col_parts.shape[0]
    blk = 512 if rows % 512 == 0 else rows
    count = rows // blk
    row_float = row_parts.astype(jnp.float32)
    row_sq = jnp.sum(row_float * row_float, axis=1)
    col_float = col_parts.astype(jnp.float32)
    col_sq = jnp.sum(col_float * col_float, axis=1)
    fpot = row_fpot.astype(jnp.float32)
    gpot = col_gpot.astype(jnp.float32)
    stacked = jnp.concatenate([col_parts, col_grads], axis=0)
    items = (
        row_parts.reshape(count, blk, width),
        fpot.reshape(count, blk),
        row_sq.reshape(count, blk),
    )

    def plan_from(cross, pot_blk, sq_blk):
        cost = (sq_blk[:, None] + col_sq[None, :] - 2.0 * cross) / (2.0 * width)
        return jnp.exp((pot_blk[:, None] + gpot[None, :] - cost) / EPS)

    def plan_only(part_blk, pot_blk, sq_blk):
        cross = jnp.einsum("rd,cd->rc", part_blk, col_parts, preferred_element_type=jnp.float32)
        return plan_from(cross, pot_blk, sq_blk)

    def first(carry, item):
        part_blk, pot_blk, sq_blk = item
        both = jnp.einsum("rd,cd->rc", part_blk, stacked, preferred_element_type=jnp.float32)
        plan = plan_from(both[:, :cols], pot_blk, sq_blk)
        weighted = plan * both[:, cols:]
        return (
            (carry[0] + jnp.sum(plan, axis=0), carry[1] + jnp.sum(weighted, axis=0)),
            (jnp.sum(plan, axis=1), jnp.sum(weighted, axis=1)),
        )

    zeros_c = jnp.zeros((cols,), jnp.float32)
    (colmass_part, colph_part), (rowmass_part, rowph_part) = lax.scan(
        first, (zeros_c, zeros_c), items
    )
    rowmass, rowph = lax.psum((rowmass_part.reshape(rows), rowph_part.reshape(rows)), "col")
    colmass, colph = lax.psum((colmass_part, colph_part), "row")
    psi = zeros_c
    phi = jnp.zeros((rows,), jnp.float32)
    for step in range(ITERS):

        def apply_rows(carry, item):
            plan = plan_only(item[0], item[1], item[2])
            return (carry, jnp.dot(plan, psi, precision=lax.Precision.HIGHEST))

        unused, row_apply = lax.scan(apply_rows, jnp.zeros((), jnp.float32), items)
        row_total = lax.psum(row_apply.reshape(rows), "col")
        phi = -(rowph + row_total) / rowmass

        def apply_cols(acc, item):
            plan = plan_only(item[0], item[1], item[2])
            return (acc + jnp.dot(item[3], plan, precision=lax.Precision.HIGHEST), None)

        col_apply, unused_out = lax.scan(apply_cols, zeros_c, items + (phi.reshape(count, blk),))
        col_total = lax.psum(col_apply, "row")
        psi = -(colph + col_total) / colmass

    def last(acc, item):
        part_blk, pot_blk, sq_blk, phi_blk = item
        both = jnp.einsum("rd,cd->rc", part_blk, stacked, preferred_element_type=jnp.float32)
        plan = plan_from(both[:, :cols], pot_blk, sq_blk)
        mixed = plan * (both[:, cols:] + phi_blk[:, None] + psi[None, :])
        qrow = jnp.sum(mixed, axis=1)
        plan_bf = plan.astype(jnp.bfloat16)
        mixed_bf = mixed.astype(jnp.bfloat16)
        rowterm = jnp.dot(plan_bf, col_grads, preferred_element_type=jnp.float32)
        rowterm = rowterm + (
            jnp.dot(mixed_bf, col_parts, preferred_element_type=jnp.float32)
            - qrow[:, None] * part_blk.astype(jnp.float32)
        ) / (width * EPS)
        return (
            acc + jnp.einsum("rc,rd->cd", mixed_bf, part_blk, preferred_element_type=jnp.float32),
            rowterm,
        )

    col_acc, row_terms = lax.scan(
        last, jnp.zeros((cols, width), jnp.float32), items + (phi.reshape(count, blk),)
    )
    row_terms = row_terms.reshape(rows, width)
    start = lax.axis_index("col") * own
    summed = lax.psum(row_terms.astype(jnp.bfloat16), "col").astype(jnp.float32)
    row_own = lax.dynamic_slice_in_dim(summed, start, own, 0)
    col_own = lax.psum_scatter(
        col_acc.astype(jnp.bfloat16), "row", scatter_dimension=0, tiled=True
    ).astype(jnp.float32)
    grad_particles = (row_own + col_own / (width * EPS)).astype(jnp.bfloat16)
    phi_own = lax.dynamic_slice_in_dim(phi, start, own, 0)
    own_wts = weights.astype(jnp.float32)
    total, wphi = lax.psum((jnp.sum(own_wts), jnp.sum(own_wts * phi_own)), ("row", "col"))
    count_all = rows * lax.axis_size("row")
    grad_weights = -(count_all / total) * (phi_own - wphi / total)
    return (grad_particles, grad_weights)


LANES = 128
SUBL = 8
SUB = 64
PLAN_BYTES = 24 * 1024 * 1024


def fold(block):
    return jnp.sum(block.reshape(block.shape[0] // SUBL, SUBL, block.shape[1]), axis=0)


def wide(column):
    return jnp.broadcast_to(column, (column.shape[0], LANES))


def nt(left, right):
    return lax.dot_general(
        left, right, (((1,), (1,)), ((), ())), preferred_element_type=jnp.float32
    )


def fused_kernel(
    ncol, x_ref, gy_ref, pot_ref, gp_ref, gw_ref,
    x_all, gy_all, pots, plan, a_col, b_col, w_col, c_col, nhc_col, psi_col,
    a_lane, b_lane, w_lane, r_acc, sums_all,
    ls, zs, zr, xs, xr, ps, pr, hs, hr_sem,
):
    nrow = 4
    own = x_ref.shape[0]
    half = own // 2
    width = x_ref.shape[1]
    blocks = nrow * ncol
    total = own * blocks
    group = own * ncol
    tiles = total // LANES
    me_r = lax.axis_index("row")
    me_c = lax.axis_index("col")
    me = me_r * ncol + me_c
    xn = me_r + 1 - 2 * (me_r % 2)
    yn = (me_r + 2) % nrow
    dn = (xn + 2) % nrow
    peers = [(dr, dc) for dr in range(nrow) for dc in range(ncol) if dr or dc]
    scale = 1.0 / (width * EPS)

    def at(row, col, part=None):
        base = (row * ncol + col) * own
        if part is None:
            return pl.ds(pl.multiple_of(base, 32), own)
        return pl.ds(pl.multiple_of(base + part * half, 16), half)

    def dev(row, col):
        return {"row": row, "col": col}

    mine = at(me_r, me_c)
    local_x = pltpu.make_async_copy(x_ref, x_all.at[mine], ls.at[0])
    local_x.start()
    local_g = pltpu.make_async_copy(gy_ref, gy_all.at[mine], ls.at[1])
    local_g.start()
    barrier = pltpu.get_barrier_semaphore()
    for dr, dc in peers:
        pl.semaphore_signal(
            barrier, inc=1, device_id=dev((me_r + dr) % nrow, (me_c + dc) % ncol),
            device_id_type=pl.DeviceIdType.MESH,
        )
    my_pot = pl.ds(pl.multiple_of(me * 16, 16), 16)
    pots[my_pot, :] = pot_ref[...]
    r_acc[...] = jnp.zeros_like(r_acc)
    c_col[...] = jnp.zeros_like(c_col)
    pl.semaphore_wait(barrier, len(peers))

    def copy(src, dst, ssem, rsem, row, col):
        c = pltpu.make_async_remote_copy(
            src_ref=src, dst_ref=dst, send_sem=ssem, recv_sem=rsem,
            device_id=dev(row, col), device_id_type=pl.DeviceIdType.MESH,
        )
        c.start()
        return c

    def send_z(buf, ref, n):
        out = []
        for dc in range(1, ncol):
            k = n * (ncol - 1) + dc - 1
            out.append(copy(ref, buf.at[mine], zs.at[k], zr.at[k], me_r, (me_c + dc) % ncol))
        return out

    def send_xy(buf, ref, n, k):
        here = buf.at[at(me_r, (me_c + ncol - k) % ncol)]
        src = ref if k == 0 else here
        s = (n * ncol + k) * 4
        return (
            copy(src, here, xs.at[s], xr.at[s], xn, me_c),
            copy(src, here, xs.at[s + 1], xr.at[s + 1], yn, me_c),
        )

    def forward(buf, n, k, first, second):
        col = (me_c + ncol - k) % ncol
        s = (n * ncol + k) * 4
        first.wait_recv()
        src = buf.at[at(xn, col, 0)]
        one = copy(src, src, xs.at[s + 2], xr.at[s + 2], yn, me_c)
        second.wait_recv()
        src = buf.at[at(yn, col, 1)]
        two = copy(src, src, xs.at[s + 3], xr.at[s + 3], xn, me_c)
        return (one, two)

    zx = send_z(x_all, x_ref, 0)
    xy_x = [send_xy(x_all, x_ref, 0, 0)]
    pot_copies = []
    for k, (dr, dc) in enumerate(peers):
        pot_copies.append(
            copy(pot_ref, pots.at[my_pot], ps.at[k], pr.at[k], (me_r + dr) % nrow, (me_c + dc) % ncol)
        )
    for k in range(1, ncol):
        zx[k - 1].wait_recv()
        xy_x.append(send_xy(x_all, x_ref, 0, k))
    zg = send_z(gy_all, gy_ref, 1)
    for c in pot_copies:
        c.wait_recv()

    eye = (
        lax.broadcasted_iota(jnp.int32, (own, LANES), 0)
        == lax.broadcasted_iota(jnp.int32, (own, LANES), 1)
    )
    eye_l = (
        lax.broadcasted_iota(jnp.int32, (LANES, LANES), 0)
        == lax.broadcasted_iota(jnp.int32, (LANES, LANES), 1)
    )

    def to_lanes(column):
        return jnp.sum(jnp.where(eye_l, column, 0.0), axis=0, keepdims=True)

    def to_column(line):
        return jnp.sum(jnp.where(eye, jnp.broadcast_to(line, (own, LANES)), 0.0), axis=1, keepdims=True)

    def spread(b, carry):
        rows = pl.ds(pl.multiple_of(b * own, 32), own)
        pot = pots[pl.ds(pl.multiple_of(b * 16, 16), 16), :].astype(jnp.float32)
        for k, dst in ((0, a_col), (1, b_col), (2, w_col)):
            dst[rows, :] = wide(to_column(pot[k : k + 1, :]))
        return carry

    lax.fori_loop(0, blocks, spread, 0)
    local_x.wait()

    def prepare(g):
        for t in range(group // LANES):
            rows = pl.ds(pl.multiple_of(g * group + t * LANES, LANES), LANES)
            xf = x_all[rows, :].astype(jnp.float32)
            sq = jnp.sum(xf * xf, axis=1, keepdims=True) * (1.0 / (2.0 * width))
            a = (a_col[rows, :] - sq) * (1.0 / EPS)
            b = (b_col[rows, :] - sq) * (1.0 / EPS)
            a_col[rows, :] = a
            b_col[rows, :] = b
            a_lane[0:1, rows] = to_lanes(a)
            b_lane[0:1, rows] = to_lanes(b)
            w_lane[0:1, rows] = to_lanes(w_col[rows, :])

    def build(gj, gi):
        down = pl.ds(pl.multiple_of(gj * group, LANES), group)
        over = pl.ds(pl.multiple_of(gi * group, LANES), group)
        cross = nt(x_all[down, :], x_all[over, :])
        accs = [jnp.zeros((SUBL, LANES), jnp.float32)] * (group // LANES)
        for s in range(group // SUB):
            rows = pl.ds(pl.multiple_of(gj * group + s * SUB, SUB), SUB)
            b = b_col[rows, :]
            part = jnp.zeros((SUB, LANES), jnp.float32)
            for t in range(group // LANES):
                lanes = pl.ds(pl.multiple_of(gi * group + t * LANES, LANES), LANES)
                piece = cross[s * SUB : (s + 1) * SUB, t * LANES : (t + 1) * LANES]
                p = jnp.exp(piece * scale + (b + a_lane[0:1, lanes]))
                plan[rows, lanes] = p
                part = part + p
                accs[t] = accs[t] + fold(p)
            c_col[rows, :] += wide(jnp.sum(part, axis=1, keepdims=True))
        for t in range(group // LANES):
            lanes = pl.ds(pl.multiple_of(gi * group + t * LANES, LANES), LANES)
            r_acc[:, lanes] += accs[t]

    def near(u):
        return (me_r // 2 + u // 2) % 2 * 2 + (me_r % 2 + u % 2) % 2

    prepare(me_r)
    build(me_r, me_r)
    fw_x = [forward(x_all, 0, k, *xy_x[k]) for k in range(ncol)]
    prepare(xn)
    prepare(yn)

    def early(i, carry):
        build(near(i // 3), near(i % 3))
        return carry

    lax.fori_loop(1, 9, early, 0)
    for one, two in fw_x:
        one.wait_recv()
        two.wait_recv()
    prepare(dn)

    x_own = x_all[mine, :]
    local_g.wait()
    cross_own = nt(x_own, x_all[...]) * scale
    pt_own = jnp.exp(cross_own + (b_col[mine, :][:, :1] + a_lane[...]))
    ht_own = nt(gy_all[mine, :], x_all[...])
    ph = pt_own * ht_own
    hc_own = jnp.sum(ph, axis=1, keepdims=True)
    slot = sums_all.at[me]
    slot[:, pl.ds(0, total)] = jnp.sum(fold(ph), axis=0, keepdims=True)
    slot[:, pl.ds(total, LANES)] = jnp.sum(jnp.where(eye, hc_own, 0.0), axis=0, keepdims=True)
    sum_copies = []
    for k, (dr, dc) in enumerate(peers):
        sum_copies.append(
            copy(slot, slot, hs.at[k], hr_sem.at[k], (me_r + dr) % nrow, (me_c + dc) % ncol)
        )
    xy_g = [send_xy(gy_all, gy_ref, 1, 0)]
    for k in range(1, ncol):
        zg[k - 1].wait_recv()
        xy_g.append(send_xy(gy_all, gy_ref, 1, k))

    def late(i, carry):
        build(near(jnp.minimum(i, 3)), near(jnp.minimum(6 - i, 3)))
        return carry

    lax.fori_loop(0, 7, late, 0)
    for c in sum_copies:
        c.wait_recv()

    def masses(b, carry):
        rows = pl.ds(pl.multiple_of(b * own, 32), own)
        inv = 1.0 / c_col[rows, :]
        c_col[rows, :] = inv
        nhc_col[rows, :] = -wide(to_column(sums_all[b, :, pl.ds(total, LANES)])) * inv
        return carry

    lax.fori_loop(0, blocks, masses, 0)
    hr = jnp.sum(sums_all[:, :, pl.ds(0, total)], axis=0)
    inv_r = 1.0 / jnp.sum(r_acc[...], axis=0, keepdims=True)
    phi = -hr * inv_r
    zeros = jnp.zeros((SUBL, total), jnp.float32)

    def cut(value, t):
        return value[:, t * LANES : (t + 1) * LANES]

    def psi_of(i, phi):
        for s in range(group // SUB):
            rows = pl.ds(pl.multiple_of(i * group + s * SUB, SUB), SUB)
            part = plan[rows, pl.ds(0, LANES)] * cut(phi, 0)
            for t in range(1, tiles):
                part = part + plan[rows, pl.ds(t * LANES, LANES)] * cut(phi, t)
            total_s = wide(jnp.sum(part, axis=1, keepdims=True))
            psi_col[rows, :] = nhc_col[rows, :] - total_s * c_col[rows, :]

    def sweep(phi):
        def body(i, acc):
            psi_of(i, phi)
            accs = [cut(acc, t) for t in range(tiles)]
            for s in range(group // SUB):
                rows = pl.ds(pl.multiple_of(i * group + s * SUB, SUB), SUB)
                psi = psi_col[rows, :]
                for t in range(tiles):
                    accs[t] = accs[t] + fold(plan[rows, pl.ds(t * LANES, LANES)] * psi)
            return jnp.concatenate(accs, axis=1)

        acc = lax.fori_loop(0, nrow, body, zeros)
        return -(hr + jnp.sum(acc, axis=0, keepdims=True)) * inv_r

    fw_g = []
    for step in range(1, ITERS):
        phi = sweep(phi)
        if step == ITERS - 2:
            fw_g = [forward(gy_all, 1, k, *xy_g[k]) for k in range(ncol)]

    def last(i, carry):
        psi_of(i, phi)
        return carry

    lax.fori_loop(0, nrow, last, 0)
    psi_lane = jnp.concatenate(
        [to_lanes(psi_col[pl.ds(t * LANES, LANES), :]) for t in range(tiles)], axis=1
    )
    pick = lax.broadcasted_iota(jnp.int32, (own, total), 1) == (
        lax.broadcasted_iota(jnp.int32, (own, total), 0) + me * own
    )
    phi_own = jnp.sum(jnp.where(pick, phi, 0.0), axis=1, keepdims=True)
    psi_own = psi_col[mine, :][:, :1]
    q_t = pt_own * (ht_own + (psi_own + phi))
    mix = jnp.dot(q_t.astype(jnp.bfloat16), x_all[...], preferred_element_type=jnp.float32)
    p_own = jnp.exp(cross_own + (a_col[mine, :][:, :1] + b_lane[...]))

    w_all = w_lane[...]
    w_sum = jnp.sum(w_all, axis=1, keepdims=True)
    w_phi = jnp.sum(w_all * phi, axis=1, keepdims=True)
    phi_row = jnp.sum(jnp.where(eye, phi_own, 0.0), axis=0, keepdims=True)
    gw_ref[...] = (-(total / w_sum) * (phi_row - w_phi / w_sum))[:, :own]

    for one, two in fw_g:
        one.wait_recv()
        two.wait_recv()
    q_own = p_own * (nt(x_own, gy_all[...]) + (phi_own + psi_lane))
    q_sum = jnp.sum(q_own, axis=1, keepdims=True)
    rowterm = jnp.dot(p_own.astype(jnp.bfloat16), gy_all[...], preferred_element_type=jnp.float32)
    mix = mix + jnp.dot(q_own.astype(jnp.bfloat16), x_all[...], preferred_element_type=jnp.float32)
    gp_ref[...] = (rowterm + (mix - q_sum * x_own.astype(jnp.float32)) * scale).astype(jnp.bfloat16)

    for c in zx + zg + pot_copies + sum_copies:
        c.wait_send()
    for pairs in (xy_x, fw_x, xy_g, fw_g):
        for one, two in pairs:
            one.wait_send()
            two.wait_send()


def local_fused(ncol, particles, cotangent, row_potential, col_potential, weights):
    own, width = particles.shape
    blocks = 4 * ncol
    total = own * blocks
    pot = jnp.pad(
        jnp.stack([row_potential, col_potential, weights]), ((0, 13), (0, LANES - own))
    )
    column = pltpu.VMEM((total, LANES), jnp.float32)
    line = pltpu.VMEM((1, total), jnp.float32)
    dma = pltpu.SemaphoreType.DMA
    vmem = pl.BlockSpec(memory_space=pltpu.VMEM)
    hbm = pl.BlockSpec(memory_space=pltpu.HBM)
    gp, gw = pl.pallas_call(
        functools.partial(fused_kernel, ncol),
        out_shape=(
            jax.ShapeDtypeStruct((own, width), jnp.bfloat16),
            jax.ShapeDtypeStruct((1, own), jnp.float32),
        ),
        in_specs=[hbm, hbm, vmem],
        out_specs=[vmem, vmem],
        scratch_shapes=[
            pltpu.VMEM((total, width), jnp.bfloat16),
            pltpu.VMEM((total, width), jnp.bfloat16),
            pltpu.VMEM((16 * blocks, LANES), jnp.bfloat16),
            pltpu.VMEM((total, total), jnp.float32),
            column, column, column, column, column, column,
            line, line, line,
            pltpu.VMEM((SUBL, total), jnp.float32),
            pltpu.VMEM((blocks, 1, total + LANES), jnp.float32),
            dma((2,)),
            dma((2 * (ncol - 1),)), dma((2 * (ncol - 1),)),
            dma((8 * ncol,)), dma((8 * ncol,)),
            dma((blocks - 1,)), dma((blocks - 1,)),
            dma((blocks - 1,)), dma((blocks - 1,)),
        ],
        compiler_params=pltpu.CompilerParams(
            collective_id=0, has_side_effects=True, vmem_limit_bytes=48 * 1024 * 1024
        ),
        cost_estimate=pl.CostEstimate(
            flops=3 * total * total * width, bytes_accessed=4 * own * width, transcendentals=total * total
        ),
    )(particles, cotangent, pot)
    return gp, gw.reshape(own)


def solution(mesh):
    nrow, ncol = mesh.shape["row"], mesh.shape["col"]

    def local(particles, cotangent, row_potential, col_potential, weights):
        args = (particles, cotangent, row_potential, col_potential, weights)
        own = particles.shape[0]
        total = own * nrow * ncol
        fits = own % 32 == 0 and own <= LANES and own * ncol % LANES == 0
        if nrow == 4 and ncol > 1 and fits and 4 * total * total <= PLAN_BYTES:
            return local_fused(ncol, *args)
        return local_general(*args)

    return jax.shard_map(
        local,
        mesh=mesh,
        in_specs=(
            P(("filt", "row", "col"), None),
            P(("filt", "row", "col"), None),
            P(("filt", "row", "col")),
            P(("filt", "row", "col")),
            P(("filt", "row", "col")),
        ),
        out_specs=(P(("filt", "row", "col"), None), P(("filt", "row", "col"))),
        check_vma=False,
    )
```

```python
import functools
import jax
import jax.numpy as jnp
from jax import lax
from jax.experimental import pallas as pl
from jax.experimental.pallas import tpu as pltpu
from jax.sharding import PartitionSpec as P

ITERS = 4


EPS = 0.09


def local_general(particles, cotangent, row_potential, col_potential, weights):
    row_parts, row_fpot, row_wts = (
        lax.all_gather(particles, "col", axis=0, tiled=True),
        lax.all_gather(row_potential, "col", axis=0, tiled=True),
        lax.all_gather(weights, "col", axis=0, tiled=True),
    )
    col_parts, col_grads, col_gpot = (
        lax.all_gather(particles, "row", axis=0, tiled=True),
        lax.all_gather(cotangent, "row", axis=0, tiled=True),
        lax.all_gather(col_potential, "row", axis=0, tiled=True),
    )
    own = particles.shape[0]
    width = particles.shape[1]
    rows = row_parts.shape[0]
    cols = col_parts.shape[0]
    blk = 512 if rows % 512 == 0 else rows
    count = rows // blk
    row_float = row_parts.astype(jnp.float32)
    row_sq = jnp.sum(row_float * row_float, axis=1)
    col_float = col_parts.astype(jnp.float32)
    col_sq = jnp.sum(col_float * col_float, axis=1)
    fpot = row_fpot.astype(jnp.float32)
    gpot = col_gpot.astype(jnp.float32)
    stacked = jnp.concatenate([col_parts, col_grads], axis=0)
    items = (
        row_parts.reshape(count, blk, width),
        fpot.reshape(count, blk),
        row_sq.reshape(count, blk),
    )

    def plan_from(cross, pot_blk, sq_blk):
        cost = (sq_blk[:, None] + col_sq[None, :] - 2.0 * cross) / (2.0 * width)
        return jnp.exp((pot_blk[:, None] + gpot[None, :] - cost) / EPS)

    def plan_only(part_blk, pot_blk, sq_blk):
        cross = jnp.einsum("rd,cd->rc", part_blk, col_parts, preferred_element_type=jnp.float32)
        return plan_from(cross, pot_blk, sq_blk)

    def first(carry, item):
        part_blk, pot_blk, sq_blk = item
        both = jnp.einsum("rd,cd->rc", part_blk, stacked, preferred_element_type=jnp.float32)
        plan = plan_from(both[:, :cols], pot_blk, sq_blk)
        weighted = plan * both[:, cols:]
        return (
            (carry[0] + jnp.sum(plan, axis=0), carry[1] + jnp.sum(weighted, axis=0)),
            (jnp.sum(plan, axis=1), jnp.sum(weighted, axis=1)),
        )

    zeros_c = jnp.zeros((cols,), jnp.float32)
    (colmass_part, colph_part), (rowmass_part, rowph_part) = lax.scan(
        first, (zeros_c, zeros_c), items
    )
    rowmass, rowph = lax.psum((rowmass_part.reshape(rows), rowph_part.reshape(rows)), "col")
    colmass, colph = lax.psum((colmass_part, colph_part), "row")
    psi = zeros_c
    phi = jnp.zeros((rows,), jnp.float32)
    for step in range(ITERS):

        def apply_rows(carry, item):
            plan = plan_only(item[0], item[1], item[2])
            return (carry, jnp.dot(plan, psi, precision=lax.Precision.HIGHEST))

        unused, row_apply = lax.scan(apply_rows, jnp.zeros((), jnp.float32), items)
        row_total = lax.psum(row_apply.reshape(rows), "col")
        phi = -(rowph + row_total) / rowmass

        def apply_cols(acc, item):
            plan = plan_only(item[0], item[1], item[2])
            return (acc + jnp.dot(item[3], plan, precision=lax.Precision.HIGHEST), None)

        col_apply, unused_out = lax.scan(apply_cols, zeros_c, items + (phi.reshape(count, blk),))
        col_total = lax.psum(col_apply, "row")
        psi = -(colph + col_total) / colmass

    def last(acc, item):
        part_blk, pot_blk, sq_blk, phi_blk = item
        both = jnp.einsum("rd,cd->rc", part_blk, stacked, preferred_element_type=jnp.float32)
        plan = plan_from(both[:, :cols], pot_blk, sq_blk)
        mixed = plan * (both[:, cols:] + phi_blk[:, None] + psi[None, :])
        qrow = jnp.sum(mixed, axis=1)
        plan_bf = plan.astype(jnp.bfloat16)
        mixed_bf = mixed.astype(jnp.bfloat16)
        rowterm = jnp.dot(plan_bf, col_grads, preferred_element_type=jnp.float32)
        rowterm = rowterm + (
            jnp.dot(mixed_bf, col_parts, preferred_element_type=jnp.float32)
            - qrow[:, None] * part_blk.astype(jnp.float32)
        ) / (width * EPS)
        return (
            acc + jnp.einsum("rc,rd->cd", mixed_bf, part_blk, preferred_element_type=jnp.float32),
            rowterm,
        )

    col_acc, row_terms = lax.scan(
        last, jnp.zeros((cols, width), jnp.float32), items + (phi.reshape(count, blk),)
    )
    row_terms = row_terms.reshape(rows, width)
    start = lax.axis_index("col") * own
    summed = lax.psum(row_terms.astype(jnp.bfloat16), "col").astype(jnp.float32)
    row_own = lax.dynamic_slice_in_dim(summed, start, own, 0)
    col_own = lax.psum_scatter(
        col_acc.astype(jnp.bfloat16), "row", scatter_dimension=0, tiled=True
    ).astype(jnp.float32)
    grad_particles = (row_own + col_own / (width * EPS)).astype(jnp.bfloat16)
    phi_own = lax.dynamic_slice_in_dim(phi, start, own, 0)
    own_wts = weights.astype(jnp.float32)
    total, wphi = lax.psum((jnp.sum(own_wts), jnp.sum(own_wts * phi_own)), ("row", "col"))
    count_all = rows * lax.axis_size("row")
    grad_weights = -(count_all / total) * (phi_own - wphi / total)
    return (grad_particles, grad_weights)


LANES = 128
SUBL = 8
SUB = 64
PLAN_BYTES = 24 * 1024 * 1024


def fold(block):
    return jnp.sum(block.reshape(block.shape[0] // SUBL, SUBL, block.shape[1]), axis=0)


def wide(column):
    return jnp.broadcast_to(column, (column.shape[0], LANES))


def nt(left, right):
    return lax.dot_general(
        left, right, (((1,), (1,)), ((), ())), preferred_element_type=jnp.float32
    )


def fused_kernel(
    ncol, x_ref, gy_ref, pot_ref, gp_ref, gw_ref,
    x_all, gy_all, pots, plan, a_col, b_col, w_col, c_col, nhc_col, psi_col,
    a_lane, b_lane, w_lane, r_acc, sums_z, sums_xy,
    ls, zs, zr, xs, xr, ps, pr, hs, hr_sem,
):
    nrow = 4
    own = x_ref.shape[0]
    half = own // 2
    width = x_ref.shape[1]
    blocks = nrow * ncol
    total = own * blocks
    group = own * ncol
    tiles = total // LANES
    me_r = lax.axis_index("row")
    me_c = lax.axis_index("col")
    me = me_r * ncol + me_c
    xn = me_r + 1 - 2 * (me_r % 2)
    yn = (me_r + 2) % nrow
    dn = (xn + 2) % nrow
    peers = [(me_r, (me_c + dc) % ncol) for dc in range(1, ncol)] + [(xn, me_c), (yn, me_c), (dn, me_c)]
    scale = 1.0 / (width * EPS)

    def at(row, col, part=None):
        base = (row * ncol + col) * own
        if part is None:
            return pl.ds(pl.multiple_of(base, 32), own)
        return pl.ds(pl.multiple_of(base + part * half, 16), half)

    def dev(row, col):
        return {"row": row, "col": col}

    mine = at(me_r, me_c)
    local_x = pltpu.make_async_copy(x_ref, x_all.at[mine], ls.at[0])
    local_x.start()
    local_g = pltpu.make_async_copy(gy_ref, gy_all.at[mine], ls.at[1])
    local_g.start()
    barrier = pltpu.get_barrier_semaphore()
    for row, col in peers:
        pl.semaphore_signal(
            barrier, inc=1, device_id=dev(row, col), device_id_type=pl.DeviceIdType.MESH
        )
    my_pot = pl.ds(pl.multiple_of(me * 16, 16), 16)
    pots[my_pot, :] = pot_ref[...]
    r_acc[...] = jnp.zeros_like(r_acc)
    c_col[...] = jnp.zeros_like(c_col)
    pl.semaphore_wait(barrier, len(peers))

    def plan_copy(src, dst, ssem, rsem, row, col):
        return pltpu.make_async_remote_copy(
            src_ref=src, dst_ref=dst, send_sem=ssem, recv_sem=rsem,
            device_id=dev(row, col), device_id_type=pl.DeviceIdType.MESH,
        )

    def copy(*args):
        c = plan_copy(*args)
        c.start()
        return c

    def send_z(buf, ref, n):
        out = []
        for dc in range(1, ncol):
            k = n * (ncol - 1) + dc - 1
            out.append(copy(ref, buf.at[mine], zs.at[k], zr.at[k], me_r, (me_c + dc) % ncol))
        return out

    def send_xy(buf, ref, n, k):
        here = buf.at[at(me_r, (me_c + ncol - k) % ncol)]
        src = ref if k == 0 else here
        s = (n * ncol + k) * 4
        return (
            copy(src, here, xs.at[s], xr.at[s], xn, me_c),
            copy(src, here, xs.at[s + 1], xr.at[s + 1], yn, me_c),
        )

    def forward(buf, n, k):
        col = (me_c + ncol - k) % ncol
        s = (n * ncol + k) * 4
        src = buf.at[at(xn, col, 0)]
        one = plan_copy(src, src, xs.at[s + 2], xr.at[s + 2], yn, me_c)
        src = buf.at[at(yn, col, 1)]
        two = plan_copy(src, src, xs.at[s + 3], xr.at[s + 3], xn, me_c)
        return (one, two)

    def start_forward(pair, group_pair):
        for came, goes in zip(pair, group_pair):
            came.wait_recv()
            goes.start()

    zx = send_z(x_all, x_ref, 0)
    xy_x = [send_xy(x_all, x_ref, 0, 0)]
    pot_z = [
        copy(pot_ref, pots.at[my_pot], ps.at[k], pr.at[k], *peers[k]) for k in range(ncol - 1)
    ]
    for k in range(1, ncol):
        zx[k - 1].wait_recv()
        xy_x.append(send_xy(x_all, x_ref, 0, k))
    for c in pot_z:
        c.wait_recv()
    column_pots = pots.at[pl.ds(pl.multiple_of(me_r * 16 * ncol, 16), 16 * ncol)]
    pot_xy = [
        copy(column_pots, column_pots, ps.at[k], pr.at[k], *peers[k]) for k in range(ncol - 1, ncol + 2)
    ]
    zg = send_z(gy_all, gy_ref, 1)
    for c in pot_xy:
        c.wait_recv()

    eye = (
        lax.broadcasted_iota(jnp.int32, (own, LANES), 0)
        == lax.broadcasted_iota(jnp.int32, (own, LANES), 1)
    )
    eye_l = (
        lax.broadcasted_iota(jnp.int32, (LANES, LANES), 0)
        == lax.broadcasted_iota(jnp.int32, (LANES, LANES), 1)
    )

    def to_lanes(column):
        return jnp.sum(jnp.where(eye_l, column, 0.0), axis=0, keepdims=True)

    def to_column(line):
        return jnp.sum(jnp.where(eye, jnp.broadcast_to(line, (own, LANES)), 0.0), axis=1, keepdims=True)

    def spread(b, carry):
        rows = pl.ds(pl.multiple_of(b * own, 32), own)
        pot = pots[pl.ds(pl.multiple_of(b * 16, 16), 16), :].astype(jnp.float32)
        for k, dst in ((0, a_col), (1, b_col), (2, w_col)):
            dst[rows, :] = wide(to_column(pot[k : k + 1, :]))
        return carry

    lax.fori_loop(0, blocks, spread, 0)
    local_x.wait()

    def prepare(g):
        def body(t, carry):
            rows = pl.ds(pl.multiple_of(g * group + t * LANES, LANES), LANES)
            xf = x_all[rows, :].astype(jnp.float32)
            sq = jnp.sum(xf * xf, axis=1, keepdims=True) * (1.0 / (2.0 * width))
            a = (a_col[rows, :] - sq) * (1.0 / EPS)
            b = (b_col[rows, :] - sq) * (1.0 / EPS)
            a_col[rows, :] = a
            b_col[rows, :] = b
            a_lane[0:1, rows] = to_lanes(a)
            b_lane[0:1, rows] = to_lanes(b)
            w_lane[0:1, rows] = to_lanes(w_col[rows, :])
            return carry

        lax.fori_loop(0, group // LANES, body, 0)

    def build(gj, gi):
        down = pl.ds(pl.multiple_of(gj * group, LANES), group)
        over = pl.ds(pl.multiple_of(gi * group, LANES), group)
        cross = nt(x_all[down, :], x_all[over, :])
        accs = [jnp.zeros((SUBL, LANES), jnp.float32)] * (group // LANES)
        for s in range(group // SUB):
            rows = pl.ds(pl.multiple_of(gj * group + s * SUB, SUB), SUB)
            b = b_col[rows, :]
            part = jnp.zeros((SUB, LANES), jnp.float32)
            for t in range(group // LANES):
                lanes = pl.ds(pl.multiple_of(gi * group + t * LANES, LANES), LANES)
                piece = cross[s * SUB : (s + 1) * SUB, t * LANES : (t + 1) * LANES]
                p = jnp.exp(piece * scale + (b + a_lane[0:1, lanes]))
                plan[rows, lanes] = p
                part = part + p
                accs[t] = accs[t] + fold(p)
            c_col[rows, :] += wide(jnp.sum(part, axis=1, keepdims=True))
        for t in range(group // LANES):
            lanes = pl.ds(pl.multiple_of(gi * group + t * LANES, LANES), LANES)
            r_acc[:, lanes] += accs[t]

    def near(u):
        return (me_r // 2 + u // 2) % 2 * 2 + (me_r % 2 + u % 2) % 2

    prepare(me_r)
    build(me_r, me_r)
    fw_x = [forward(x_all, 0, k) for k in range(ncol)]
    for k in range(ncol):
        start_forward(xy_x[k], fw_x[k])
    prepare(xn)
    prepare(yn)

    def early(i, carry):
        build(near(i // 3), near(i % 3))
        return carry

    lax.fori_loop(1, 9, early, 0)
    for one, two in fw_x:
        one.wait_recv()
        two.wait_recv()
    prepare(dn)

    x_own = x_all[mine, :]
    local_g.wait()
    cross_own = nt(x_own, x_all[...]) * scale
    pt_own = jnp.exp(cross_own + (b_col[mine, :][:, :1] + a_lane[...]))
    ht_own = nt(gy_all[mine, :], x_all[...])
    ph = pt_own * ht_own
    hc_own = jnp.sum(ph, axis=1, keepdims=True)
    slot = sums_z.at[me_c]
    slot[:, pl.ds(0, total)] = jnp.sum(fold(ph), axis=0, keepdims=True)
    slot[:, pl.ds(total, LANES)] = jnp.sum(jnp.where(eye, hc_own, 0.0), axis=0, keepdims=True)
    sum_z = [copy(slot, slot, hs.at[k], hr_sem.at[k], *peers[k]) for k in range(ncol - 1)]
    xy_g = [send_xy(gy_all, gy_ref, 1, 0)]
    for k in range(1, ncol):
        zg[k - 1].wait_recv()
        if k < ncol - 1:
            xy_g.append(send_xy(gy_all, gy_ref, 1, k))

    def late(i, carry):
        build(near(jnp.minimum(i, 3)), near(jnp.minimum(6 - i, 3)))

        @pl.when(i == 2)
        def exchange():
            for c in sum_z:
                c.wait_recv()
            sums_xy[me_r, :, pl.ds(0, total)] = jnp.sum(sums_z[:, :, pl.ds(0, total)], axis=0)
            for k in range(ncol):
                sums_xy[me_r, :, pl.ds(total + k * LANES, LANES)] = sums_z[k, :, pl.ds(total, LANES)]
            for c in sum_xy:
                c.start()

        return carry

    mine_xy = sums_xy.at[me_r]
    sum_xy = [
        plan_copy(mine_xy, mine_xy, hs.at[k], hr_sem.at[k], *peers[k]) for k in range(ncol - 1, ncol + 2)
    ]
    lax.fori_loop(0, 7, late, 0)
    xy_g.append(send_xy(gy_all, gy_ref, 1, ncol - 1))
    for c in sum_xy:
        c.wait_recv()

    def masses(b, carry):
        rows = pl.ds(pl.multiple_of(b * own, 32), own)
        inv = 1.0 / c_col[rows, :]
        c_col[rows, :] = inv
        nhc_col[rows, :] = -wide(
            to_column(sums_xy[b // ncol, :, pl.ds(pl.multiple_of(total + b % ncol * LANES, LANES), LANES)])
        ) * inv
        return carry

    lax.fori_loop(0, blocks, masses, 0)
    hr = jnp.sum(sums_xy[:, :, pl.ds(0, total)], axis=0)
    inv_r = 1.0 / jnp.sum(r_acc[...], axis=0, keepdims=True)
    phi = -hr * inv_r
    zeros = jnp.zeros((SUBL, total), jnp.float32)

    def cut(value, t):
        return value[:, t * LANES : (t + 1) * LANES]

    def psi_of(i, phi):
        for s in range(group // SUB):
            rows = pl.ds(pl.multiple_of(i * group + s * SUB, SUB), SUB)
            part = plan[rows, pl.ds(0, LANES)] * cut(phi, 0)
            for t in range(1, tiles):
                part = part + plan[rows, pl.ds(t * LANES, LANES)] * cut(phi, t)
            total_s = wide(jnp.sum(part, axis=1, keepdims=True))
            psi_col[rows, :] = nhc_col[rows, :] - total_s * c_col[rows, :]

    def sweep(phi):
        def body(i, acc):
            psi_of(i, phi)
            accs = [cut(acc, t) for t in range(tiles)]
            for s in range(group // SUB):
                rows = pl.ds(pl.multiple_of(i * group + s * SUB, SUB), SUB)
                psi = psi_col[rows, :]
                for t in range(tiles):
                    accs[t] = accs[t] + fold(plan[rows, pl.ds(t * LANES, LANES)] * psi)
            return jnp.concatenate(accs, axis=1)

        acc = lax.fori_loop(0, nrow, body, zeros)
        return -(hr + jnp.sum(acc, axis=0, keepdims=True)) * inv_r

    fw_g = [forward(gy_all, 1, k) for k in range(ncol)]

    def step(i, phi):
        phi = sweep(phi)

        @pl.when(i == ITERS - 2)
        def forwards():
            for k in range(ncol):
                start_forward(xy_g[k], fw_g[k])

        return phi

    phi = lax.fori_loop(1, ITERS, step, phi)

    def last(i, carry):
        psi_of(i, phi)
        return carry

    lax.fori_loop(0, nrow, last, 0)
    psi_lane = jnp.concatenate(
        [to_lanes(psi_col[pl.ds(t * LANES, LANES), :]) for t in range(tiles)], axis=1
    )
    pick = lax.broadcasted_iota(jnp.int32, (own, total), 1) == (
        lax.broadcasted_iota(jnp.int32, (own, total), 0) + me * own
    )
    phi_own = jnp.sum(jnp.where(pick, phi, 0.0), axis=1, keepdims=True)
    psi_own = psi_col[mine, :][:, :1]
    q_t = pt_own * (ht_own + (psi_own + phi))
    mix = jnp.dot(q_t.astype(jnp.bfloat16), x_all[...], preferred_element_type=jnp.float32)
    p_own = jnp.exp(cross_own + (a_col[mine, :][:, :1] + b_lane[...]))

    w_all = w_lane[...]
    w_sum = jnp.sum(w_all, axis=1, keepdims=True)
    w_phi = jnp.sum(w_all * phi, axis=1, keepdims=True)
    phi_row = jnp.sum(jnp.where(eye, phi_own, 0.0), axis=0, keepdims=True)
    gw_ref[...] = (-(total / w_sum) * (phi_row - w_phi / w_sum))[:, :own]

    for one, two in fw_g:
        one.wait_recv()
        two.wait_recv()
    q_own = p_own * (nt(x_own, gy_all[...]) + (phi_own + psi_lane))
    q_sum = jnp.sum(q_own, axis=1, keepdims=True)
    rowterm = jnp.dot(p_own.astype(jnp.bfloat16), gy_all[...], preferred_element_type=jnp.float32)
    mix = mix + jnp.dot(q_own.astype(jnp.bfloat16), x_all[...], preferred_element_type=jnp.float32)
    gp_ref[...] = (rowterm + (mix - q_sum * x_own.astype(jnp.float32)) * scale).astype(jnp.bfloat16)

    for c in zx + zg + pot_z + pot_xy + sum_z + sum_xy:
        c.wait_send()
    for pairs in (xy_x, fw_x, xy_g, fw_g):
        for one, two in pairs:
            one.wait_send()
            two.wait_send()


def local_fused(ncol, particles, cotangent, row_potential, col_potential, weights):
    own, width = particles.shape
    blocks = 4 * ncol
    total = own * blocks
    pot = jnp.pad(
        jnp.stack([row_potential, col_potential, weights]), ((0, 13), (0, LANES - own))
    )
    column = pltpu.VMEM((total, LANES), jnp.float32)
    line = pltpu.VMEM((1, total), jnp.float32)
    dma = pltpu.SemaphoreType.DMA
    vmem = pl.BlockSpec(memory_space=pltpu.VMEM)
    hbm = pl.BlockSpec(memory_space=pltpu.HBM)
    gp, gw = pl.pallas_call(
        functools.partial(fused_kernel, ncol),
        out_shape=(
            jax.ShapeDtypeStruct((own, width), jnp.bfloat16),
            jax.ShapeDtypeStruct((1, own), jnp.float32),
        ),
        in_specs=[hbm, hbm, vmem],
        out_specs=[vmem, vmem],
        scratch_shapes=[
            pltpu.VMEM((total, width), jnp.bfloat16),
            pltpu.VMEM((total, width), jnp.bfloat16),
            pltpu.VMEM((16 * blocks, LANES), jnp.bfloat16),
            pltpu.VMEM((total, total), jnp.float32),
            column, column, column, column, column, column,
            line, line, line,
            pltpu.VMEM((SUBL, total), jnp.float32),
            pltpu.VMEM((ncol, 1, total + LANES), jnp.float32),
            pltpu.VMEM((4, 1, total + ncol * LANES), jnp.float32),
            dma((2,)),
            dma((2 * (ncol - 1),)), dma((2 * (ncol - 1),)),
            dma((8 * ncol,)), dma((8 * ncol,)),
            dma((ncol + 2,)), dma((ncol + 2,)),
            dma((ncol + 2,)), dma((ncol + 2,)),
        ],
        compiler_params=pltpu.CompilerParams(
            collective_id=0, has_side_effects=True, vmem_limit_bytes=62 * 1024 * 1024
        ),
        cost_estimate=pl.CostEstimate(
            flops=3 * total * total * width, bytes_accessed=4 * own * width, transcendentals=total * total
        ),
    )(particles, cotangent, pot)
    return gp, gw.reshape(own)


def solution(mesh):
    nrow, ncol = mesh.shape["row"], mesh.shape["col"]

    def local(particles, cotangent, row_potential, col_potential, weights):
        args = (particles, cotangent, row_potential, col_potential, weights)
        own = particles.shape[0]
        total = own * nrow * ncol
        fits = own % 32 == 0 and own <= LANES and own * ncol % LANES == 0
        if nrow == 4 and ncol > 1 and fits and 4 * total * total <= PLAN_BYTES:
            return local_fused(ncol, *args)
        return local_general(*args)

    return jax.shard_map(
        local,
        mesh=mesh,
        in_specs=(
            P(("filt", "row", "col"), None),
            P(("filt", "row", "col"), None),
            P(("filt", "row", "col")),
            P(("filt", "row", "col")),
            P(("filt", "row", "col")),
        ),
        out_specs=(P(("filt", "row", "col"), None), P(("filt", "row", "col"))),
        check_vma=False,
    )
```

```python
import functools
import jax
import jax.numpy as jnp
from jax import lax
from jax.experimental import pallas as pl
from jax.experimental.pallas import tpu as pltpu
from jax.sharding import PartitionSpec as P

ITERS = 4


EPS = 0.09


def local_general(particles, cotangent, row_potential, col_potential, weights):
    row_parts, row_fpot, row_wts = (
        lax.all_gather(particles, "col", axis=0, tiled=True),
        lax.all_gather(row_potential, "col", axis=0, tiled=True),
        lax.all_gather(weights, "col", axis=0, tiled=True),
    )
    col_parts, col_grads, col_gpot = (
        lax.all_gather(particles, "row", axis=0, tiled=True),
        lax.all_gather(cotangent, "row", axis=0, tiled=True),
        lax.all_gather(col_potential, "row", axis=0, tiled=True),
    )
    own = particles.shape[0]
    width = particles.shape[1]
    rows = row_parts.shape[0]
    cols = col_parts.shape[0]
    blk = 512 if rows % 512 == 0 else rows
    count = rows // blk
    row_float = row_parts.astype(jnp.float32)
    row_sq = jnp.sum(row_float * row_float, axis=1)
    col_float = col_parts.astype(jnp.float32)
    col_sq = jnp.sum(col_float * col_float, axis=1)
    fpot = row_fpot.astype(jnp.float32)
    gpot = col_gpot.astype(jnp.float32)
    stacked = jnp.concatenate([col_parts, col_grads], axis=0)
    items = (
        row_parts.reshape(count, blk, width),
        fpot.reshape(count, blk),
        row_sq.reshape(count, blk),
    )

    def plan_from(cross, pot_blk, sq_blk):
        cost = (sq_blk[:, None] + col_sq[None, :] - 2.0 * cross) / (2.0 * width)
        return jnp.exp((pot_blk[:, None] + gpot[None, :] - cost) / EPS)

    def plan_only(part_blk, pot_blk, sq_blk):
        cross = jnp.einsum("rd,cd->rc", part_blk, col_parts, preferred_element_type=jnp.float32)
        return plan_from(cross, pot_blk, sq_blk)

    def first(carry, item):
        part_blk, pot_blk, sq_blk = item
        both = jnp.einsum("rd,cd->rc", part_blk, stacked, preferred_element_type=jnp.float32)
        plan = plan_from(both[:, :cols], pot_blk, sq_blk)
        weighted = plan * both[:, cols:]
        return (
            (carry[0] + jnp.sum(plan, axis=0), carry[1] + jnp.sum(weighted, axis=0)),
            (jnp.sum(plan, axis=1), jnp.sum(weighted, axis=1)),
        )

    zeros_c = jnp.zeros((cols,), jnp.float32)
    (colmass_part, colph_part), (rowmass_part, rowph_part) = lax.scan(
        first, (zeros_c, zeros_c), items
    )
    rowmass, rowph = lax.psum((rowmass_part.reshape(rows), rowph_part.reshape(rows)), "col")
    colmass, colph = lax.psum((colmass_part, colph_part), "row")
    psi = zeros_c
    phi = jnp.zeros((rows,), jnp.float32)
    for step in range(ITERS):

        def apply_rows(carry, item):
            plan = plan_only(item[0], item[1], item[2])
            return (carry, jnp.dot(plan, psi, precision=lax.Precision.HIGHEST))

        unused, row_apply = lax.scan(apply_rows, jnp.zeros((), jnp.float32), items)
        row_total = lax.psum(row_apply.reshape(rows), "col")
        phi = -(rowph + row_total) / rowmass

        def apply_cols(acc, item):
            plan = plan_only(item[0], item[1], item[2])
            return (acc + jnp.dot(item[3], plan, precision=lax.Precision.HIGHEST), None)

        col_apply, unused_out = lax.scan(apply_cols, zeros_c, items + (phi.reshape(count, blk),))
        col_total = lax.psum(col_apply, "row")
        psi = -(colph + col_total) / colmass

    def last(acc, item):
        part_blk, pot_blk, sq_blk, phi_blk = item
        both = jnp.einsum("rd,cd->rc", part_blk, stacked, preferred_element_type=jnp.float32)
        plan = plan_from(both[:, :cols], pot_blk, sq_blk)
        mixed = plan * (both[:, cols:] + phi_blk[:, None] + psi[None, :])
        qrow = jnp.sum(mixed, axis=1)
        plan_bf = plan.astype(jnp.bfloat16)
        mixed_bf = mixed.astype(jnp.bfloat16)
        rowterm = jnp.dot(plan_bf, col_grads, preferred_element_type=jnp.float32)
        rowterm = rowterm + (
            jnp.dot(mixed_bf, col_parts, preferred_element_type=jnp.float32)
            - qrow[:, None] * part_blk.astype(jnp.float32)
        ) / (width * EPS)
        return (
            acc + jnp.einsum("rc,rd->cd", mixed_bf, part_blk, preferred_element_type=jnp.float32),
            rowterm,
        )

    col_acc, row_terms = lax.scan(
        last, jnp.zeros((cols, width), jnp.float32), items + (phi.reshape(count, blk),)
    )
    row_terms = row_terms.reshape(rows, width)
    start = lax.axis_index("col") * own
    summed = lax.psum(row_terms.astype(jnp.bfloat16), "col").astype(jnp.float32)
    row_own = lax.dynamic_slice_in_dim(summed, start, own, 0)
    col_own = lax.psum_scatter(
        col_acc.astype(jnp.bfloat16), "row", scatter_dimension=0, tiled=True
    ).astype(jnp.float32)
    grad_particles = (row_own + col_own / (width * EPS)).astype(jnp.bfloat16)
    phi_own = lax.dynamic_slice_in_dim(phi, start, own, 0)
    own_wts = weights.astype(jnp.float32)
    total, wphi = lax.psum((jnp.sum(own_wts), jnp.sum(own_wts * phi_own)), ("row", "col"))
    count_all = rows * lax.axis_size("row")
    grad_weights = -(count_all / total) * (phi_own - wphi / total)
    return (grad_particles, grad_weights)


LANES = 128
SUBL = 8
SUB = 64
PLAN_BYTES = 24 * 1024 * 1024


def fold(block):
    return jnp.sum(block.reshape(block.shape[0] // SUBL, SUBL, block.shape[1]), axis=0)


def wide(column):
    return jnp.broadcast_to(column, (column.shape[0], LANES))


def nt(left, right):
    return lax.dot_general(
        left, right, (((1,), (1,)), ((), ())), preferred_element_type=jnp.float32
    )


def fused_kernel(
    ncol, own, pack_ref, gp_ref, gw_ref,
    x_all, gy_all, pots, plan, a_col, b_col, w_col, c_col, nhc_col, psi_col,
    a_lane, b_lane, w_lane, r_acc, sums_all,
    ls, zs, zr, xs, xr, ps, pr, hs, hr_sem,
):
    nrow = 4
    half = own // 2
    width = pack_ref.shape[1]
    x_ref = pack_ref.at[pl.ds(0, own)]
    gy_ref = pack_ref.at[pl.ds(own, own)]
    pot_ref = pack_ref.at[pl.ds(2 * own, 16), pl.ds(0, LANES)]
    blocks = nrow * ncol
    total = own * blocks
    group = own * ncol
    tiles = total // LANES
    me_r = lax.axis_index("row")
    me_c = lax.axis_index("col")
    me = me_r * ncol + me_c
    xn = me_r + 1 - 2 * (me_r % 2)
    yn = (me_r + 2) % nrow
    dn = (xn + 2) % nrow
    peers = [
        ((me_r + dr) % nrow, (me_c + dc) % ncol) for dr in range(nrow) for dc in range(ncol) if dr or dc
    ]
    scale = 1.0 / (width * EPS)

    def at(row, col, part=None):
        base = (row * ncol + col) * own
        if part is None:
            return pl.ds(pl.multiple_of(base, 32), own)
        return pl.ds(pl.multiple_of(base + part * half, 16), half)

    def dev(row, col):
        return {"row": row, "col": col}

    mine = at(me_r, me_c)
    local_x = pltpu.make_async_copy(x_ref, x_all.at[mine], ls.at[0])
    local_x.start()
    local_g = pltpu.make_async_copy(gy_ref, gy_all.at[mine], ls.at[1])
    local_g.start()
    barrier = pltpu.get_barrier_semaphore()
    for row, col in peers:
        pl.semaphore_signal(
            barrier, inc=1, device_id=dev(row, col), device_id_type=pl.DeviceIdType.MESH
        )
    my_pot = pl.ds(pl.multiple_of(me * 16, 16), 16)
    pots[my_pot, :] = pot_ref[...]
    r_acc[...] = jnp.zeros_like(r_acc)
    c_col[...] = jnp.zeros_like(c_col)
    pl.semaphore_wait(barrier, len(peers))

    def plan_copy(src, dst, ssem, rsem, row, col):
        return pltpu.make_async_remote_copy(
            src_ref=src, dst_ref=dst, send_sem=ssem, recv_sem=rsem,
            device_id=dev(row, col), device_id_type=pl.DeviceIdType.MESH,
        )

    def copy(*args):
        c = plan_copy(*args)
        c.start()
        return c

    def send_z(buf, ref, n):
        out = []
        for dc in range(1, ncol):
            k = n * (ncol - 1) + dc - 1
            out.append(copy(ref, buf.at[mine], zs.at[k], zr.at[k], me_r, (me_c + dc) % ncol))
        return out

    def send_plane(buf, ref, n, k):
        col = (me_c + ncol - k) % ncol
        here = buf.at[at(me_r, col)]
        src = ref if k == 0 else here
        s = (n * ncol + k) * 3
        out = [
            copy(src, here, xs.at[s], xr.at[s], xn, me_c),
            copy(src, here, xs.at[s + 1], xr.at[s + 1], yn, me_c),
        ]
        if k == 0:
            out.append(copy(src, here, xs.at[s + 2], xr.at[s + 2], dn, me_c))
        else:
            here = buf.at[at(me_r, col, 0)]
            out.append(copy(here, here, xs.at[s + 2], xr.at[s + 2], dn, me_c))
        return out

    def relay(buf, n, came):
        came.wait_recv()
        here = buf.at[at(dn, me_c, 1)]
        out = []
        for dc in range(1, ncol):
            k = (2 + n) * (ncol - 1) + dc - 1
            out.append(copy(here, here, zs.at[k], zr.at[k], me_r, (me_c + dc) % ncol))
        return out

    zx = send_z(x_all, x_ref, 0)
    plane_x = [send_plane(x_all, x_ref, 0, 0)]
    pot_copies = [
        copy(pot_ref, pots.at[my_pot], ps.at[k], pr.at[k], *peers[k]) for k in range(len(peers))
    ]
    for k in range(1, ncol):
        zx[k - 1].wait_recv()
        plane_x.append(send_plane(x_all, x_ref, 0, k))
    zx += relay(x_all, 0, plane_x[0][2])
    zg = send_z(gy_all, gy_ref, 1)
    plane_g = [send_plane(gy_all, gy_ref, 1, 0)]
    for c in pot_copies:
        c.wait_recv()

    eye = (
        lax.broadcasted_iota(jnp.int32, (own, LANES), 0)
        == lax.broadcasted_iota(jnp.int32, (own, LANES), 1)
    )
    eye_l = (
        lax.broadcasted_iota(jnp.int32, (LANES, LANES), 0)
        == lax.broadcasted_iota(jnp.int32, (LANES, LANES), 1)
    )

    def to_lanes(column):
        return jnp.sum(jnp.where(eye_l, column, 0.0), axis=0, keepdims=True)

    def to_column(line):
        return jnp.sum(jnp.where(eye, jnp.broadcast_to(line, (own, LANES)), 0.0), axis=1, keepdims=True)

    def spread(b, carry):
        rows = pl.ds(pl.multiple_of(b * own, 32), own)
        pot = pots[pl.ds(pl.multiple_of(b * 16, 16), 16), :].astype(jnp.float32)
        for k, dst in ((0, a_col), (1, b_col), (2, w_col)):
            dst[rows, :] = wide(to_column(pot[k : k + 1, :]))
        return carry

    lax.fori_loop(0, blocks, spread, 0)
    local_x.wait()

    def prepare(g):
        def body(t, carry):
            rows = pl.ds(pl.multiple_of(g * group + t * LANES, LANES), LANES)
            xf = x_all[rows, :].astype(jnp.float32)
            sq = jnp.sum(xf * xf, axis=1, keepdims=True) * (1.0 / (2.0 * width))
            a = (a_col[rows, :] - sq) * (1.0 / EPS)
            b = (b_col[rows, :] - sq) * (1.0 / EPS)
            a_col[rows, :] = a
            b_col[rows, :] = b
            a_lane[0:1, rows] = to_lanes(a)
            b_lane[0:1, rows] = to_lanes(b)
            w_lane[0:1, rows] = to_lanes(w_col[rows, :])
            return carry

        lax.fori_loop(0, group // LANES, body, 0)

    def build(gj, gi):
        down = pl.ds(pl.multiple_of(gj * group, LANES), group)
        over = pl.ds(pl.multiple_of(gi * group, LANES), group)
        cross = nt(x_all[down, :], x_all[over, :])
        accs = [jnp.zeros((SUBL, LANES), jnp.float32)] * (group // LANES)
        for s in range(group // SUB):
            rows = pl.ds(pl.multiple_of(gj * group + s * SUB, SUB), SUB)
            b = b_col[rows, :]
            part = jnp.zeros((SUB, LANES), jnp.float32)
            for t in range(group // LANES):
                lanes = pl.ds(pl.multiple_of(gi * group + t * LANES, LANES), LANES)
                piece = cross[s * SUB : (s + 1) * SUB, t * LANES : (t + 1) * LANES]
                p = jnp.exp(piece * scale + (b + a_lane[0:1, lanes]))
                plan[rows, lanes] = p
                part = part + p
                accs[t] = accs[t] + fold(p)
            c_col[rows, :] += wide(jnp.sum(part, axis=1, keepdims=True))
        for t in range(group // LANES):
            lanes = pl.ds(pl.multiple_of(gi * group + t * LANES, LANES), LANES)
            r_acc[:, lanes] += accs[t]

    def near(u):
        return (me_r // 2 + u // 2) % 2 * 2 + (me_r % 2 + u % 2) % 2

    prepare(me_r)
    build(me_r, me_r)
    for sent in plane_x:
        sent[0].wait_recv()
    prepare(xn)
    for sent in plane_x:
        sent[1].wait_recv()
    prepare(yn)

    def early(i, carry):
        build(near(i // 3), near(i % 3))
        return carry

    lax.fori_loop(1, 9, early, 0)
    for sent in plane_x[1:]:
        sent[2].wait_recv()
    for c in zx[ncol - 1 :]:
        c.wait_recv()
    prepare(dn)

    x_own = x_all[mine, :]
    local_g.wait()
    cross_own = nt(x_own, x_all[...]) * scale
    pt_own = jnp.exp(cross_own + (b_col[mine, :][:, :1] + a_lane[...]))
    ht_own = nt(gy_all[mine, :], x_all[...])
    ph = pt_own * ht_own
    hc_own = jnp.sum(ph, axis=1, keepdims=True)
    slot = sums_all.at[me]
    slot[:, pl.ds(0, total)] = jnp.sum(fold(ph), axis=0, keepdims=True)
    slot[:, pl.ds(total, LANES)] = jnp.sum(jnp.where(eye, hc_own, 0.0), axis=0, keepdims=True)
    sum_copies = [
        copy(slot, slot, hs.at[k], hr_sem.at[k], *peers[k]) for k in range(len(peers))
    ]

    def late(i, carry):
        build(near(jnp.minimum(i, 3)), near(jnp.minimum(6 - i, 3)))
        return carry

    lax.fori_loop(0, 7, late, 0)
    for c in sum_copies:
        c.wait_recv()
    for k in range(1, ncol):
        zg[k - 1].wait_recv()
        plane_g.append(send_plane(gy_all, gy_ref, 1, k))
    zg += relay(gy_all, 1, plane_g[0][2])

    def masses(b, carry):
        rows = pl.ds(pl.multiple_of(b * own, 32), own)
        inv = 1.0 / c_col[rows, :]
        c_col[rows, :] = inv
        nhc_col[rows, :] = -wide(to_column(sums_all[b, :, pl.ds(total, LANES)])) * inv
        return carry

    lax.fori_loop(0, blocks, masses, 0)
    hr = jnp.sum(sums_all[:, :, pl.ds(0, total)], axis=0)
    inv_r = 1.0 / jnp.sum(r_acc[...], axis=0, keepdims=True)
    phi = -hr * inv_r
    zeros = jnp.zeros((SUBL, total), jnp.float32)

    def cut(value, t):
        return value[:, t * LANES : (t + 1) * LANES]

    def psi_of(i, phi):
        for s in range(group // SUB):
            rows = pl.ds(pl.multiple_of(i * group + s * SUB, SUB), SUB)
            part = plan[rows, pl.ds(0, LANES)] * cut(phi, 0)
            for t in range(1, tiles):
                part = part + plan[rows, pl.ds(t * LANES, LANES)] * cut(phi, t)
            total_s = wide(jnp.sum(part, axis=1, keepdims=True))
            psi_col[rows, :] = nhc_col[rows, :] - total_s * c_col[rows, :]

    def sweep(phi):
        def body(i, acc):
            psi_of(i, phi)
            accs = [cut(acc, t) for t in range(tiles)]
            for s in range(group // SUB):
                rows = pl.ds(pl.multiple_of(i * group + s * SUB, SUB), SUB)
                psi = psi_col[rows, :]
                for t in range(tiles):
                    accs[t] = accs[t] + fold(plan[rows, pl.ds(t * LANES, LANES)] * psi)
            return jnp.concatenate(accs, axis=1)

        acc = lax.fori_loop(0, nrow, body, zeros)
        return -(hr + jnp.sum(acc, axis=0, keepdims=True)) * inv_r

    phi = lax.fori_loop(1, ITERS, lambda i, line: sweep(line), phi)

    def last(i, carry):
        psi_of(i, phi)
        return carry

    lax.fori_loop(0, nrow, last, 0)
    psi_lane = jnp.concatenate(
        [to_lanes(psi_col[pl.ds(t * LANES, LANES), :]) for t in range(tiles)], axis=1
    )
    pick = lax.broadcasted_iota(jnp.int32, (own, total), 1) == (
        lax.broadcasted_iota(jnp.int32, (own, total), 0) + me * own
    )
    phi_own = jnp.sum(jnp.where(pick, phi, 0.0), axis=1, keepdims=True)
    psi_own = psi_col[mine, :][:, :1]
    q_t = pt_own * (ht_own + (psi_own + phi))
    mix = jnp.dot(q_t.astype(jnp.bfloat16), x_all[...], preferred_element_type=jnp.float32)
    p_own = jnp.exp(cross_own + (a_col[mine, :][:, :1] + b_lane[...]))

    w_all = w_lane[...]
    w_sum = jnp.sum(w_all, axis=1, keepdims=True)
    w_phi = jnp.sum(w_all * phi, axis=1, keepdims=True)
    phi_row = jnp.sum(jnp.where(eye, phi_own, 0.0), axis=0, keepdims=True)
    gw_ref[...] = (-(total / w_sum) * (phi_row - w_phi / w_sum))[:, :own]

    for k in range(ncol):
        plane_g[k][0].wait_recv()
        plane_g[k][1].wait_recv()
        if k:
            plane_g[k][2].wait_recv()
    for c in zg[ncol - 1 :]:
        c.wait_recv()
    q_own = p_own * (nt(x_own, gy_all[...]) + (phi_own + psi_lane))
    q_sum = jnp.sum(q_own, axis=1, keepdims=True)
    rowterm = jnp.dot(p_own.astype(jnp.bfloat16), gy_all[...], preferred_element_type=jnp.float32)
    mix = mix + jnp.dot(q_own.astype(jnp.bfloat16), x_all[...], preferred_element_type=jnp.float32)
    gp_ref[...] = (rowterm + (mix - q_sum * x_own.astype(jnp.float32)) * scale).astype(jnp.bfloat16)

    for c in zx + zg + pot_copies + sum_copies:
        c.wait_send()
    for sent in plane_x + plane_g:
        for c in sent:
            c.wait_send()


def local_fused(ncol, particles, cotangent, row_potential, col_potential, weights):
    own, width = particles.shape
    blocks = 4 * ncol
    total = own * blocks
    pot = jnp.pad(
        jnp.stack([row_potential, col_potential, weights]), ((0, 13), (0, width - own))
    )
    pack = jnp.concatenate([particles, cotangent, pot], axis=0)
    column = pltpu.VMEM((total, LANES), jnp.float32)
    line = pltpu.VMEM((1, total), jnp.float32)
    dma = pltpu.SemaphoreType.DMA
    vmem = pl.BlockSpec(memory_space=pltpu.VMEM)
    gp, gw = pl.pallas_call(
        functools.partial(fused_kernel, ncol, own),
        out_shape=(
            jax.ShapeDtypeStruct((own, width), jnp.bfloat16),
            jax.ShapeDtypeStruct((1, own), jnp.float32),
        ),
        in_specs=[vmem],
        out_specs=[vmem, vmem],
        scratch_shapes=[
            pltpu.VMEM((total, width), jnp.bfloat16),
            pltpu.VMEM((total, width), jnp.bfloat16),
            pltpu.VMEM((16 * blocks, LANES), jnp.bfloat16),
            pltpu.VMEM((total, total), jnp.float32),
            column, column, column, column, column, column,
            line, line, line,
            pltpu.VMEM((SUBL, total), jnp.float32),
            pltpu.VMEM((blocks, 1, total + LANES), jnp.float32),
            dma((2,)),
            dma((4 * (ncol - 1),)), dma((4 * (ncol - 1),)),
            dma((6 * ncol,)), dma((6 * ncol,)),
            dma((blocks - 1,)), dma((blocks - 1,)),
            dma((blocks - 1,)), dma((blocks - 1,)),
        ],
        compiler_params=pltpu.CompilerParams(
            collective_id=0, has_side_effects=True, vmem_limit_bytes=48 * 1024 * 1024
        ),
        cost_estimate=pl.CostEstimate(
            flops=3 * total * total * width, bytes_accessed=4 * own * width, transcendentals=total * total
        ),
    )(pack)
    return gp, gw.reshape(own)


def solution(mesh):
    nrow, ncol = mesh.shape["row"], mesh.shape["col"]

    def local(particles, cotangent, row_potential, col_potential, weights):
        args = (particles, cotangent, row_potential, col_potential, weights)
        own = particles.shape[0]
        total = own * nrow * ncol
        fits = own % 32 == 0 and own <= LANES and own * ncol % LANES == 0
        if nrow == 4 and ncol > 1 and fits and 4 * total * total <= PLAN_BYTES:
            return local_fused(ncol, *args)
        return local_general(*args)

    return jax.shard_map(
        local,
        mesh=mesh,
        in_specs=(
            P(("filt", "row", "col"), None),
            P(("filt", "row", "col"), None),
            P(("filt", "row", "col")),
            P(("filt", "row", "col")),
            P(("filt", "row", "col")),
        ),
        out_specs=(P(("filt", "row", "col"), None), P(("filt", "row", "col"))),
        check_vma=False,
    )
```

```python
import functools
import jax
import jax.numpy as jnp
from jax import lax
from jax.experimental import pallas as pl
from jax.experimental.pallas import tpu as pltpu
from jax.sharding import PartitionSpec as P

ITERS = 4


EPS = 0.09


def local_general(particles, cotangent, row_potential, col_potential, weights):
    row_parts, row_fpot, row_wts = (
        lax.all_gather(particles, "col", axis=0, tiled=True),
        lax.all_gather(row_potential, "col", axis=0, tiled=True),
        lax.all_gather(weights, "col", axis=0, tiled=True),
    )
    col_parts, col_grads, col_gpot = (
        lax.all_gather(particles, "row", axis=0, tiled=True),
        lax.all_gather(cotangent, "row", axis=0, tiled=True),
        lax.all_gather(col_potential, "row", axis=0, tiled=True),
    )
    own = particles.shape[0]
    width = particles.shape[1]
    rows = row_parts.shape[0]
    cols = col_parts.shape[0]
    blk = 512 if rows % 512 == 0 else rows
    count = rows // blk
    row_float = row_parts.astype(jnp.float32)
    row_sq = jnp.sum(row_float * row_float, axis=1)
    col_float = col_parts.astype(jnp.float32)
    col_sq = jnp.sum(col_float * col_float, axis=1)
    fpot = row_fpot.astype(jnp.float32)
    gpot = col_gpot.astype(jnp.float32)
    stacked = jnp.concatenate([col_parts, col_grads], axis=0)
    items = (
        row_parts.reshape(count, blk, width),
        fpot.reshape(count, blk),
        row_sq.reshape(count, blk),
    )

    def plan_from(cross, pot_blk, sq_blk):
        cost = (sq_blk[:, None] + col_sq[None, :] - 2.0 * cross) / (2.0 * width)
        return jnp.exp((pot_blk[:, None] + gpot[None, :] - cost) / EPS)

    def plan_only(part_blk, pot_blk, sq_blk):
        cross = jnp.einsum("rd,cd->rc", part_blk, col_parts, preferred_element_type=jnp.float32)
        return plan_from(cross, pot_blk, sq_blk)

    def first(carry, item):
        part_blk, pot_blk, sq_blk = item
        both = jnp.einsum("rd,cd->rc", part_blk, stacked, preferred_element_type=jnp.float32)
        plan = plan_from(both[:, :cols], pot_blk, sq_blk)
        weighted = plan * both[:, cols:]
        return (
            (carry[0] + jnp.sum(plan, axis=0), carry[1] + jnp.sum(weighted, axis=0)),
            (jnp.sum(plan, axis=1), jnp.sum(weighted, axis=1)),
        )

    zeros_c = jnp.zeros((cols,), jnp.float32)
    (colmass_part, colph_part), (rowmass_part, rowph_part) = lax.scan(
        first, (zeros_c, zeros_c), items
    )
    rowmass, rowph = lax.psum((rowmass_part.reshape(rows), rowph_part.reshape(rows)), "col")
    colmass, colph = lax.psum((colmass_part, colph_part), "row")
    psi = zeros_c
    phi = jnp.zeros((rows,), jnp.float32)
    for step in range(ITERS):

        def apply_rows(carry, item):
            plan = plan_only(item[0], item[1], item[2])
            return (carry, jnp.dot(plan, psi, precision=lax.Precision.HIGHEST))

        unused, row_apply = lax.scan(apply_rows, jnp.zeros((), jnp.float32), items)
        row_total = lax.psum(row_apply.reshape(rows), "col")
        phi = -(rowph + row_total) / rowmass

        def apply_cols(acc, item):
            plan = plan_only(item[0], item[1], item[2])
            return (acc + jnp.dot(item[3], plan, precision=lax.Precision.HIGHEST), None)

        col_apply, unused_out = lax.scan(apply_cols, zeros_c, items + (phi.reshape(count, blk),))
        col_total = lax.psum(col_apply, "row")
        psi = -(colph + col_total) / colmass

    def last(acc, item):
        part_blk, pot_blk, sq_blk, phi_blk = item
        both = jnp.einsum("rd,cd->rc", part_blk, stacked, preferred_element_type=jnp.float32)
        plan = plan_from(both[:, :cols], pot_blk, sq_blk)
        mixed = plan * (both[:, cols:] + phi_blk[:, None] + psi[None, :])
        qrow = jnp.sum(mixed, axis=1)
        plan_bf = plan.astype(jnp.bfloat16)
        mixed_bf = mixed.astype(jnp.bfloat16)
        rowterm = jnp.dot(plan_bf, col_grads, preferred_element_type=jnp.float32)
        rowterm = rowterm + (
            jnp.dot(mixed_bf, col_parts, preferred_element_type=jnp.float32)
            - qrow[:, None] * part_blk.astype(jnp.float32)
        ) / (width * EPS)
        return (
            acc + jnp.einsum("rc,rd->cd", mixed_bf, part_blk, preferred_element_type=jnp.float32),
            rowterm,
        )

    col_acc, row_terms = lax.scan(
        last, jnp.zeros((cols, width), jnp.float32), items + (phi.reshape(count, blk),)
    )
    row_terms = row_terms.reshape(rows, width)
    start = lax.axis_index("col") * own
    summed = lax.psum(row_terms.astype(jnp.bfloat16), "col").astype(jnp.float32)
    row_own = lax.dynamic_slice_in_dim(summed, start, own, 0)
    col_own = lax.psum_scatter(
        col_acc.astype(jnp.bfloat16), "row", scatter_dimension=0, tiled=True
    ).astype(jnp.float32)
    grad_particles = (row_own + col_own / (width * EPS)).astype(jnp.bfloat16)
    phi_own = lax.dynamic_slice_in_dim(phi, start, own, 0)
    own_wts = weights.astype(jnp.float32)
    total, wphi = lax.psum((jnp.sum(own_wts), jnp.sum(own_wts * phi_own)), ("row", "col"))
    count_all = rows * lax.axis_size("row")
    grad_weights = -(count_all / total) * (phi_own - wphi / total)
    return (grad_particles, grad_weights)


LANES = 128
SUBL = 8
SUB = 64
PLAN_BYTES = 24 * 1024 * 1024


def fold(block):
    return jnp.sum(block.reshape(block.shape[0] // SUBL, SUBL, block.shape[1]), axis=0)


def wide(column):
    return jnp.broadcast_to(column, (column.shape[0], LANES))


def lane_sums(parts):
    high = parts.astype(jnp.bfloat16)
    low = (parts - high.astype(jnp.float32)).astype(jnp.bfloat16)
    both = jnp.concatenate([high, low], axis=1)
    ones = jnp.ones((both.shape[1], LANES), jnp.bfloat16)
    return jnp.dot(both, ones, preferred_element_type=jnp.float32)


def nt(left, right):
    return lax.dot_general(
        left, right, (((1,), (1,)), ((), ())), preferred_element_type=jnp.float32
    )


def fused_kernel(
    ncol, own, pack_ref, gp_ref, gw_ref,
    x_all, gy_all, pots, plan, a_col, b_col, c_col, nhc_col, psi_col,
    a_lane, b_lane, w_lane, r_acc, sums_all,
    ls, zs, zr, xs, xr, ps, pr, hs, hr_sem,
):
    nrow = 4
    half = own // 2
    width = pack_ref.shape[1]
    x_ref = pack_ref.at[pl.ds(0, own)]
    gy_ref = pack_ref.at[pl.ds(own, own)]
    pot_ref = pack_ref.at[pl.ds(2 * own, 16), pl.ds(0, LANES)]
    blocks = nrow * ncol
    total = own * blocks
    group = own * ncol
    tiles = total // LANES
    me_r = lax.axis_index("row")
    me_c = lax.axis_index("col")
    me = me_r * ncol + me_c
    xn = me_r + 1 - 2 * (me_r % 2)
    yn = (me_r + 2) % nrow
    dn = (xn + 2) % nrow
    peers = [
        ((me_r + dr) % nrow, (me_c + dc) % ncol) for dr in range(nrow) for dc in range(ncol) if dr or dc
    ]
    scale = 1.0 / (width * EPS)

    def at(row, col, part=None):
        base = (row * ncol + col) * own
        if part is None:
            return pl.ds(pl.multiple_of(base, 32), own)
        return pl.ds(pl.multiple_of(base + part * half, 16), half)

    def dev(row, col):
        return {"row": row, "col": col}

    mine = at(me_r, me_c)
    local_x = pltpu.make_async_copy(x_ref, x_all.at[mine], ls.at[0])
    local_x.start()
    local_g = pltpu.make_async_copy(gy_ref, gy_all.at[mine], ls.at[1])
    local_g.start()
    barrier = pltpu.get_barrier_semaphore()
    for row, col in peers:
        pl.semaphore_signal(
            barrier, inc=1, device_id=dev(row, col), device_id_type=pl.DeviceIdType.MESH
        )
    my_pot = pl.ds(pl.multiple_of(me * 16, 16), 16)
    pots[my_pot, :] = pot_ref[...]
    r_acc[...] = jnp.zeros_like(r_acc)
    c_col[...] = jnp.zeros_like(c_col)
    pl.semaphore_wait(barrier, len(peers))

    def plan_copy(src, dst, ssem, rsem, row, col):
        return pltpu.make_async_remote_copy(
            src_ref=src, dst_ref=dst, send_sem=ssem, recv_sem=rsem,
            device_id=dev(row, col), device_id_type=pl.DeviceIdType.MESH,
        )

    def copy(*args):
        c = plan_copy(*args)
        c.start()
        return c

    def send_z(buf, ref, n):
        out = []
        for dc in range(1, ncol):
            k = n * (ncol - 1) + dc - 1
            out.append(copy(ref, buf.at[mine], zs.at[k], zr.at[k], me_r, (me_c + dc) % ncol))
        return out

    def send_plane(buf, ref, n, k):
        col = (me_c + ncol - k) % ncol
        here = buf.at[at(me_r, col)]
        src = ref if k == 0 else here
        s = (n * ncol + k) * 3
        out = [
            copy(src, here, xs.at[s], xr.at[s], xn, me_c),
            copy(src, here, xs.at[s + 1], xr.at[s + 1], yn, me_c),
        ]
        if k == 0:
            out.append(copy(src, here, xs.at[s + 2], xr.at[s + 2], dn, me_c))
        else:
            here = buf.at[at(me_r, col, 0)]
            out.append(copy(here, here, xs.at[s + 2], xr.at[s + 2], dn, me_c))
        return out

    def relay(buf, n, came):
        came.wait_recv()
        here = buf.at[at(dn, me_c, 1)]
        out = []
        for dc in range(1, ncol):
            k = (2 + n) * (ncol - 1) + dc - 1
            out.append(copy(here, here, zs.at[k], zr.at[k], me_r, (me_c + dc) % ncol))
        return out

    zx = send_z(x_all, x_ref, 0)
    plane_x = [send_plane(x_all, x_ref, 0, 0)]
    pot_copies = [
        copy(pot_ref, pots.at[my_pot], ps.at[k], pr.at[k], *peers[k]) for k in range(len(peers))
    ]
    for k in range(1, ncol):
        zx[k - 1].wait_recv()
        plane_x.append(send_plane(x_all, x_ref, 0, k))
    zx += relay(x_all, 0, plane_x[0][2])
    zg = send_z(gy_all, gy_ref, 1)
    plane_g = [send_plane(gy_all, gy_ref, 1, 0)]
    for c in pot_copies:
        c.wait_recv()

    eye = (
        lax.broadcasted_iota(jnp.int32, (own, LANES), 0)
        == lax.broadcasted_iota(jnp.int32, (own, LANES), 1)
    )
    eye_l = (
        lax.broadcasted_iota(jnp.int32, (LANES, LANES), 0)
        == lax.broadcasted_iota(jnp.int32, (LANES, LANES), 1)
    )

    def to_lanes(column):
        return jnp.sum(jnp.where(eye_l, column, 0.0), axis=0, keepdims=True)

    def on_diagonal(lines):
        spots = [jnp.where(eye, jnp.broadcast_to(line, (own, LANES)), 0.0) for line in lines]
        return jnp.concatenate(spots, axis=0)

    ones = jnp.ones((LANES, LANES), jnp.bfloat16)
    local_x.wait()

    def prepare(g):
        rows = pl.ds(pl.multiple_of(g * group, LANES), group)
        pot = pots[pl.ds(pl.multiple_of(g * 16 * ncol, 16), 16 * ncol), :].astype(jnp.float32)
        f, gp, w = [
            jnp.dot(
                on_diagonal([pot[16 * b + k : 16 * b + k + 1, :] for b in range(ncol)]).astype(jnp.bfloat16),
                ones,
                preferred_element_type=jnp.float32,
            )
            for k in range(3)
        ]
        xf = x_all[rows, :].astype(jnp.float32)
        sq = lane_sums(xf * xf) * (1.0 / (2.0 * width))
        a = (f - sq) * (1.0 / EPS)
        b = (gp - sq) * (1.0 / EPS)
        a_col[rows, :] = a
        b_col[rows, :] = b
        for t in range(group // LANES):
            lanes = pl.ds(pl.multiple_of(g * group + t * LANES, LANES), LANES)
            here = slice(t * LANES, (t + 1) * LANES)
            a_lane[0:1, lanes] = to_lanes(a[here])
            b_lane[0:1, lanes] = to_lanes(b[here])
            w_lane[0:1, lanes] = to_lanes(w[here])

    def build(gj, gi):
        down = pl.ds(pl.multiple_of(gj * group, LANES), group)
        over = pl.ds(pl.multiple_of(gi * group, LANES), group)
        cross = nt(x_all[down, :], x_all[over, :])
        accs = [jnp.zeros((SUBL, LANES), jnp.float32)] * (group // LANES)
        for s in range(group // SUB):
            rows = pl.ds(pl.multiple_of(gj * group + s * SUB, SUB), SUB)
            b = b_col[rows, :]
            part = jnp.zeros((SUB, LANES), jnp.float32)
            for t in range(group // LANES):
                lanes = pl.ds(pl.multiple_of(gi * group + t * LANES, LANES), LANES)
                piece = cross[s * SUB : (s + 1) * SUB, t * LANES : (t + 1) * LANES]
                p = jnp.exp(piece * scale + (b + a_lane[0:1, lanes]))
                plan[rows, lanes] = p
                part = part + p
                accs[t] = accs[t] + fold(p)
            c_col[rows, :] += part
        for t in range(group // LANES):
            lanes = pl.ds(pl.multiple_of(gi * group + t * LANES, LANES), LANES)
            r_acc[:, lanes] += accs[t]

    def near(u):
        return (me_r // 2 + u // 2) % 2 * 2 + (me_r % 2 + u % 2) % 2

    prepare(me_r)
    build(me_r, me_r)
    for sent in plane_x:
        sent[0].wait_recv()
    prepare(xn)
    for sent in plane_x:
        sent[1].wait_recv()
    prepare(yn)

    def early(i, carry):
        build(near(i // 3), near(i % 3))
        return carry

    lax.fori_loop(1, 9, early, 0)
    for sent in plane_x[1:]:
        sent[2].wait_recv()
    for c in zx[ncol - 1 :]:
        c.wait_recv()
    prepare(dn)

    x_own = x_all[mine, :]
    local_g.wait()
    cross_own = nt(x_own, x_all[...]) * scale
    pt_own = jnp.exp(cross_own + (b_col[mine, :][:, :1] + a_lane[...]))
    ht_own = nt(gy_all[mine, :], x_all[...])
    ph = pt_own * ht_own
    hc_own = jnp.sum(ph, axis=1, keepdims=True)
    slot = sums_all.at[me]
    slot[:, pl.ds(0, total)] = jnp.sum(fold(ph), axis=0, keepdims=True)
    slot[:, pl.ds(total, LANES)] = jnp.sum(jnp.where(eye, hc_own, 0.0), axis=0, keepdims=True)
    sum_copies = [
        copy(slot, slot, hs.at[k], hr_sem.at[k], *peers[k]) for k in range(len(peers))
    ]

    def late(i, carry):
        build(near(jnp.minimum(i, 3)), near(jnp.minimum(6 - i, 3)))
        return carry

    lax.fori_loop(0, 7, late, 0)
    for c in sum_copies:
        c.wait_recv()
    for k in range(1, ncol):
        zg[k - 1].wait_recv()
        plane_g.append(send_plane(gy_all, gy_ref, 1, k))
    zg += relay(gy_all, 1, plane_g[0][2])

    for g in range(nrow):
        rows = pl.ds(g * group, group)
        inv = 1.0 / lane_sums(c_col[rows, :])
        c_col[rows, :] = inv
        lines = [sums_all[g * ncol + b, :, pl.ds(total, LANES)] for b in range(ncol)]
        nhc_col[rows, :] = -lane_sums(on_diagonal(lines)) * inv
    hr = jnp.sum(sums_all[:, :, pl.ds(0, total)], axis=0)
    inv_r = 1.0 / jnp.sum(r_acc[...], axis=0, keepdims=True)
    phi = -hr * inv_r

    def cut(value, t):
        return value[:, t * LANES : (t + 1) * LANES]

    def psi_of(g, phi):
        phi8 = jnp.broadcast_to(phi, (SUBL, total))
        parts = []
        for s in range(group // SUB):
            rows = pl.ds(pl.multiple_of(g * group + s * SUB, SUB), SUB)
            part = jnp.zeros((SUB // SUBL, SUBL, LANES), jnp.float32)
            for t in range(tiles):
                piece = plan[rows, pl.ds(t * LANES, LANES)].reshape(SUB // SUBL, SUBL, LANES)
                part = part + piece * cut(phi8, t)[None]
            parts.append(part.reshape(SUB, LANES))
        rows = pl.ds(pl.multiple_of(g * group, LANES), group)
        return nhc_col[rows, :] - lane_sums(jnp.concatenate(parts, axis=0)) * c_col[rows, :]

    def add_columns(g, psi, accs):
        out = list(accs)
        for s in range(group // SUB):
            rows = pl.ds(g * group + s * SUB, SUB)
            here = psi[s * SUB : (s + 1) * SUB]
            for t in range(tiles):
                out[t] = out[t] + fold(plan[rows, pl.ds(t * LANES, LANES)] * here)
        return out

    def sweep(i, phi):
        accs = [jnp.zeros((SUBL, LANES), jnp.float32)] * tiles
        psi = psi_of(0, phi)
        for g in range(1, nrow):
            later = psi_of(g, phi)
            accs = add_columns(g - 1, psi, accs)
            psi = later
        accs = add_columns(nrow - 1, psi, accs)
        return -(hr + jnp.sum(jnp.concatenate(accs, axis=1), axis=0, keepdims=True)) * inv_r

    phi = lax.fori_loop(1, ITERS, sweep, phi)
    for g in range(nrow):
        psi_col[pl.ds(g * group, group), :] = psi_of(g, phi)
    psi_lane = jnp.concatenate(
        [to_lanes(psi_col[pl.ds(t * LANES, LANES), :]) for t in range(tiles)], axis=1
    )
    pick = lax.broadcasted_iota(jnp.int32, (own, total), 1) == (
        lax.broadcasted_iota(jnp.int32, (own, total), 0) + me * own
    )
    phi_own = jnp.sum(jnp.where(pick, phi, 0.0), axis=1, keepdims=True)
    psi_own = psi_col[mine, :][:, :1]
    q_t = pt_own * (ht_own + (psi_own + phi))
    mix = jnp.dot(q_t.astype(jnp.bfloat16), x_all[...], preferred_element_type=jnp.float32)
    p_own = jnp.exp(cross_own + (a_col[mine, :][:, :1] + b_lane[...]))

    w_all = w_lane[...]
    w_sum = jnp.sum(w_all, axis=1, keepdims=True)
    w_phi = jnp.sum(w_all * phi, axis=1, keepdims=True)
    phi_row = jnp.sum(jnp.where(eye, phi_own, 0.0), axis=0, keepdims=True)
    gw_ref[...] = (-(total / w_sum) * (phi_row - w_phi / w_sum))[:, :own]

    for k in range(ncol):
        plane_g[k][0].wait_recv()
        plane_g[k][1].wait_recv()
        if k:
            plane_g[k][2].wait_recv()
    for c in zg[ncol - 1 :]:
        c.wait_recv()
    q_own = p_own * (nt(x_own, gy_all[...]) + (phi_own + psi_lane))
    q_sum = jnp.sum(q_own, axis=1, keepdims=True)
    rowterm = jnp.dot(p_own.astype(jnp.bfloat16), gy_all[...], preferred_element_type=jnp.float32)
    mix = mix + jnp.dot(q_own.astype(jnp.bfloat16), x_all[...], preferred_element_type=jnp.float32)
    gp_ref[...] = (rowterm + (mix - q_sum * x_own.astype(jnp.float32)) * scale).astype(jnp.bfloat16)

    for c in zx + zg + pot_copies + sum_copies:
        c.wait_send()
    for sent in plane_x + plane_g:
        for c in sent:
            c.wait_send()


def local_fused(ncol, particles, cotangent, row_potential, col_potential, weights):
    own, width = particles.shape
    blocks = 4 * ncol
    total = own * blocks
    pot = jnp.pad(
        jnp.stack([row_potential, col_potential, weights]), ((0, 13), (0, width - own))
    )
    pack = jnp.concatenate([particles, cotangent, pot], axis=0)
    column = pltpu.VMEM((total, LANES), jnp.float32)
    line = pltpu.VMEM((1, total), jnp.float32)
    dma = pltpu.SemaphoreType.DMA
    vmem = pl.BlockSpec(memory_space=pltpu.VMEM)
    gp, gw = pl.pallas_call(
        functools.partial(fused_kernel, ncol, own),
        out_shape=(
            jax.ShapeDtypeStruct((own, width), jnp.bfloat16),
            jax.ShapeDtypeStruct((1, own), jnp.float32),
        ),
        in_specs=[vmem],
        out_specs=[vmem, vmem],
        scratch_shapes=[
            pltpu.VMEM((total, width), jnp.bfloat16),
            pltpu.VMEM((total, width), jnp.bfloat16),
            pltpu.VMEM((16 * blocks, LANES), jnp.bfloat16),
            pltpu.VMEM((total, total), jnp.float32),
            column, column, column, column, column,
            line, line, line,
            pltpu.VMEM((SUBL, total), jnp.float32),
            pltpu.VMEM((blocks, 1, total + LANES), jnp.float32),
            dma((2,)),
            dma((4 * (ncol - 1),)), dma((4 * (ncol - 1),)),
            dma((6 * ncol,)), dma((6 * ncol,)),
            dma((blocks - 1,)), dma((blocks - 1,)),
            dma((blocks - 1,)), dma((blocks - 1,)),
        ],
        compiler_params=pltpu.CompilerParams(
            collective_id=0, has_side_effects=True, vmem_limit_bytes=48 * 1024 * 1024
        ),
        cost_estimate=pl.CostEstimate(
            flops=3 * total * total * width, bytes_accessed=4 * own * width, transcendentals=total * total
        ),
    )(pack)
    return gp, gw.reshape(own)


def solution(mesh):
    nrow, ncol = mesh.shape["row"], mesh.shape["col"]

    def local(particles, cotangent, row_potential, col_potential, weights):
        args = (particles, cotangent, row_potential, col_potential, weights)
        own = particles.shape[0]
        total = own * nrow * ncol
        fits = own % 32 == 0 and own <= LANES and own * ncol % LANES == 0
        if nrow == 4 and ncol > 1 and fits and 4 * total * total <= PLAN_BYTES:
            return local_fused(ncol, *args)
        return local_general(*args)

    return jax.shard_map(
        local,
        mesh=mesh,
        in_specs=(
            P(("filt", "row", "col"), None),
            P(("filt", "row", "col"), None),
            P(("filt", "row", "col")),
            P(("filt", "row", "col")),
            P(("filt", "row", "col")),
        ),
        out_specs=(P(("filt", "row", "col"), None), P(("filt", "row", "col"))),
        check_vma=False,
    )
```

```python
import functools
import jax
import jax.numpy as jnp
from jax import lax
from jax.experimental import pallas as pl
from jax.experimental.pallas import tpu as pltpu
from jax.sharding import PartitionSpec as P

ITERS = 4


EPS = 0.09


def local_general(particles, cotangent, row_potential, col_potential, weights):
    row_parts, row_fpot, row_wts = (
        lax.all_gather(particles, "col", axis=0, tiled=True),
        lax.all_gather(row_potential, "col", axis=0, tiled=True),
        lax.all_gather(weights, "col", axis=0, tiled=True),
    )
    col_parts, col_grads, col_gpot = (
        lax.all_gather(particles, "row", axis=0, tiled=True),
        lax.all_gather(cotangent, "row", axis=0, tiled=True),
        lax.all_gather(col_potential, "row", axis=0, tiled=True),
    )
    own = particles.shape[0]
    width = particles.shape[1]
    rows = row_parts.shape[0]
    cols = col_parts.shape[0]
    blk = 512 if rows % 512 == 0 else rows
    count = rows // blk
    row_float = row_parts.astype(jnp.float32)
    row_sq = jnp.sum(row_float * row_float, axis=1)
    col_float = col_parts.astype(jnp.float32)
    col_sq = jnp.sum(col_float * col_float, axis=1)
    fpot = row_fpot.astype(jnp.float32)
    gpot = col_gpot.astype(jnp.float32)
    stacked = jnp.concatenate([col_parts, col_grads], axis=0)
    items = (
        row_parts.reshape(count, blk, width),
        fpot.reshape(count, blk),
        row_sq.reshape(count, blk),
    )

    def plan_from(cross, pot_blk, sq_blk):
        cost = (sq_blk[:, None] + col_sq[None, :] - 2.0 * cross) / (2.0 * width)
        return jnp.exp((pot_blk[:, None] + gpot[None, :] - cost) / EPS)

    def plan_only(part_blk, pot_blk, sq_blk):
        cross = jnp.einsum("rd,cd->rc", part_blk, col_parts, preferred_element_type=jnp.float32)
        return plan_from(cross, pot_blk, sq_blk)

    def first(carry, item):
        part_blk, pot_blk, sq_blk = item
        both = jnp.einsum("rd,cd->rc", part_blk, stacked, preferred_element_type=jnp.float32)
        plan = plan_from(both[:, :cols], pot_blk, sq_blk)
        weighted = plan * both[:, cols:]
        return (
            (carry[0] + jnp.sum(plan, axis=0), carry[1] + jnp.sum(weighted, axis=0)),
            (jnp.sum(plan, axis=1), jnp.sum(weighted, axis=1)),
        )

    zeros_c = jnp.zeros((cols,), jnp.float32)
    (colmass_part, colph_part), (rowmass_part, rowph_part) = lax.scan(
        first, (zeros_c, zeros_c), items
    )
    rowmass, rowph = lax.psum((rowmass_part.reshape(rows), rowph_part.reshape(rows)), "col")
    colmass, colph = lax.psum((colmass_part, colph_part), "row")
    psi = zeros_c
    phi = jnp.zeros((rows,), jnp.float32)
    for step in range(ITERS):

        def apply_rows(carry, item):
            plan = plan_only(item[0], item[1], item[2])
            return (carry, jnp.dot(plan, psi, precision=lax.Precision.HIGHEST))

        unused, row_apply = lax.scan(apply_rows, jnp.zeros((), jnp.float32), items)
        row_total = lax.psum(row_apply.reshape(rows), "col")
        phi = -(rowph + row_total) / rowmass

        def apply_cols(acc, item):
            plan = plan_only(item[0], item[1], item[2])
            return (acc + jnp.dot(item[3], plan, precision=lax.Precision.HIGHEST), None)

        col_apply, unused_out = lax.scan(apply_cols, zeros_c, items + (phi.reshape(count, blk),))
        col_total = lax.psum(col_apply, "row")
        psi = -(colph + col_total) / colmass

    def last(acc, item):
        part_blk, pot_blk, sq_blk, phi_blk = item
        both = jnp.einsum("rd,cd->rc", part_blk, stacked, preferred_element_type=jnp.float32)
        plan = plan_from(both[:, :cols], pot_blk, sq_blk)
        mixed = plan * (both[:, cols:] + phi_blk[:, None] + psi[None, :])
        qrow = jnp.sum(mixed, axis=1)
        plan_bf = plan.astype(jnp.bfloat16)
        mixed_bf = mixed.astype(jnp.bfloat16)
        rowterm = jnp.dot(plan_bf, col_grads, preferred_element_type=jnp.float32)
        rowterm = rowterm + (
            jnp.dot(mixed_bf, col_parts, preferred_element_type=jnp.float32)
            - qrow[:, None] * part_blk.astype(jnp.float32)
        ) / (width * EPS)
        return (
            acc + jnp.einsum("rc,rd->cd", mixed_bf, part_blk, preferred_element_type=jnp.float32),
            rowterm,
        )

    col_acc, row_terms = lax.scan(
        last, jnp.zeros((cols, width), jnp.float32), items + (phi.reshape(count, blk),)
    )
    row_terms = row_terms.reshape(rows, width)
    start = lax.axis_index("col") * own
    summed = lax.psum(row_terms.astype(jnp.bfloat16), "col").astype(jnp.float32)
    row_own = lax.dynamic_slice_in_dim(summed, start, own, 0)
    col_own = lax.psum_scatter(
        col_acc.astype(jnp.bfloat16), "row", scatter_dimension=0, tiled=True
    ).astype(jnp.float32)
    grad_particles = (row_own + col_own / (width * EPS)).astype(jnp.bfloat16)
    phi_own = lax.dynamic_slice_in_dim(phi, start, own, 0)
    own_wts = weights.astype(jnp.float32)
    total, wphi = lax.psum((jnp.sum(own_wts), jnp.sum(own_wts * phi_own)), ("row", "col"))
    count_all = rows * lax.axis_size("row")
    grad_weights = -(count_all / total) * (phi_own - wphi / total)
    return (grad_particles, grad_weights)


LANES = 128
SUBL = 8
SUB = 64
PLAN_BYTES = 24 * 1024 * 1024


def fold(block):
    return jnp.sum(block.reshape(block.shape[0] // SUBL, SUBL, block.shape[1]), axis=0)


def lane_sums(parts):
    high = parts.astype(jnp.bfloat16)
    low = (parts - high.astype(jnp.float32)).astype(jnp.bfloat16)
    both = jnp.concatenate([high, low], axis=1)
    ones = jnp.ones((both.shape[1], LANES), jnp.bfloat16)
    return jnp.dot(both, ones, preferred_element_type=jnp.float32)


def nt(left, right):
    return lax.dot_general(
        left, right, (((1,), (1,)), ((), ())), preferred_element_type=jnp.float32
    )


def fused_kernel(
    ncol, own, pack_ref, pot_ref, gp_ref, gw_ref,
    x_all, gy_all, pots, plan, a_col, b_col, c_col, nhc_col, psi_col,
    a_lane, b_lane, w_lane, r_acc, sums_all,
    ls, zs, zr, xs, xr, ps, pr, hs, hr_sem,
):
    nrow = 4
    half = own // 2
    width = pack_ref.shape[1]
    x_ref = pack_ref.at[pl.ds(0, own)]
    gy_ref = pack_ref.at[pl.ds(own, own)]
    blocks = nrow * ncol
    total = own * blocks
    group = own * ncol
    tiles = total // LANES
    me_r = lax.axis_index("row")
    me_c = lax.axis_index("col")
    me = me_r * ncol + me_c
    xn = me_r + 1 - 2 * (me_r % 2)
    yn = (me_r + 2) % nrow
    dn = (xn + 2) % nrow
    peers = [
        ((me_r + dr) % nrow, (me_c + dc) % ncol) for dr in range(nrow) for dc in range(ncol) if dr or dc
    ]
    scale = 1.0 / (width * EPS)

    def at(row, col, part=None):
        base = (row * ncol + col) * own
        if part is None:
            return pl.ds(pl.multiple_of(base, 32), own)
        return pl.ds(pl.multiple_of(base + part * half, 16), half)

    def dev(row, col):
        return {"row": row, "col": col}

    mine = at(me_r, me_c)
    local_x = pltpu.make_async_copy(x_ref, x_all.at[mine], ls.at[0])
    local_x.start()
    local_g = pltpu.make_async_copy(gy_ref, gy_all.at[mine], ls.at[1])
    local_g.start()
    barrier = pltpu.get_barrier_semaphore()
    for row, col in peers:
        pl.semaphore_signal(
            barrier, inc=1, device_id=dev(row, col), device_id_type=pl.DeviceIdType.MESH
        )
    pots[me, :, :] = pot_ref[...]
    r_acc[...] = jnp.zeros_like(r_acc)
    c_col[...] = jnp.zeros_like(c_col)
    pl.semaphore_wait(barrier, len(peers))

    def plan_copy(src, dst, ssem, rsem, row, col):
        return pltpu.make_async_remote_copy(
            src_ref=src, dst_ref=dst, send_sem=ssem, recv_sem=rsem,
            device_id=dev(row, col), device_id_type=pl.DeviceIdType.MESH,
        )

    def copy(*args):
        c = plan_copy(*args)
        c.start()
        return c

    def send_z(buf, ref, n):
        out = []
        for dc in range(1, ncol):
            k = n * (ncol - 1) + dc - 1
            out.append(copy(ref, buf.at[mine], zs.at[k], zr.at[k], me_r, (me_c + dc) % ncol))
        return out

    def send_plane(buf, ref, n, k):
        col = (me_c + ncol - k) % ncol
        here = buf.at[at(me_r, col)]
        src = ref if k == 0 else here
        s = (n * ncol + k) * 3
        out = [
            copy(src, here, xs.at[s], xr.at[s], xn, me_c),
            copy(src, here, xs.at[s + 1], xr.at[s + 1], yn, me_c),
        ]
        if k == 0:
            out.append(copy(src, here, xs.at[s + 2], xr.at[s + 2], dn, me_c))
        else:
            here = buf.at[at(me_r, col, 0)]
            out.append(copy(here, here, xs.at[s + 2], xr.at[s + 2], dn, me_c))
        return out

    def relay(buf, n, came):
        came.wait_recv()
        here = buf.at[at(dn, me_c, 1)]
        out = []
        for dc in range(1, ncol):
            k = (2 + n) * (ncol - 1) + dc - 1
            out.append(copy(here, here, zs.at[k], zr.at[k], me_r, (me_c + dc) % ncol))
        return out

    zx = send_z(x_all, x_ref, 0)
    plane_x = [send_plane(x_all, x_ref, 0, 0)]
    pot_copies = [
        copy(pot_ref, pots.at[me], ps.at[k], pr.at[k], *peers[k]) for k in range(len(peers))
    ]
    for k in range(1, ncol):
        zx[k - 1].wait_recv()
        plane_x.append(send_plane(x_all, x_ref, 0, k))
    zx += relay(x_all, 0, plane_x[0][2])
    for c in pot_copies:
        c.wait_recv()

    eye = (
        lax.broadcasted_iota(jnp.int32, (own, LANES), 0)
        == lax.broadcasted_iota(jnp.int32, (own, LANES), 1)
    )
    eye_l = (
        lax.broadcasted_iota(jnp.int32, (LANES, LANES), 0)
        == lax.broadcasted_iota(jnp.int32, (LANES, LANES), 1)
    )

    def to_lanes(column):
        return jnp.sum(jnp.where(eye_l, column, 0.0), axis=0, keepdims=True)

    def on_diagonal(lines):
        spots = [jnp.where(eye, jnp.broadcast_to(line, (own, LANES)), 0.0) for line in lines]
        return jnp.concatenate(spots, axis=0)

    ones = jnp.ones((LANES, LANES), jnp.bfloat16)
    local_x.wait()

    def prepare(g):
        rows = pl.ds(pl.multiple_of(g * group, LANES), group)
        f, gp, w = [
            jnp.dot(
                on_diagonal(
                    [pots[g * ncol + b, :, pl.ds(k * LANES, LANES)] for b in range(ncol)]
                ).astype(jnp.bfloat16),
                ones,
                preferred_element_type=jnp.float32,
            )
            for k in range(3)
        ]
        xf = x_all[rows, :].astype(jnp.float32)
        sq = lane_sums(xf * xf) * (1.0 / (2.0 * width))
        a = (f - sq) * (1.0 / EPS)
        b = (gp - sq) * (1.0 / EPS)
        a_col[rows, :] = a
        b_col[rows, :] = b
        for t in range(group // LANES):
            lanes = pl.ds(pl.multiple_of(g * group + t * LANES, LANES), LANES)
            here = slice(t * LANES, (t + 1) * LANES)
            a_lane[0:1, lanes] = to_lanes(a[here])
            b_lane[0:1, lanes] = to_lanes(b[here])
            w_lane[0:1, lanes] = to_lanes(w[here])

    def build(gj, gi):
        down = pl.ds(pl.multiple_of(gj * group, LANES), group)
        over = pl.ds(pl.multiple_of(gi * group, LANES), group)
        cross = nt(x_all[down, :], x_all[over, :])
        accs = [jnp.zeros((SUBL, LANES), jnp.float32)] * (group // LANES)
        for s in range(group // SUB):
            rows = pl.ds(pl.multiple_of(gj * group + s * SUB, SUB), SUB)
            b = b_col[rows, :]
            part = jnp.zeros((SUB, LANES), jnp.float32)
            for t in range(group // LANES):
                lanes = pl.ds(pl.multiple_of(gi * group + t * LANES, LANES), LANES)
                piece = cross[s * SUB : (s + 1) * SUB, t * LANES : (t + 1) * LANES]
                p = jnp.exp(piece * scale + (b + a_lane[0:1, lanes]))
                plan[rows, lanes] = p
                part = part + p
                accs[t] = accs[t] + fold(p)
            c_col[rows, :] += part
        for t in range(group // LANES):
            lanes = pl.ds(pl.multiple_of(gi * group + t * LANES, LANES), LANES)
            r_acc[:, lanes] += accs[t]

    def near(u):
        return (me_r // 2 + u // 2) % 2 * 2 + (me_r % 2 + u % 2) % 2

    prepare(me_r)
    build(me_r, me_r)
    for sent in plane_x:
        sent[0].wait_recv()
    prepare(xn)
    for sent in plane_x:
        sent[1].wait_recv()
    prepare(yn)

    def early(i, carry):
        build(near(i // 3), near(i % 3))
        return carry

    lax.fori_loop(1, 9, early, 0)
    for sent in plane_x[1:]:
        sent[2].wait_recv()
    for c in zx[ncol - 1 :]:
        c.wait_recv()
    prepare(dn)

    x_own = x_all[mine, :]
    local_g.wait()
    cross_own = nt(x_own, x_all[...]) * scale
    pt_own = jnp.exp(cross_own + (b_col[mine, :][:, :1] + a_lane[...]))
    ht_own = nt(gy_all[mine, :], x_all[...])
    ph = pt_own * ht_own
    hc_own = jnp.sum(ph, axis=1, keepdims=True)
    slot = sums_all.at[me]
    slot[:, pl.ds(0, total)] = jnp.sum(fold(ph), axis=0, keepdims=True)
    slot[:, pl.ds(total, LANES)] = jnp.sum(jnp.where(eye, hc_own, 0.0), axis=0, keepdims=True)
    sum_copies = [
        copy(slot, slot, hs.at[k], hr_sem.at[k], *peers[k]) for k in range(len(peers))
    ]

    zg = send_z(gy_all, gy_ref, 1)
    plane_g = [send_plane(gy_all, gy_ref, 1, 0)]

    def late(i, carry):
        build(near(jnp.minimum(i, 3)), near(jnp.minimum(6 - i, 3)))
        return carry

    lax.fori_loop(0, 7, late, 0)
    p_own = jnp.exp(cross_own + (a_col[mine, :][:, :1] + b_lane[...]))
    w_all = w_lane[...]
    w_sum = jnp.sum(w_all, axis=1, keepdims=True)
    for c in sum_copies:
        c.wait_recv()
    for k in range(1, ncol):
        zg[k - 1].wait_recv()
        plane_g.append(send_plane(gy_all, gy_ref, 1, k))
    zg += relay(gy_all, 1, plane_g[0][2])

    for g in range(nrow):
        rows = pl.ds(g * group, group)
        inv = 1.0 / lane_sums(c_col[rows, :])
        c_col[rows, :] = inv
        lines = [sums_all[g * ncol + b, :, pl.ds(total, LANES)] for b in range(ncol)]
        nhc_col[rows, :] = -lane_sums(on_diagonal(lines)) * inv
    hr = jnp.sum(sums_all[:, :, pl.ds(0, total)], axis=0)
    inv_r = 1.0 / jnp.sum(r_acc[...], axis=0, keepdims=True)
    phi = -hr * inv_r

    def cut(value, t):
        return value[:, t * LANES : (t + 1) * LANES]

    def psi_of(g, phi):
        phi8 = jnp.broadcast_to(phi, (SUBL, total))
        parts = []
        for s in range(group // SUB):
            rows = pl.ds(pl.multiple_of(g * group + s * SUB, SUB), SUB)
            part = jnp.zeros((SUB // SUBL, SUBL, LANES), jnp.float32)
            for t in range(tiles):
                piece = plan[rows, pl.ds(t * LANES, LANES)].reshape(SUB // SUBL, SUBL, LANES)
                part = part + piece * cut(phi8, t)[None]
            parts.append(part.reshape(SUB, LANES))
        rows = pl.ds(pl.multiple_of(g * group, LANES), group)
        return nhc_col[rows, :] - lane_sums(jnp.concatenate(parts, axis=0)) * c_col[rows, :]

    def add_columns(g, psi, accs):
        out = list(accs)
        for s in range(group // SUB):
            rows = pl.ds(g * group + s * SUB, SUB)
            here = psi[s * SUB : (s + 1) * SUB]
            for t in range(tiles):
                out[t] = out[t] + fold(plan[rows, pl.ds(t * LANES, LANES)] * here)
        return out

    def sweep(i, phi):
        accs = [jnp.zeros((SUBL, LANES), jnp.float32)] * tiles
        psi = psi_of(0, phi)
        for g in range(1, nrow):
            later = psi_of(g, phi)
            accs = add_columns(g - 1, psi, accs)
            psi = later
        accs = add_columns(nrow - 1, psi, accs)
        return -(hr + jnp.sum(jnp.concatenate(accs, axis=1), axis=0, keepdims=True)) * inv_r

    phi = lax.fori_loop(1, ITERS, sweep, phi)
    for g in range(nrow):
        psi_col[pl.ds(g * group, group), :] = psi_of(g, phi)
    psi_lane = jnp.concatenate(
        [to_lanes(psi_col[pl.ds(t * LANES, LANES), :]) for t in range(tiles)], axis=1
    )
    pick = lax.broadcasted_iota(jnp.int32, (own, total), 1) == (
        lax.broadcasted_iota(jnp.int32, (own, total), 0) + me * own
    )
    phi_own = jnp.sum(jnp.where(pick, phi, 0.0), axis=1, keepdims=True)
    psi_own = psi_col[mine, :][:, :1]
    q_t = pt_own * (ht_own + (psi_own + phi))
    mix = jnp.dot(q_t.astype(jnp.bfloat16), x_all[...], preferred_element_type=jnp.float32)
    w_phi = jnp.sum(w_all * phi, axis=1, keepdims=True)
    phi_row = jnp.sum(jnp.where(eye, phi_own, 0.0), axis=0, keepdims=True)
    gw_ref[...] = (-(total / w_sum) * (phi_row - w_phi / w_sum))[:, :own]

    for k in range(ncol):
        plane_g[k][0].wait_recv()
        plane_g[k][1].wait_recv()
        if k:
            plane_g[k][2].wait_recv()
    for c in zg[ncol - 1 :]:
        c.wait_recv()
    q_own = p_own * (nt(x_own, gy_all[...]) + (phi_own + psi_lane))
    q_sum = jnp.sum(q_own, axis=1, keepdims=True)
    rowterm = jnp.dot(p_own.astype(jnp.bfloat16), gy_all[...], preferred_element_type=jnp.float32)
    mix = mix + jnp.dot(q_own.astype(jnp.bfloat16), x_all[...], preferred_element_type=jnp.float32)
    gp_ref[...] = (rowterm + (mix - q_sum * x_own.astype(jnp.float32)) * scale).astype(jnp.bfloat16)

    for c in zx + zg + pot_copies + sum_copies:
        c.wait_send()
    for sent in plane_x + plane_g:
        for c in sent:
            c.wait_send()


def local_fused(ncol, particles, cotangent, row_potential, col_potential, weights):
    own, width = particles.shape
    blocks = 4 * ncol
    total = own * blocks
    pot = jnp.pad(
        jnp.stack([row_potential, col_potential, weights]).astype(jnp.float32), ((0, 0), (0, LANES - own))
    ).reshape(1, 3 * LANES)
    pack = jnp.concatenate([particles, cotangent], axis=0)
    column = pltpu.VMEM((total, LANES), jnp.float32)
    line = pltpu.VMEM((1, total), jnp.float32)
    dma = pltpu.SemaphoreType.DMA
    vmem = pl.BlockSpec(memory_space=pltpu.VMEM)
    gp, gw = pl.pallas_call(
        functools.partial(fused_kernel, ncol, own),
        out_shape=(
            jax.ShapeDtypeStruct((own, width), jnp.bfloat16),
            jax.ShapeDtypeStruct((1, own), jnp.float32),
        ),
        in_specs=[vmem, vmem],
        out_specs=[vmem, vmem],
        scratch_shapes=[
            pltpu.VMEM((total, width), jnp.bfloat16),
            pltpu.VMEM((total, width), jnp.bfloat16),
            pltpu.VMEM((blocks, 1, 3 * LANES), jnp.float32),
            pltpu.VMEM((total, total), jnp.float32),
            column, column, column, column, column,
            line, line, line,
            pltpu.VMEM((SUBL, total), jnp.float32),
            pltpu.VMEM((blocks, 1, total + LANES), jnp.float32),
            dma((2,)),
            dma((4 * (ncol - 1),)), dma((4 * (ncol - 1),)),
            dma((6 * ncol,)), dma((6 * ncol,)),
            dma((blocks - 1,)), dma((blocks - 1,)),
            dma((blocks - 1,)), dma((blocks - 1,)),
        ],
        compiler_params=pltpu.CompilerParams(
            collective_id=0, has_side_effects=True, vmem_limit_bytes=48 * 1024 * 1024
        ),
        cost_estimate=pl.CostEstimate(
            flops=3 * total * total * width, bytes_accessed=4 * own * width, transcendentals=total * total
        ),
    )(pack, pot)
    return gp, gw.reshape(own)


def solution(mesh):
    nrow, ncol = mesh.shape["row"], mesh.shape["col"]

    def local(particles, cotangent, row_potential, col_potential, weights):
        args = (particles, cotangent, row_potential, col_potential, weights)
        own = particles.shape[0]
        total = own * nrow * ncol
        fits = own % 32 == 0 and own <= LANES and own * ncol % LANES == 0
        if nrow == 4 and ncol > 1 and fits and 4 * total * total <= PLAN_BYTES:
            return local_fused(ncol, *args)
        return local_general(*args)

    return jax.shard_map(
        local,
        mesh=mesh,
        in_specs=(
            P(("filt", "row", "col"), None),
            P(("filt", "row", "col"), None),
            P(("filt", "row", "col")),
            P(("filt", "row", "col")),
            P(("filt", "row", "col")),
        ),
        out_specs=(P(("filt", "row", "col"), None), P(("filt", "row", "col"))),
        check_vma=False,
    )
```

```python
import functools
import jax
import jax.numpy as jnp
from jax import lax
from jax.experimental import pallas as pl
from jax.experimental.pallas import tpu as pltpu
from jax.sharding import PartitionSpec as P

ITERS = 4


EPS = 0.09


def local_general(particles, cotangent, row_potential, col_potential, weights):
    row_parts, row_fpot, row_wts = (
        lax.all_gather(particles, "col", axis=0, tiled=True),
        lax.all_gather(row_potential, "col", axis=0, tiled=True),
        lax.all_gather(weights, "col", axis=0, tiled=True),
    )
    col_parts, col_grads, col_gpot = (
        lax.all_gather(particles, "row", axis=0, tiled=True),
        lax.all_gather(cotangent, "row", axis=0, tiled=True),
        lax.all_gather(col_potential, "row", axis=0, tiled=True),
    )
    own = particles.shape[0]
    width = particles.shape[1]
    rows = row_parts.shape[0]
    cols = col_parts.shape[0]
    blk = 512 if rows % 512 == 0 else rows
    count = rows // blk
    row_float = row_parts.astype(jnp.float32)
    row_sq = jnp.sum(row_float * row_float, axis=1)
    col_float = col_parts.astype(jnp.float32)
    col_sq = jnp.sum(col_float * col_float, axis=1)
    fpot = row_fpot.astype(jnp.float32)
    gpot = col_gpot.astype(jnp.float32)
    stacked = jnp.concatenate([col_parts, col_grads], axis=0)
    items = (
        row_parts.reshape(count, blk, width),
        fpot.reshape(count, blk),
        row_sq.reshape(count, blk),
    )

    def plan_from(cross, pot_blk, sq_blk):
        cost = (sq_blk[:, None] + col_sq[None, :] - 2.0 * cross) / (2.0 * width)
        return jnp.exp((pot_blk[:, None] + gpot[None, :] - cost) / EPS)

    def plan_only(part_blk, pot_blk, sq_blk):
        cross = jnp.einsum("rd,cd->rc", part_blk, col_parts, preferred_element_type=jnp.float32)
        return plan_from(cross, pot_blk, sq_blk)

    def first(carry, item):
        part_blk, pot_blk, sq_blk = item
        both = jnp.einsum("rd,cd->rc", part_blk, stacked, preferred_element_type=jnp.float32)
        plan = plan_from(both[:, :cols], pot_blk, sq_blk)
        weighted = plan * both[:, cols:]
        return (
            (carry[0] + jnp.sum(plan, axis=0), carry[1] + jnp.sum(weighted, axis=0)),
            (jnp.sum(plan, axis=1), jnp.sum(weighted, axis=1)),
        )

    zeros_c = jnp.zeros((cols,), jnp.float32)
    (colmass_part, colph_part), (rowmass_part, rowph_part) = lax.scan(
        first, (zeros_c, zeros_c), items
    )
    rowmass, rowph = lax.psum((rowmass_part.reshape(rows), rowph_part.reshape(rows)), "col")
    colmass, colph = lax.psum((colmass_part, colph_part), "row")
    psi = zeros_c
    phi = jnp.zeros((rows,), jnp.float32)
    for step in range(ITERS):

        def apply_rows(carry, item):
            plan = plan_only(item[0], item[1], item[2])
            return (carry, jnp.dot(plan, psi, precision=lax.Precision.HIGHEST))

        unused, row_apply = lax.scan(apply_rows, jnp.zeros((), jnp.float32), items)
        row_total = lax.psum(row_apply.reshape(rows), "col")
        phi = -(rowph + row_total) / rowmass

        def apply_cols(acc, item):
            plan = plan_only(item[0], item[1], item[2])
            return (acc + jnp.dot(item[3], plan, precision=lax.Precision.HIGHEST), None)

        col_apply, unused_out = lax.scan(apply_cols, zeros_c, items + (phi.reshape(count, blk),))
        col_total = lax.psum(col_apply, "row")
        psi = -(colph + col_total) / colmass

    def last(acc, item):
        part_blk, pot_blk, sq_blk, phi_blk = item
        both = jnp.einsum("rd,cd->rc", part_blk, stacked, preferred_element_type=jnp.float32)
        plan = plan_from(both[:, :cols], pot_blk, sq_blk)
        mixed = plan * (both[:, cols:] + phi_blk[:, None] + psi[None, :])
        qrow = jnp.sum(mixed, axis=1)
        plan_bf = plan.astype(jnp.bfloat16)
        mixed_bf = mixed.astype(jnp.bfloat16)
        rowterm = jnp.dot(plan_bf, col_grads, preferred_element_type=jnp.float32)
        rowterm = rowterm + (
            jnp.dot(mixed_bf, col_parts, preferred_element_type=jnp.float32)
            - qrow[:, None] * part_blk.astype(jnp.float32)
        ) / (width * EPS)
        return (
            acc + jnp.einsum("rc,rd->cd", mixed_bf, part_blk, preferred_element_type=jnp.float32),
            rowterm,
        )

    col_acc, row_terms = lax.scan(
        last, jnp.zeros((cols, width), jnp.float32), items + (phi.reshape(count, blk),)
    )
    row_terms = row_terms.reshape(rows, width)
    start = lax.axis_index("col") * own
    summed = lax.psum(row_terms.astype(jnp.bfloat16), "col").astype(jnp.float32)
    row_own = lax.dynamic_slice_in_dim(summed, start, own, 0)
    col_own = lax.psum_scatter(
        col_acc.astype(jnp.bfloat16), "row", scatter_dimension=0, tiled=True
    ).astype(jnp.float32)
    grad_particles = (row_own + col_own / (width * EPS)).astype(jnp.bfloat16)
    phi_own = lax.dynamic_slice_in_dim(phi, start, own, 0)
    own_wts = weights.astype(jnp.float32)
    total, wphi = lax.psum((jnp.sum(own_wts), jnp.sum(own_wts * phi_own)), ("row", "col"))
    count_all = rows * lax.axis_size("row")
    grad_weights = -(count_all / total) * (phi_own - wphi / total)
    return (grad_particles, grad_weights)


LANES = 128
SUBL = 8
SUB = 64
PLAN_BYTES = 24 * 1024 * 1024


def fold(block):
    return jnp.sum(block.reshape(block.shape[0] // SUBL, SUBL, block.shape[1]), axis=0)


def lane_sums(parts):
    high = parts.astype(jnp.bfloat16)
    low = (parts - high.astype(jnp.float32)).astype(jnp.bfloat16)
    both = jnp.concatenate([high, low], axis=1)
    ones = jnp.ones((both.shape[1], LANES), jnp.bfloat16)
    return jnp.dot(both, ones, preferred_element_type=jnp.float32)


def nt(left, right):
    return lax.dot_general(
        left, right, (((1,), (1,)), ((), ())), preferred_element_type=jnp.float32
    )


def fused_kernel(
    ncol, own, pack_ref, pot_ref, gp_ref, gw_ref,
    x_all, gy_all, pots, plan, a_col, b_col, c_col, nhc_col, psi_col,
    a_lane, b_lane, w_lane, r_acc, sums_all, p_own, pt_own, ht_own,
    ls, zs, zr, xs, xr, ps, pr, hs, hr_sem,
):
    nrow = 4
    half = own // 2
    width = pack_ref.shape[1]
    x_ref = pack_ref.at[pl.ds(0, own)]
    gy_ref = pack_ref.at[pl.ds(own, own)]
    blocks = nrow * ncol
    total = own * blocks
    group = own * ncol
    tiles = total // LANES
    me_r = lax.axis_index("row")
    me_c = lax.axis_index("col")
    me = me_r * ncol + me_c
    xn = me_r + 1 - 2 * (me_r % 2)
    yn = (me_r + 2) % nrow
    dn = (xn + 2) % nrow
    peers = [
        ((me_r + dr) % nrow, (me_c + dc) % ncol) for dr in range(nrow) for dc in range(ncol) if dr or dc
    ]
    scale = 1.0 / (width * EPS)

    def at(row, col, part=None):
        base = (row * ncol + col) * own
        if part is None:
            return pl.ds(pl.multiple_of(base, 32), own)
        return pl.ds(pl.multiple_of(base + part * half, 16), half)

    def dev(row, col):
        return {"row": row, "col": col}

    mine = at(me_r, me_c)
    local_x = pltpu.make_async_copy(x_ref, x_all.at[mine], ls.at[0])
    local_x.start()
    local_g = pltpu.make_async_copy(gy_ref, gy_all.at[mine], ls.at[1])
    local_g.start()
    barrier = pltpu.get_barrier_semaphore()
    for row, col in peers:
        pl.semaphore_signal(
            barrier, inc=1, device_id=dev(row, col), device_id_type=pl.DeviceIdType.MESH
        )
    pots[me, :, :] = pot_ref[...]
    r_acc[...] = jnp.zeros_like(r_acc)
    c_col[...] = jnp.zeros_like(c_col)
    pl.semaphore_wait(barrier, len(peers))

    def plan_copy(src, dst, ssem, rsem, row, col):
        return pltpu.make_async_remote_copy(
            src_ref=src, dst_ref=dst, send_sem=ssem, recv_sem=rsem,
            device_id=dev(row, col), device_id_type=pl.DeviceIdType.MESH,
        )

    def copy(*args):
        c = plan_copy(*args)
        c.start()
        return c

    def send_z(buf, ref, n):
        out = []
        for dc in range(1, ncol):
            k = n * (ncol - 1) + dc - 1
            out.append(copy(ref, buf.at[mine], zs.at[k], zr.at[k], me_r, (me_c + dc) % ncol))
        return out

    def send_plane(buf, ref, n, k):
        col = (me_c + ncol - k) % ncol
        here = buf.at[at(me_r, col)]
        src = ref if k == 0 else here
        s = (n * ncol + k) * 3
        out = [
            copy(src, here, xs.at[s], xr.at[s], xn, me_c),
            copy(src, here, xs.at[s + 1], xr.at[s + 1], yn, me_c),
        ]
        if k == 0:
            out.append(copy(src, here, xs.at[s + 2], xr.at[s + 2], dn, me_c))
        else:
            here = buf.at[at(me_r, col, 0)]
            out.append(copy(here, here, xs.at[s + 2], xr.at[s + 2], dn, me_c))
        return out

    def relay(buf, n, came):
        came.wait_recv()
        here = buf.at[at(dn, me_c, 1)]
        out = []
        for dc in range(1, ncol):
            k = (2 + n) * (ncol - 1) + dc - 1
            out.append(copy(here, here, zs.at[k], zr.at[k], me_r, (me_c + dc) % ncol))
        return out

    zx = send_z(x_all, x_ref, 0)
    plane_x = [send_plane(x_all, x_ref, 0, 0)]
    pot_copies = [
        copy(pot_ref, pots.at[me], ps.at[k], pr.at[k], *peers[k]) for k in range(len(peers))
    ]
    for k in range(1, ncol):
        zx[k - 1].wait_recv()
        plane_x.append(send_plane(x_all, x_ref, 0, k))
    zx += relay(x_all, 0, plane_x[0][2])
    zg = send_z(gy_all, gy_ref, 1)
    for c in pot_copies:
        c.wait_recv()

    eye = (
        lax.broadcasted_iota(jnp.int32, (own, LANES), 0)
        == lax.broadcasted_iota(jnp.int32, (own, LANES), 1)
    )
    eye_l = (
        lax.broadcasted_iota(jnp.int32, (LANES, LANES), 0)
        == lax.broadcasted_iota(jnp.int32, (LANES, LANES), 1)
    )

    def to_lanes(column):
        return jnp.sum(jnp.where(eye_l, column, 0.0), axis=0, keepdims=True)

    def on_diagonal(lines):
        spots = [jnp.where(eye, jnp.broadcast_to(line, (own, LANES)), 0.0) for line in lines]
        return jnp.concatenate(spots, axis=0)

    ones = jnp.ones((LANES, LANES), jnp.bfloat16)
    local_x.wait()

    def prepare(g):
        rows = pl.ds(pl.multiple_of(g * group, LANES), group)
        f, gp, w = [
            jnp.dot(
                on_diagonal(
                    [pots[g * ncol + b, :, pl.ds(k * LANES, LANES)] for b in range(ncol)]
                ).astype(jnp.bfloat16),
                ones,
                preferred_element_type=jnp.float32,
            )
            for k in range(3)
        ]
        xf = x_all[rows, :].astype(jnp.float32)
        sq = lane_sums(xf * xf) * (1.0 / (2.0 * width))
        a = (f - sq) * (1.0 / EPS)
        b = (gp - sq) * (1.0 / EPS)
        a_col[rows, :] = a
        b_col[rows, :] = b
        for t in range(group // LANES):
            lanes = pl.ds(pl.multiple_of(g * group + t * LANES, LANES), LANES)
            here = slice(t * LANES, (t + 1) * LANES)
            a_lane[0:1, lanes] = to_lanes(a[here])
            b_lane[0:1, lanes] = to_lanes(b[here])
            w_lane[0:1, lanes] = to_lanes(w[here])

    def build(gj, gi):
        down = pl.ds(pl.multiple_of(gj * group, LANES), group)
        over = pl.ds(pl.multiple_of(gi * group, LANES), group)
        cross = nt(x_all[down, :], x_all[over, :])
        accs = [jnp.zeros((SUBL, LANES), jnp.float32)] * (group // LANES)
        for s in range(group // SUB):
            rows = pl.ds(pl.multiple_of(gj * group + s * SUB, SUB), SUB)
            b = b_col[rows, :]
            part = jnp.zeros((SUB, LANES), jnp.float32)
            for t in range(group // LANES):
                lanes = pl.ds(pl.multiple_of(gi * group + t * LANES, LANES), LANES)
                piece = cross[s * SUB : (s + 1) * SUB, t * LANES : (t + 1) * LANES]
                p = jnp.exp(piece * scale + (b + a_lane[0:1, lanes]))
                plan[rows, lanes] = p
                part = part + p
                accs[t] = accs[t] + fold(p)
            c_col[rows, :] += part
        for t in range(group // LANES):
            lanes = pl.ds(pl.multiple_of(gi * group + t * LANES, LANES), LANES)
            r_acc[:, lanes] += accs[t]

    def near(u):
        return (me_r // 2 + u // 2) % 2 * 2 + (me_r % 2 + u % 2) % 2

    prepare(me_r)
    build(me_r, me_r)
    for sent in plane_x:
        sent[0].wait_recv()
    prepare(xn)
    for sent in plane_x:
        sent[1].wait_recv()
    prepare(yn)

    def early(i, carry):
        build(near(i // 3), near(i % 3))
        return carry

    lax.fori_loop(1, 9, early, 0)
    x_own = x_ref[...]
    gy_own = gy_ref[...]
    slot = sums_all.at[me]

    def own_terms(g):
        rows = pl.ds(pl.multiple_of(g * group, LANES), group)
        cross = nt(x_own, x_all[rows, :]) * scale
        a = a_col[mine, :][:, :1]
        b = b_col[mine, :][:, :1]
        p_own[:, rows] = jnp.exp(cross + (a + b_lane[0:1, rows]))
        p_t = jnp.exp(cross + (b + a_lane[0:1, rows]))
        h_t = nt(gy_own, x_all[rows, :])
        pt_own[:, rows] = p_t
        ht_own[:, rows] = h_t
        ph = p_t * h_t
        slot[:, rows] = jnp.sum(fold(ph), axis=0, keepdims=True)
        part = ph[:, :LANES]
        for t in range(1, group // LANES):
            part = part + ph[:, t * LANES : (t + 1) * LANES]
        return part

    hc_part = lax.fori_loop(
        0, 3, lambda i, part: part + own_terms(near(i)), jnp.zeros((own, LANES), jnp.float32)
    )
    for sent in plane_x[1:]:
        sent[2].wait_recv()
    for c in zx[ncol - 1 :]:
        c.wait_recv()
    prepare(dn)
    hc_own = lane_sums(hc_part + own_terms(dn))
    slot[:, pl.ds(total, LANES)] = jnp.sum(jnp.where(eye, hc_own, 0.0), axis=0, keepdims=True)
    sum_copies = [
        copy(slot, slot, hs.at[k], hr_sem.at[k], *peers[k]) for k in range(len(peers))
    ]
    plane_g = [send_plane(gy_all, gy_ref, 1, 0)]

    def late(i, carry):
        build(near(jnp.minimum(i, 3)), near(jnp.minimum(6 - i, 3)))
        return carry

    lax.fori_loop(0, 7, late, 0)
    local_g.wait()
    for k in range(1, ncol):
        zg[k - 1].wait_recv()
        plane_g.append(send_plane(gy_all, gy_ref, 1, k))
    zg += relay(gy_all, 1, plane_g[0][2])
    w_all = w_lane[...]
    w_sum = jnp.sum(w_all, axis=1, keepdims=True)
    for c in sum_copies:
        c.wait_recv()

    for g in range(nrow):
        rows = pl.ds(g * group, group)
        inv = 1.0 / lane_sums(c_col[rows, :])
        c_col[rows, :] = inv
        lines = [sums_all[g * ncol + b, :, pl.ds(total, LANES)] for b in range(ncol)]
        nhc_col[rows, :] = -lane_sums(on_diagonal(lines)) * inv
    hr = jnp.sum(sums_all[:, :, pl.ds(0, total)], axis=0)
    inv_r = 1.0 / jnp.sum(r_acc[...], axis=0, keepdims=True)
    phi = -hr * inv_r

    def cut(value, t):
        return value[:, t * LANES : (t + 1) * LANES]

    def psi_of(g, phi):
        phi8 = jnp.broadcast_to(phi, (SUBL, total))
        parts = []
        for s in range(group // SUB):
            rows = pl.ds(pl.multiple_of(g * group + s * SUB, SUB), SUB)
            part = jnp.zeros((SUB // SUBL, SUBL, LANES), jnp.float32)
            for t in range(tiles):
                piece = plan[rows, pl.ds(t * LANES, LANES)].reshape(SUB // SUBL, SUBL, LANES)
                part = part + piece * cut(phi8, t)[None]
            parts.append(part.reshape(SUB, LANES))
        rows = pl.ds(pl.multiple_of(g * group, LANES), group)
        return nhc_col[rows, :] - lane_sums(jnp.concatenate(parts, axis=0)) * c_col[rows, :]

    def add_columns(g, psi, accs):
        out = list(accs)
        for s in range(group // SUB):
            rows = pl.ds(g * group + s * SUB, SUB)
            here = psi[s * SUB : (s + 1) * SUB]
            for t in range(tiles):
                out[t] = out[t] + fold(plan[rows, pl.ds(t * LANES, LANES)] * here)
        return out

    def sweep(i, phi):
        accs = [jnp.zeros((SUBL, LANES), jnp.float32)] * tiles
        psi = psi_of(0, phi)
        for g in range(1, nrow):
            later = psi_of(g, phi)
            accs = add_columns(g - 1, psi, accs)
            psi = later
        accs = add_columns(nrow - 1, psi, accs)
        return -(hr + jnp.sum(jnp.concatenate(accs, axis=1), axis=0, keepdims=True)) * inv_r

    phi = lax.fori_loop(1, ITERS, sweep, phi)
    for g in range(nrow):
        psi_col[pl.ds(g * group, group), :] = psi_of(g, phi)
    psi_lane = jnp.concatenate(
        [to_lanes(psi_col[pl.ds(t * LANES, LANES), :]) for t in range(tiles)], axis=1
    )
    pick = lax.broadcasted_iota(jnp.int32, (own, total), 1) == (
        lax.broadcasted_iota(jnp.int32, (own, total), 0) + me * own
    )
    phi_own = jnp.sum(jnp.where(pick, phi, 0.0), axis=1, keepdims=True)
    psi_own = psi_col[mine, :][:, :1]
    q_t = pt_own[...] * (ht_own[...] + (psi_own + phi))
    mix = jnp.dot(q_t.astype(jnp.bfloat16), x_all[...], preferred_element_type=jnp.float32)
    w_phi = jnp.sum(w_all * phi, axis=1, keepdims=True)
    phi_row = jnp.sum(jnp.where(eye, phi_own, 0.0), axis=0, keepdims=True)
    gw_ref[...] = (-(total / w_sum) * (phi_row - w_phi / w_sum))[:, :own]

    for k in range(ncol):
        plane_g[k][0].wait_recv()
        plane_g[k][1].wait_recv()
        if k:
            plane_g[k][2].wait_recv()
    for c in zg[ncol - 1 :]:
        c.wait_recv()
    q_own = p_own[...] * (nt(x_own, gy_all[...]) + (phi_own + psi_lane))
    q_sum = jnp.sum(q_own, axis=1, keepdims=True)
    rowterm = jnp.dot(p_own[...].astype(jnp.bfloat16), gy_all[...], preferred_element_type=jnp.float32)
    mix = mix + jnp.dot(q_own.astype(jnp.bfloat16), x_all[...], preferred_element_type=jnp.float32)
    gp_ref[...] = (rowterm + (mix - q_sum * x_own.astype(jnp.float32)) * scale).astype(jnp.bfloat16)

    for c in zx + zg + pot_copies + sum_copies:
        c.wait_send()
    for sent in plane_x + plane_g:
        for c in sent:
            c.wait_send()


def local_fused(ncol, particles, cotangent, row_potential, col_potential, weights):
    own, width = particles.shape
    blocks = 4 * ncol
    total = own * blocks
    pot = jnp.pad(
        jnp.stack([row_potential, col_potential, weights]).astype(jnp.float32), ((0, 0), (0, LANES - own))
    ).reshape(1, 3 * LANES)
    pack = jnp.concatenate([particles, cotangent], axis=0)
    column = pltpu.VMEM((total, LANES), jnp.float32)
    strip = pltpu.VMEM((own, total), jnp.float32)
    line = pltpu.VMEM((1, total), jnp.float32)
    dma = pltpu.SemaphoreType.DMA
    vmem = pl.BlockSpec(memory_space=pltpu.VMEM)
    gp, gw = pl.pallas_call(
        functools.partial(fused_kernel, ncol, own),
        out_shape=(
            jax.ShapeDtypeStruct((own, width), jnp.bfloat16),
            jax.ShapeDtypeStruct((1, own), jnp.float32),
        ),
        in_specs=[vmem, vmem],
        out_specs=[vmem, vmem],
        scratch_shapes=[
            pltpu.VMEM((total, width), jnp.bfloat16),
            pltpu.VMEM((total, width), jnp.bfloat16),
            pltpu.VMEM((blocks, 1, 3 * LANES), jnp.float32),
            pltpu.VMEM((total, total), jnp.float32),
            column, column, column, column, column,
            line, line, line,
            pltpu.VMEM((SUBL, total), jnp.float32),
            pltpu.VMEM((blocks, 1, total + LANES), jnp.float32),
            strip, strip, strip,
            dma((2,)),
            dma((4 * (ncol - 1),)), dma((4 * (ncol - 1),)),
            dma((6 * ncol,)), dma((6 * ncol,)),
            dma((blocks - 1,)), dma((blocks - 1,)),
            dma((blocks - 1,)), dma((blocks - 1,)),
        ],
        compiler_params=pltpu.CompilerParams(
            collective_id=0, has_side_effects=True, vmem_limit_bytes=48 * 1024 * 1024
        ),
        cost_estimate=pl.CostEstimate(
            flops=3 * total * total * width, bytes_accessed=4 * own * width, transcendentals=total * total
        ),
    )(pack, pot)
    return gp, gw.reshape(own)


def solution(mesh):
    nrow, ncol = mesh.shape["row"], mesh.shape["col"]

    def local(particles, cotangent, row_potential, col_potential, weights):
        args = (particles, cotangent, row_potential, col_potential, weights)
        own = particles.shape[0]
        total = own * nrow * ncol
        fits = own % 32 == 0 and own <= LANES and own * ncol % LANES == 0
        if nrow == 4 and ncol > 1 and fits and 4 * total * total <= PLAN_BYTES:
            return local_fused(ncol, *args)
        return local_general(*args)

    return jax.shard_map(
        local,
        mesh=mesh,
        in_specs=(
            P(("filt", "row", "col"), None),
            P(("filt", "row", "col"), None),
            P(("filt", "row", "col")),
            P(("filt", "row", "col")),
            P(("filt", "row", "col")),
        ),
        out_specs=(P(("filt", "row", "col"), None), P(("filt", "row", "col"))),
        check_vma=False,
    )
```

```python
import functools
import jax
import jax.numpy as jnp
from jax import lax
from jax.experimental import pallas as pl
from jax.experimental.pallas import tpu as pltpu
from jax.sharding import PartitionSpec as P

ITERS = 4


EPS = 0.09


def local_general(particles, cotangent, row_potential, col_potential, weights):
    row_parts, row_fpot, row_wts = (
        lax.all_gather(particles, "col", axis=0, tiled=True),
        lax.all_gather(row_potential, "col", axis=0, tiled=True),
        lax.all_gather(weights, "col", axis=0, tiled=True),
    )
    col_parts, col_grads, col_gpot = (
        lax.all_gather(particles, "row", axis=0, tiled=True),
        lax.all_gather(cotangent, "row", axis=0, tiled=True),
        lax.all_gather(col_potential, "row", axis=0, tiled=True),
    )
    own = particles.shape[0]
    width = particles.shape[1]
    rows = row_parts.shape[0]
    cols = col_parts.shape[0]
    blk = 512 if rows % 512 == 0 else rows
    count = rows // blk
    row_float = row_parts.astype(jnp.float32)
    row_sq = jnp.sum(row_float * row_float, axis=1)
    col_float = col_parts.astype(jnp.float32)
    col_sq = jnp.sum(col_float * col_float, axis=1)
    fpot = row_fpot.astype(jnp.float32)
    gpot = col_gpot.astype(jnp.float32)
    stacked = jnp.concatenate([col_parts, col_grads], axis=0)
    items = (
        row_parts.reshape(count, blk, width),
        fpot.reshape(count, blk),
        row_sq.reshape(count, blk),
    )

    def plan_from(cross, pot_blk, sq_blk):
        cost = (sq_blk[:, None] + col_sq[None, :] - 2.0 * cross) / (2.0 * width)
        return jnp.exp((pot_blk[:, None] + gpot[None, :] - cost) / EPS)

    def plan_only(part_blk, pot_blk, sq_blk):
        cross = jnp.einsum("rd,cd->rc", part_blk, col_parts, preferred_element_type=jnp.float32)
        return plan_from(cross, pot_blk, sq_blk)

    def first(carry, item):
        part_blk, pot_blk, sq_blk = item
        both = jnp.einsum("rd,cd->rc", part_blk, stacked, preferred_element_type=jnp.float32)
        plan = plan_from(both[:, :cols], pot_blk, sq_blk)
        weighted = plan * both[:, cols:]
        return (
            (carry[0] + jnp.sum(plan, axis=0), carry[1] + jnp.sum(weighted, axis=0)),
            (jnp.sum(plan, axis=1), jnp.sum(weighted, axis=1)),
        )

    zeros_c = jnp.zeros((cols,), jnp.float32)
    (colmass_part, colph_part), (rowmass_part, rowph_part) = lax.scan(
        first, (zeros_c, zeros_c), items
    )
    rowmass, rowph = lax.psum((rowmass_part.reshape(rows), rowph_part.reshape(rows)), "col")
    colmass, colph = lax.psum((colmass_part, colph_part), "row")
    psi = zeros_c
    phi = jnp.zeros((rows,), jnp.float32)
    for step in range(ITERS):

        def apply_rows(carry, item):
            plan = plan_only(item[0], item[1], item[2])
            return (carry, jnp.dot(plan, psi, precision=lax.Precision.HIGHEST))

        unused, row_apply = lax.scan(apply_rows, jnp.zeros((), jnp.float32), items)
        row_total = lax.psum(row_apply.reshape(rows), "col")
        phi = -(rowph + row_total) / rowmass

        def apply_cols(acc, item):
            plan = plan_only(item[0], item[1], item[2])
            return (acc + jnp.dot(item[3], plan, precision=lax.Precision.HIGHEST), None)

        col_apply, unused_out = lax.scan(apply_cols, zeros_c, items + (phi.reshape(count, blk),))
        col_total = lax.psum(col_apply, "row")
        psi = -(colph + col_total) / colmass

    def last(acc, item):
        part_blk, pot_blk, sq_blk, phi_blk = item
        both = jnp.einsum("rd,cd->rc", part_blk, stacked, preferred_element_type=jnp.float32)
        plan = plan_from(both[:, :cols], pot_blk, sq_blk)
        mixed = plan * (both[:, cols:] + phi_blk[:, None] + psi[None, :])
        qrow = jnp.sum(mixed, axis=1)
        plan_bf = plan.astype(jnp.bfloat16)
        mixed_bf = mixed.astype(jnp.bfloat16)
        rowterm = jnp.dot(plan_bf, col_grads, preferred_element_type=jnp.float32)
        rowterm = rowterm + (
            jnp.dot(mixed_bf, col_parts, preferred_element_type=jnp.float32)
            - qrow[:, None] * part_blk.astype(jnp.float32)
        ) / (width * EPS)
        return (
            acc + jnp.einsum("rc,rd->cd", mixed_bf, part_blk, preferred_element_type=jnp.float32),
            rowterm,
        )

    col_acc, row_terms = lax.scan(
        last, jnp.zeros((cols, width), jnp.float32), items + (phi.reshape(count, blk),)
    )
    row_terms = row_terms.reshape(rows, width)
    start = lax.axis_index("col") * own
    summed = lax.psum(row_terms.astype(jnp.bfloat16), "col").astype(jnp.float32)
    row_own = lax.dynamic_slice_in_dim(summed, start, own, 0)
    col_own = lax.psum_scatter(
        col_acc.astype(jnp.bfloat16), "row", scatter_dimension=0, tiled=True
    ).astype(jnp.float32)
    grad_particles = (row_own + col_own / (width * EPS)).astype(jnp.bfloat16)
    phi_own = lax.dynamic_slice_in_dim(phi, start, own, 0)
    own_wts = weights.astype(jnp.float32)
    total, wphi = lax.psum((jnp.sum(own_wts), jnp.sum(own_wts * phi_own)), ("row", "col"))
    count_all = rows * lax.axis_size("row")
    grad_weights = -(count_all / total) * (phi_own - wphi / total)
    return (grad_particles, grad_weights)


LANES = 128
SUBL = 8
SUB = 64
PLAN_BYTES = 24 * 1024 * 1024


def fold(block):
    return jnp.sum(block.reshape(block.shape[0] // SUBL, SUBL, block.shape[1]), axis=0)


def lane_sums(parts):
    high = parts.astype(jnp.bfloat16)
    low = (parts - high.astype(jnp.float32)).astype(jnp.bfloat16)
    both = jnp.concatenate([high, low], axis=1)
    ones = jnp.ones((both.shape[1], LANES), jnp.bfloat16)
    return jnp.dot(both, ones, preferred_element_type=jnp.float32)


def nt(left, right):
    return lax.dot_general(
        left, right, (((1,), (1,)), ((), ())), preferred_element_type=jnp.float32
    )


def fused_kernel(
    ncol, own, pack_ref, pot_ref, gp_ref, gw_ref,
    x_all, gy_all, pots, plan, a_col, b_col, c_col, nhc_col, psi_col,
    a_lane, b_lane, w_lane, r_acc, sums_all, p_own, pt_own, ht_own,
    ls, zs, zr, xs, xr, ps, pr, hs, hr_sem,
):
    nrow = 4
    half = own // 2
    width = pack_ref.shape[1]
    x_ref = pack_ref.at[pl.ds(0, own)]
    gy_ref = pack_ref.at[pl.ds(own, own)]
    blocks = nrow * ncol
    total = own * blocks
    group = own * ncol
    tiles = total // LANES
    me_r = lax.axis_index("row")
    me_c = lax.axis_index("col")
    me = me_r * ncol + me_c
    xn = me_r + 1 - 2 * (me_r % 2)
    yn = (me_r + 2) % nrow
    dn = (xn + 2) % nrow
    peers = [
        ((me_r + dr) % nrow, (me_c + dc) % ncol) for dr in range(nrow) for dc in range(ncol) if dr or dc
    ]
    scale = 1.0 / (width * EPS)

    def at(row, col, part=None):
        base = (row * ncol + col) * own
        if part is None:
            return pl.ds(pl.multiple_of(base, 32), own)
        return pl.ds(pl.multiple_of(base + part * half, 16), half)

    def dev(row, col):
        return {"row": row, "col": col}

    mine = at(me_r, me_c)
    local_x = pltpu.make_async_copy(x_ref, x_all.at[mine], ls.at[0])
    local_x.start()
    local_g = pltpu.make_async_copy(gy_ref, gy_all.at[mine], ls.at[1])
    local_g.start()
    barrier = pltpu.get_barrier_semaphore()
    for row, col in peers:
        pl.semaphore_signal(
            barrier, inc=1, device_id=dev(row, col), device_id_type=pl.DeviceIdType.MESH
        )
    pots[me, :, :] = pot_ref[...]
    r_acc[...] = jnp.zeros_like(r_acc)
    c_col[...] = jnp.zeros_like(c_col)
    pl.semaphore_wait(barrier, len(peers))

    def plan_copy(src, dst, ssem, rsem, row, col):
        return pltpu.make_async_remote_copy(
            src_ref=src, dst_ref=dst, send_sem=ssem, recv_sem=rsem,
            device_id=dev(row, col), device_id_type=pl.DeviceIdType.MESH,
        )

    def copy(*args):
        c = plan_copy(*args)
        c.start()
        return c

    def send_z(buf, ref, n):
        out = []
        for dc in range(1, ncol):
            k = n * (ncol - 1) + dc - 1
            out.append(copy(ref, buf.at[mine], zs.at[k], zr.at[k], me_r, (me_c + dc) % ncol))
        return out

    def send_plane(buf, ref, n, k):
        col = (me_c + ncol - k) % ncol
        here = buf.at[at(me_r, col)]
        src = ref if k == 0 else here
        s = (n * ncol + k) * 3
        out = [
            copy(src, here, xs.at[s], xr.at[s], xn, me_c),
            copy(src, here, xs.at[s + 1], xr.at[s + 1], yn, me_c),
        ]
        if k == 0:
            out.append(copy(src, here, xs.at[s + 2], xr.at[s + 2], dn, me_c))
        else:
            here = buf.at[at(me_r, col, 0)]
            out.append(copy(here, here, xs.at[s + 2], xr.at[s + 2], dn, me_c))
        return out

    def relay(buf, n, came):
        came.wait_recv()
        here = buf.at[at(dn, me_c, 1)]
        out = []
        for dc in range(1, ncol):
            k = (2 + n) * (ncol - 1) + dc - 1
            out.append(copy(here, here, zs.at[k], zr.at[k], me_r, (me_c + dc) % ncol))
        return out

    zx = send_z(x_all, x_ref, 0)
    plane_x = [send_plane(x_all, x_ref, 0, 0)]
    pot_copies = [
        copy(pot_ref, pots.at[me], ps.at[k], pr.at[k], *peers[k]) for k in range(len(peers))
    ]
    for k in range(1, ncol):
        zx[k - 1].wait_recv()
        plane_x.append(send_plane(x_all, x_ref, 0, k))
    zx += relay(x_all, 0, plane_x[0][2])
    zg = send_z(gy_all, gy_ref, 1)
    for c in pot_copies:
        c.wait_recv()

    eye = (
        lax.broadcasted_iota(jnp.int32, (own, LANES), 0)
        == lax.broadcasted_iota(jnp.int32, (own, LANES), 1)
    )
    eye_l = (
        lax.broadcasted_iota(jnp.int32, (LANES, LANES), 0)
        == lax.broadcasted_iota(jnp.int32, (LANES, LANES), 1)
    )

    def to_lanes(column):
        return jnp.sum(jnp.where(eye_l, column, 0.0), axis=0, keepdims=True)

    def on_diagonal(lines):
        spots = [jnp.where(eye, jnp.broadcast_to(line, (own, LANES)), 0.0) for line in lines]
        return jnp.concatenate(spots, axis=0)

    ones = jnp.ones((LANES, LANES), jnp.bfloat16)
    local_x.wait()

    def prepare(g):
        rows = pl.ds(pl.multiple_of(g * group, LANES), group)
        f, gp, w = [
            jnp.dot(
                on_diagonal(
                    [pots[g * ncol + b, :, pl.ds(k * LANES, LANES)] for b in range(ncol)]
                ).astype(jnp.bfloat16),
                ones,
                preferred_element_type=jnp.float32,
            )
            for k in range(3)
        ]
        xf = x_all[rows, :].astype(jnp.float32)
        sq = lane_sums(xf * xf) * (1.0 / (2.0 * width))
        a = (f - sq) * (1.0 / EPS)
        b = (gp - sq) * (1.0 / EPS)
        a_col[rows, :] = a
        b_col[rows, :] = b
        for t in range(group // LANES):
            lanes = pl.ds(pl.multiple_of(g * group + t * LANES, LANES), LANES)
            here = slice(t * LANES, (t + 1) * LANES)
            a_lane[0:1, lanes] = to_lanes(a[here])
            b_lane[0:1, lanes] = to_lanes(b[here])
            w_lane[0:1, lanes] = to_lanes(w[here])

    def build(gj, gi):
        down = pl.ds(pl.multiple_of(gj * group, LANES), group)
        over = pl.ds(pl.multiple_of(gi * group, LANES), group)
        cross = nt(x_all[down, :], x_all[over, :])
        accs = [jnp.zeros((SUBL, LANES), jnp.float32)] * (group // LANES)
        for s in range(group // SUB):
            rows = pl.ds(pl.multiple_of(gj * group + s * SUB, SUB), SUB)
            b = b_col[rows, :]
            part = jnp.zeros((SUB, LANES), jnp.float32)
            for t in range(group // LANES):
                lanes = pl.ds(pl.multiple_of(gi * group + t * LANES, LANES), LANES)
                piece = cross[s * SUB : (s + 1) * SUB, t * LANES : (t + 1) * LANES]
                p = jnp.exp(piece * scale + (b + a_lane[0:1, lanes]))
                plan[rows, lanes] = p
                part = part + p
                accs[t] = accs[t] + fold(p)
            c_col[rows, :] += part
        for t in range(group // LANES):
            lanes = pl.ds(pl.multiple_of(gi * group + t * LANES, LANES), LANES)
            r_acc[:, lanes] += accs[t]

    def near(u):
        return (me_r // 2 + u // 2) % 2 * 2 + (me_r % 2 + u % 2) % 2

    prepare(me_r)
    build(me_r, me_r)
    for sent in plane_x:
        sent[0].wait_recv()
        sent[1].wait_recv()

    def prepare_near(u, carry):
        prepare(near(u))
        return carry

    lax.fori_loop(1, 3, prepare_near, 0)

    def early(i, carry):
        build(near(i // 3), near(i % 3))
        return carry

    lax.fori_loop(1, 9, early, 0)
    x_own = x_ref[...]
    gy_own = gy_ref[...]
    slot = sums_all.at[me]

    def own_terms(g):
        rows = pl.ds(pl.multiple_of(g * group, LANES), group)
        cross = nt(x_own, x_all[rows, :]) * scale
        a = a_col[mine, :][:, :1]
        b = b_col[mine, :][:, :1]
        p_own[:, rows] = jnp.exp(cross + (a + b_lane[0:1, rows]))
        p_t = jnp.exp(cross + (b + a_lane[0:1, rows]))
        h_t = nt(gy_own, x_all[rows, :])
        pt_own[:, rows] = p_t
        ht_own[:, rows] = h_t
        ph = p_t * h_t
        slot[:, rows] = jnp.sum(fold(ph), axis=0, keepdims=True)
        part = ph[:, :LANES]
        for t in range(1, group // LANES):
            part = part + ph[:, t * LANES : (t + 1) * LANES]
        return part

    hc_part = lax.fori_loop(
        0, 3, lambda i, part: part + own_terms(near(i)), jnp.zeros((own, LANES), jnp.float32)
    )
    for sent in plane_x[1:]:
        sent[2].wait_recv()
    for c in zx[ncol - 1 :]:
        c.wait_recv()
    prepare(dn)
    hc_own = lane_sums(hc_part + own_terms(dn))
    slot[:, pl.ds(total, LANES)] = jnp.sum(jnp.where(eye, hc_own, 0.0), axis=0, keepdims=True)
    sum_copies = [
        copy(slot, slot, hs.at[k], hr_sem.at[k], *peers[k]) for k in range(len(peers))
    ]

    def late(i, carry):
        build(near(jnp.minimum(i, 3)), near(jnp.minimum(6 - i, 3)))
        return carry

    lax.fori_loop(0, 7, late, 0)
    local_g.wait()
    plane_g = [send_plane(gy_all, gy_ref, 1, 0)]
    for k in range(1, ncol):
        zg[k - 1].wait_recv()
        plane_g.append(send_plane(gy_all, gy_ref, 1, k))
    zg += relay(gy_all, 1, plane_g[0][2])
    w_all = w_lane[...]
    w_sum = jnp.sum(w_all, axis=1, keepdims=True)
    for c in sum_copies:
        c.wait_recv()

    def masses(g, carry):
        rows = pl.ds(pl.multiple_of(g * group, LANES), group)
        inv = 1.0 / lane_sums(c_col[rows, :])
        c_col[rows, :] = inv
        lines = [sums_all[g * ncol + b, :, pl.ds(total, LANES)] for b in range(ncol)]
        nhc_col[rows, :] = -lane_sums(on_diagonal(lines)) * inv
        return carry

    lax.fori_loop(0, nrow, masses, 0)
    hr = jnp.sum(sums_all[:, :, pl.ds(0, total)], axis=0)
    inv_r = 1.0 / jnp.sum(r_acc[...], axis=0, keepdims=True)
    phi = -hr * inv_r

    def cut(value, t):
        return value[:, t * LANES : (t + 1) * LANES]

    def psi_of(g, phi):
        phi8 = jnp.broadcast_to(phi, (SUBL, total))
        parts = []
        for s in range(group // SUB):
            rows = pl.ds(pl.multiple_of(g * group + s * SUB, SUB), SUB)
            part = jnp.zeros((SUB // SUBL, SUBL, LANES), jnp.float32)
            for t in range(tiles):
                piece = plan[rows, pl.ds(t * LANES, LANES)].reshape(SUB // SUBL, SUBL, LANES)
                part = part + piece * cut(phi8, t)[None]
            parts.append(part.reshape(SUB, LANES))
        rows = pl.ds(pl.multiple_of(g * group, LANES), group)
        return nhc_col[rows, :] - lane_sums(jnp.concatenate(parts, axis=0)) * c_col[rows, :]

    def add_columns(g, psi, accs):
        out = list(accs)
        for s in range(group // SUB):
            rows = pl.ds(g * group + s * SUB, SUB)
            here = psi[s * SUB : (s + 1) * SUB]
            for t in range(tiles):
                out[t] = out[t] + fold(plan[rows, pl.ds(t * LANES, LANES)] * here)
        return out

    def sweep(i, phi):
        accs = [jnp.zeros((SUBL, LANES), jnp.float32)] * tiles
        psi = psi_of(0, phi)
        for g in range(1, nrow):
            later = psi_of(g, phi)
            accs = add_columns(g - 1, psi, accs)
            psi = later
        accs = add_columns(nrow - 1, psi, accs)
        return -(hr + jnp.sum(jnp.concatenate(accs, axis=1), axis=0, keepdims=True)) * inv_r

    phi = lax.fori_loop(1, ITERS, sweep, phi)

    def last(g, carry):
        psi_col[pl.ds(pl.multiple_of(g * group, LANES), group), :] = psi_of(g, phi)
        return carry

    lax.fori_loop(0, nrow, last, 0)
    psi_lane = jnp.concatenate(
        [to_lanes(psi_col[pl.ds(t * LANES, LANES), :]) for t in range(tiles)], axis=1
    )
    pick = lax.broadcasted_iota(jnp.int32, (own, total), 1) == (
        lax.broadcasted_iota(jnp.int32, (own, total), 0) + me * own
    )
    phi_own = jnp.sum(jnp.where(pick, phi, 0.0), axis=1, keepdims=True)
    psi_own = psi_col[mine, :][:, :1]
    q_t = pt_own[...] * (ht_own[...] + (psi_own + phi))
    mix = jnp.dot(q_t.astype(jnp.bfloat16), x_all[...], preferred_element_type=jnp.float32)
    w_phi = jnp.sum(w_all * phi, axis=1, keepdims=True)
    phi_row = jnp.sum(jnp.where(eye, phi_own, 0.0), axis=0, keepdims=True)
    gw_ref[...] = (-(total / w_sum) * (phi_row - w_phi / w_sum))[:, :own]

    for k in range(ncol):
        plane_g[k][0].wait_recv()
        plane_g[k][1].wait_recv()
        if k:
            plane_g[k][2].wait_recv()
    for c in zg[ncol - 1 :]:
        c.wait_recv()
    q_own = p_own[...] * (nt(x_own, gy_all[...]) + (phi_own + psi_lane))
    q_sum = jnp.sum(q_own, axis=1, keepdims=True)
    rowterm = jnp.dot(p_own[...].astype(jnp.bfloat16), gy_all[...], preferred_element_type=jnp.float32)
    mix = mix + jnp.dot(q_own.astype(jnp.bfloat16), x_all[...], preferred_element_type=jnp.float32)
    gp_ref[...] = (rowterm + (mix - q_sum * x_own.astype(jnp.float32)) * scale).astype(jnp.bfloat16)

    for c in zx + zg + pot_copies + sum_copies:
        c.wait_send()
    for sent in plane_x + plane_g:
        for c in sent:
            c.wait_send()


def local_fused(ncol, particles, cotangent, row_potential, col_potential, weights):
    own, width = particles.shape
    blocks = 4 * ncol
    total = own * blocks
    pot = jnp.pad(
        jnp.stack([row_potential, col_potential, weights]).astype(jnp.float32), ((0, 0), (0, LANES - own))
    ).reshape(1, 3 * LANES)
    pack = jnp.concatenate([particles, cotangent], axis=0)
    column = pltpu.VMEM((total, LANES), jnp.float32)
    strip = pltpu.VMEM((own, total), jnp.float32)
    line = pltpu.VMEM((1, total), jnp.float32)
    dma = pltpu.SemaphoreType.DMA
    vmem = pl.BlockSpec(memory_space=pltpu.VMEM)
    gp, gw = pl.pallas_call(
        functools.partial(fused_kernel, ncol, own),
        out_shape=(
            jax.ShapeDtypeStruct((own, width), jnp.bfloat16),
            jax.ShapeDtypeStruct((1, own), jnp.float32),
        ),
        in_specs=[vmem, vmem],
        out_specs=[vmem, vmem],
        scratch_shapes=[
            pltpu.VMEM((total, width), jnp.bfloat16),
            pltpu.VMEM((total, width), jnp.bfloat16),
            pltpu.VMEM((blocks, 1, 3 * LANES), jnp.float32),
            pltpu.VMEM((total, total), jnp.float32),
            column, column, column, column, column,
            line, line, line,
            pltpu.VMEM((SUBL, total), jnp.float32),
            pltpu.VMEM((blocks, 1, total + LANES), jnp.float32),
            strip, strip, strip,
            dma((2,)),
            dma((4 * (ncol - 1),)), dma((4 * (ncol - 1),)),
            dma((6 * ncol,)), dma((6 * ncol,)),
            dma((blocks - 1,)), dma((blocks - 1,)),
            dma((blocks - 1,)), dma((blocks - 1,)),
        ],
        compiler_params=pltpu.CompilerParams(
            collective_id=0, has_side_effects=True, vmem_limit_bytes=48 * 1024 * 1024
        ),
        cost_estimate=pl.CostEstimate(
            flops=3 * total * total * width, bytes_accessed=4 * own * width, transcendentals=total * total
        ),
    )(pack, pot)
    return gp, gw.reshape(own)


def solution(mesh):
    nrow, ncol = mesh.shape["row"], mesh.shape["col"]

    def local(particles, cotangent, row_potential, col_potential, weights):
        args = (particles, cotangent, row_potential, col_potential, weights)
        own = particles.shape[0]
        total = own * nrow * ncol
        fits = own % 32 == 0 and own <= LANES and own * ncol % LANES == 0
        if nrow == 4 and ncol > 1 and fits and 4 * total * total <= PLAN_BYTES:
            return local_fused(ncol, *args)
        return local_general(*args)

    return jax.shard_map(
        local,
        mesh=mesh,
        in_specs=(
            P(("filt", "row", "col"), None),
            P(("filt", "row", "col"), None),
            P(("filt", "row", "col")),
            P(("filt", "row", "col")),
            P(("filt", "row", "col")),
        ),
        out_specs=(P(("filt", "row", "col"), None), P(("filt", "row", "col"))),
        check_vma=False,
    )
```

```python
import functools
import jax
import jax.numpy as jnp
from jax import lax
from jax.experimental import pallas as pl
from jax.experimental.pallas import tpu as pltpu
from jax.sharding import PartitionSpec as P

ITERS = 4


EPS = 0.09


def local_general(particles, cotangent, row_potential, col_potential, weights):
    row_parts, row_fpot, row_wts = (
        lax.all_gather(particles, "col", axis=0, tiled=True),
        lax.all_gather(row_potential, "col", axis=0, tiled=True),
        lax.all_gather(weights, "col", axis=0, tiled=True),
    )
    col_parts, col_grads, col_gpot = (
        lax.all_gather(particles, "row", axis=0, tiled=True),
        lax.all_gather(cotangent, "row", axis=0, tiled=True),
        lax.all_gather(col_potential, "row", axis=0, tiled=True),
    )
    own = particles.shape[0]
    width = particles.shape[1]
    rows = row_parts.shape[0]
    cols = col_parts.shape[0]
    blk = 512 if rows % 512 == 0 else rows
    count = rows // blk
    row_float = row_parts.astype(jnp.float32)
    row_sq = jnp.sum(row_float * row_float, axis=1)
    col_float = col_parts.astype(jnp.float32)
    col_sq = jnp.sum(col_float * col_float, axis=1)
    fpot = row_fpot.astype(jnp.float32)
    gpot = col_gpot.astype(jnp.float32)
    stacked = jnp.concatenate([col_parts, col_grads], axis=0)
    items = (
        row_parts.reshape(count, blk, width),
        fpot.reshape(count, blk),
        row_sq.reshape(count, blk),
    )

    def plan_from(cross, pot_blk, sq_blk):
        cost = (sq_blk[:, None] + col_sq[None, :] - 2.0 * cross) / (2.0 * width)
        return jnp.exp((pot_blk[:, None] + gpot[None, :] - cost) / EPS)

    def plan_only(part_blk, pot_blk, sq_blk):
        cross = jnp.einsum("rd,cd->rc", part_blk, col_parts, preferred_element_type=jnp.float32)
        return plan_from(cross, pot_blk, sq_blk)

    def first(carry, item):
        part_blk, pot_blk, sq_blk = item
        both = jnp.einsum("rd,cd->rc", part_blk, stacked, preferred_element_type=jnp.float32)
        plan = plan_from(both[:, :cols], pot_blk, sq_blk)
        weighted = plan * both[:, cols:]
        return (
            (carry[0] + jnp.sum(plan, axis=0), carry[1] + jnp.sum(weighted, axis=0)),
            (jnp.sum(plan, axis=1), jnp.sum(weighted, axis=1)),
        )

    zeros_c = jnp.zeros((cols,), jnp.float32)
    (colmass_part, colph_part), (rowmass_part, rowph_part) = lax.scan(
        first, (zeros_c, zeros_c), items
    )
    rowmass, rowph = lax.psum((rowmass_part.reshape(rows), rowph_part.reshape(rows)), "col")
    colmass, colph = lax.psum((colmass_part, colph_part), "row")
    psi = zeros_c
    phi = jnp.zeros((rows,), jnp.float32)
    for step in range(ITERS):

        def apply_rows(carry, item):
            plan = plan_only(item[0], item[1], item[2])
            return (carry, jnp.dot(plan, psi, precision=lax.Precision.HIGHEST))

        unused, row_apply = lax.scan(apply_rows, jnp.zeros((), jnp.float32), items)
        row_total = lax.psum(row_apply.reshape(rows), "col")
        phi = -(rowph + row_total) / rowmass

        def apply_cols(acc, item):
            plan = plan_only(item[0], item[1], item[2])
            return (acc + jnp.dot(item[3], plan, precision=lax.Precision.HIGHEST), None)

        col_apply, unused_out = lax.scan(apply_cols, zeros_c, items + (phi.reshape(count, blk),))
        col_total = lax.psum(col_apply, "row")
        psi = -(colph + col_total) / colmass

    def last(acc, item):
        part_blk, pot_blk, sq_blk, phi_blk = item
        both = jnp.einsum("rd,cd->rc", part_blk, stacked, preferred_element_type=jnp.float32)
        plan = plan_from(both[:, :cols], pot_blk, sq_blk)
        mixed = plan * (both[:, cols:] + phi_blk[:, None] + psi[None, :])
        qrow = jnp.sum(mixed, axis=1)
        plan_bf = plan.astype(jnp.bfloat16)
        mixed_bf = mixed.astype(jnp.bfloat16)
        rowterm = jnp.dot(plan_bf, col_grads, preferred_element_type=jnp.float32)
        rowterm = rowterm + (
            jnp.dot(mixed_bf, col_parts, preferred_element_type=jnp.float32)
            - qrow[:, None] * part_blk.astype(jnp.float32)
        ) / (width * EPS)
        return (
            acc + jnp.einsum("rc,rd->cd", mixed_bf, part_blk, preferred_element_type=jnp.float32),
            rowterm,
        )

    col_acc, row_terms = lax.scan(
        last, jnp.zeros((cols, width), jnp.float32), items + (phi.reshape(count, blk),)
    )
    row_terms = row_terms.reshape(rows, width)
    start = lax.axis_index("col") * own
    summed = lax.psum(row_terms.astype(jnp.bfloat16), "col").astype(jnp.float32)
    row_own = lax.dynamic_slice_in_dim(summed, start, own, 0)
    col_own = lax.psum_scatter(
        col_acc.astype(jnp.bfloat16), "row", scatter_dimension=0, tiled=True
    ).astype(jnp.float32)
    grad_particles = (row_own + col_own / (width * EPS)).astype(jnp.bfloat16)
    phi_own = lax.dynamic_slice_in_dim(phi, start, own, 0)
    own_wts = weights.astype(jnp.float32)
    total, wphi = lax.psum((jnp.sum(own_wts), jnp.sum(own_wts * phi_own)), ("row", "col"))
    count_all = rows * lax.axis_size("row")
    grad_weights = -(count_all / total) * (phi_own - wphi / total)
    return (grad_particles, grad_weights)


LANES = 128
SUBL = 8
SUB = 64
PLAN_BYTES = 24 * 1024 * 1024


def fold(block):
    return jnp.sum(block.reshape(block.shape[0] // SUBL, SUBL, block.shape[1]), axis=0)


def lane_sums(parts):
    high = parts.astype(jnp.bfloat16)
    low = (parts - high.astype(jnp.float32)).astype(jnp.bfloat16)
    both = jnp.concatenate([high, low], axis=1)
    ones = jnp.ones((both.shape[1], LANES), jnp.bfloat16)
    return jnp.dot(both, ones, preferred_element_type=jnp.float32)


def nt(left, right):
    return lax.dot_general(
        left, right, (((1,), (1,)), ((), ())), preferred_element_type=jnp.float32
    )


def fused_kernel(
    ncol, own, pack_ref, pot_ref, gp_ref, gw_ref,
    x_all, gy_all, pots, plan, a_col, b_col, c_col, nhc_col, psi_col,
    a_lane, b_lane, w_lane, r_acc, sums_all, p_own, pt_own, ht_own,
    ls, zs, zr, xs, xr, ps, pr, hs, hr_sem,
):
    nrow = 4
    half = own // 2
    width = pack_ref.shape[1]
    x_ref = pack_ref.at[pl.ds(0, own)]
    gy_ref = pack_ref.at[pl.ds(own, own)]
    blocks = nrow * ncol
    total = own * blocks
    group = own * ncol
    tiles = total // LANES
    me_r = lax.axis_index("row")
    me_c = lax.axis_index("col")
    me = me_r * ncol + me_c
    xn = me_r + 1 - 2 * (me_r % 2)
    yn = (me_r + 2) % nrow
    dn = (xn + 2) % nrow
    peers = [
        ((me_r + dr) % nrow, (me_c + dc) % ncol) for dr in range(nrow) for dc in range(ncol) if dr or dc
    ]
    scale = 1.0 / (width * EPS)

    def at(row, col, part=None):
        base = (row * ncol + col) * own
        if part is None:
            return pl.ds(pl.multiple_of(base, 32), own)
        return pl.ds(pl.multiple_of(base + part * half, 16), half)

    def dev(row, col):
        return {"row": row, "col": col}

    mine = at(me_r, me_c)
    local_x = pltpu.make_async_copy(x_ref, x_all.at[mine], ls.at[0])
    local_x.start()
    local_g = pltpu.make_async_copy(gy_ref, gy_all.at[mine], ls.at[1])
    local_g.start()
    barrier = pltpu.get_barrier_semaphore()
    for row, col in peers:
        pl.semaphore_signal(
            barrier, inc=1, device_id=dev(row, col), device_id_type=pl.DeviceIdType.MESH
        )
    pots[me, :, :] = pot_ref[...]
    r_acc[...] = jnp.zeros_like(r_acc)
    c_col[...] = jnp.zeros_like(c_col)
    pl.semaphore_wait(barrier, len(peers))

    def plan_copy(src, dst, ssem, rsem, row, col):
        return pltpu.make_async_remote_copy(
            src_ref=src, dst_ref=dst, send_sem=ssem, recv_sem=rsem,
            device_id=dev(row, col), device_id_type=pl.DeviceIdType.MESH,
        )

    def copy(*args):
        c = plan_copy(*args)
        c.start()
        return c

    def send_z(buf, ref, n):
        out = []
        for dc in range(1, ncol):
            k = n * (ncol - 1) + dc - 1
            out.append(copy(ref, buf.at[mine], zs.at[k], zr.at[k], me_r, (me_c + dc) % ncol))
        return out

    def send_plane(buf, ref, n, k):
        col = (me_c + ncol - k) % ncol
        here = buf.at[at(me_r, col)]
        src = ref if k == 0 else here
        s = (n * ncol + k) * 3
        out = [
            copy(src, here, xs.at[s], xr.at[s], xn, me_c),
            copy(src, here, xs.at[s + 1], xr.at[s + 1], yn, me_c),
        ]
        if k == 0:
            out.append(copy(src, here, xs.at[s + 2], xr.at[s + 2], dn, me_c))
        else:
            here = buf.at[at(me_r, col, 0)]
            out.append(copy(here, here, xs.at[s + 2], xr.at[s + 2], dn, me_c))
        return out

    def relay(buf, n, came):
        came.wait_recv()
        here = buf.at[at(dn, me_c, 1)]
        out = []
        for dc in range(1, ncol):
            k = (2 + n) * (ncol - 1) + dc - 1
            out.append(copy(here, here, zs.at[k], zr.at[k], me_r, (me_c + dc) % ncol))
        return out

    zx = send_z(x_all, x_ref, 0)
    plane_x = [send_plane(x_all, x_ref, 0, 0)]
    pot_copies = [
        copy(pot_ref, pots.at[me], ps.at[k], pr.at[k], *peers[k]) for k in range(len(peers))
    ]
    for k in range(1, ncol):
        zx[k - 1].wait_recv()
        plane_x.append(send_plane(x_all, x_ref, 0, k))
    zx += relay(x_all, 0, plane_x[0][2])
    zg = send_z(gy_all, gy_ref, 1)
    plane_g = [send_plane(gy_all, gy_ref, 1, 0)]
    for c in pot_copies:
        c.wait_recv()

    eye = (
        lax.broadcasted_iota(jnp.int32, (own, LANES), 0)
        == lax.broadcasted_iota(jnp.int32, (own, LANES), 1)
    )
    eye_l = (
        lax.broadcasted_iota(jnp.int32, (LANES, LANES), 0)
        == lax.broadcasted_iota(jnp.int32, (LANES, LANES), 1)
    )

    def to_lanes(column):
        return jnp.sum(jnp.where(eye_l, column, 0.0), axis=0, keepdims=True)

    def on_diagonal(lines):
        spots = [jnp.where(eye, jnp.broadcast_to(line, (own, LANES)), 0.0) for line in lines]
        return jnp.concatenate(spots, axis=0)

    ones = jnp.ones((LANES, LANES), jnp.bfloat16)
    local_x.wait()

    def prepare(g):
        rows = pl.ds(pl.multiple_of(g * group, LANES), group)
        f, gp, w = [
            jnp.dot(
                on_diagonal(
                    [pots[g * ncol + b, :, pl.ds(k * LANES, LANES)] for b in range(ncol)]
                ).astype(jnp.bfloat16),
                ones,
                preferred_element_type=jnp.float32,
            )
            for k in range(3)
        ]
        xf = x_all[rows, :].astype(jnp.float32)
        sq = lane_sums(xf * xf) * (1.0 / (2.0 * width))
        a = (f - sq) * (1.0 / EPS)
        b = (gp - sq) * (1.0 / EPS)
        a_col[rows, :] = a
        b_col[rows, :] = b
        for t in range(group // LANES):
            lanes = pl.ds(pl.multiple_of(g * group + t * LANES, LANES), LANES)
            here = slice(t * LANES, (t + 1) * LANES)
            a_lane[0:1, lanes] = to_lanes(a[here])
            b_lane[0:1, lanes] = to_lanes(b[here])
            w_lane[0:1, lanes] = to_lanes(w[here])

    def build(gj, gi):
        down = pl.ds(pl.multiple_of(gj * group, LANES), group)
        over = pl.ds(pl.multiple_of(gi * group, LANES), group)
        cross = nt(x_all[down, :], x_all[over, :])
        accs = [jnp.zeros((SUBL, LANES), jnp.float32)] * (group // LANES)
        for s in range(group // SUB):
            rows = pl.ds(pl.multiple_of(gj * group + s * SUB, SUB), SUB)
            b = b_col[rows, :]
            part = jnp.zeros((SUB, LANES), jnp.float32)
            for t in range(group // LANES):
                lanes = pl.ds(pl.multiple_of(gi * group + t * LANES, LANES), LANES)
                piece = cross[s * SUB : (s + 1) * SUB, t * LANES : (t + 1) * LANES]
                p = jnp.exp(piece * scale + (b + a_lane[0:1, lanes]))
                plan[rows, lanes] = p
                part = part + p
                accs[t] = accs[t] + fold(p)
            c_col[rows, :] += part
        for t in range(group // LANES):
            lanes = pl.ds(pl.multiple_of(gi * group + t * LANES, LANES), LANES)
            r_acc[:, lanes] += accs[t]

    def near(u):
        return (me_r // 2 + u // 2) % 2 * 2 + (me_r % 2 + u % 2) % 2

    prepare(me_r)
    build(me_r, me_r)
    for sent in plane_x:
        sent[0].wait_recv()
    prepare(xn)
    for sent in plane_x:
        sent[1].wait_recv()
    prepare(yn)

    def early(i, carry):
        build(near(i // 3), near(i % 3))
        return carry

    lax.fori_loop(1, 9, early, 0)
    x_own = x_ref[...]
    gy_own = gy_ref[...]
    slot = sums_all.at[me]

    def own_terms(g):
        rows = pl.ds(pl.multiple_of(g * group, LANES), group)
        cross = nt(x_own, x_all[rows, :]) * scale
        a = a_col[mine, :][:, :1]
        b = b_col[mine, :][:, :1]
        p_own[:, rows] = jnp.exp(cross + (a + b_lane[0:1, rows]))
        p_t = jnp.exp(cross + (b + a_lane[0:1, rows]))
        h_t = nt(gy_own, x_all[rows, :])
        pt_own[:, rows] = p_t
        ht_own[:, rows] = h_t
        ph = p_t * h_t
        slot[:, rows] = jnp.sum(fold(ph), axis=0, keepdims=True)
        part = ph[:, :LANES]
        for t in range(1, group // LANES):
            part = part + ph[:, t * LANES : (t + 1) * LANES]
        return part

    hc_part = lax.fori_loop(
        0, 3, lambda i, part: part + own_terms(near(i)), jnp.zeros((own, LANES), jnp.float32)
    )
    for sent in plane_x[1:]:
        sent[2].wait_recv()
    for c in zx[ncol - 1 :]:
        c.wait_recv()
    prepare(dn)
    hc_own = lane_sums(hc_part + own_terms(dn))
    slot[:, pl.ds(total, LANES)] = jnp.sum(jnp.where(eye, hc_own, 0.0), axis=0, keepdims=True)
    sum_copies = [
        copy(slot, slot, hs.at[k], hr_sem.at[k], *peers[k]) for k in range(len(peers))
    ]
    for k in range(1, ncol):
        zg[k - 1].wait_recv()
        plane_g.append(send_plane(gy_all, gy_ref, 1, k))
    zg += relay(gy_all, 1, plane_g[0][2])

    def late(i, carry):
        build(near(jnp.minimum(i, 3)), near(jnp.minimum(6 - i, 3)))
        return carry

    lax.fori_loop(0, 7, late, 0)
    local_g.wait()
    w_all = w_lane[...]
    w_sum = jnp.sum(w_all, axis=1, keepdims=True)
    for c in sum_copies:
        c.wait_recv()

    for g in range(nrow):
        rows = pl.ds(g * group, group)
        inv = 1.0 / lane_sums(c_col[rows, :])
        c_col[rows, :] = inv
        lines = [sums_all[g * ncol + b, :, pl.ds(total, LANES)] for b in range(ncol)]
        nhc_col[rows, :] = -lane_sums(on_diagonal(lines)) * inv
    hr = jnp.sum(sums_all[:, :, pl.ds(0, total)], axis=0)
    inv_r = 1.0 / jnp.sum(r_acc[...], axis=0, keepdims=True)
    phi = -hr * inv_r

    def cut(value, t):
        return value[:, t * LANES : (t + 1) * LANES]

    def psi_of(g, phi):
        phi8 = jnp.broadcast_to(phi, (SUBL, total))
        parts = []
        for s in range(group // SUB):
            rows = pl.ds(pl.multiple_of(g * group + s * SUB, SUB), SUB)
            part = jnp.zeros((SUB // SUBL, SUBL, LANES), jnp.float32)
            for t in range(tiles):
                piece = plan[rows, pl.ds(t * LANES, LANES)].reshape(SUB // SUBL, SUBL, LANES)
                part = part + piece * cut(phi8, t)[None]
            parts.append(part.reshape(SUB, LANES))
        rows = pl.ds(pl.multiple_of(g * group, LANES), group)
        return nhc_col[rows, :] - lane_sums(jnp.concatenate(parts, axis=0)) * c_col[rows, :]

    def add_columns(g, psi, accs):
        out = list(accs)
        for s in range(group // SUB):
            rows = pl.ds(g * group + s * SUB, SUB)
            here = psi[s * SUB : (s + 1) * SUB]
            for t in range(tiles):
                out[t] = out[t] + fold(plan[rows, pl.ds(t * LANES, LANES)] * here)
        return out

    def sweep(i, phi):
        accs = [jnp.zeros((SUBL, LANES), jnp.float32)] * tiles
        psi = psi_of(0, phi)
        for g in range(1, nrow):
            later = psi_of(g, phi)
            accs = add_columns(g - 1, psi, accs)
            psi = later
        accs = add_columns(nrow - 1, psi, accs)
        return -(hr + jnp.sum(jnp.concatenate(accs, axis=1), axis=0, keepdims=True)) * inv_r

    phi = lax.fori_loop(1, ITERS, sweep, phi)
    for g in range(nrow):
        psi_col[pl.ds(g * group, group), :] = psi_of(g, phi)
    psi_lane = jnp.concatenate(
        [to_lanes(psi_col[pl.ds(t * LANES, LANES), :]) for t in range(tiles)], axis=1
    )
    pick = lax.broadcasted_iota(jnp.int32, (own, total), 1) == (
        lax.broadcasted_iota(jnp.int32, (own, total), 0) + me * own
    )
    phi_own = jnp.sum(jnp.where(pick, phi, 0.0), axis=1, keepdims=True)
    psi_own = psi_col[mine, :][:, :1]
    q_t = pt_own[...] * (ht_own[...] + (psi_own + phi))
    mix = jnp.dot(q_t.astype(jnp.bfloat16), x_all[...], preferred_element_type=jnp.float32)
    w_phi = jnp.sum(w_all * phi, axis=1, keepdims=True)
    phi_row = jnp.sum(jnp.where(eye, phi_own, 0.0), axis=0, keepdims=True)
    gw_ref[...] = (-(total / w_sum) * (phi_row - w_phi / w_sum))[:, :own]

    for k in range(ncol):
        plane_g[k][0].wait_recv()
        plane_g[k][1].wait_recv()
        if k:
            plane_g[k][2].wait_recv()
    for c in zg[ncol - 1 :]:
        c.wait_recv()
    q_own = p_own[...] * (nt(x_own, gy_all[...]) + (phi_own + psi_lane))
    q_sum = jnp.sum(q_own, axis=1, keepdims=True)
    rowterm = jnp.dot(p_own[...].astype(jnp.bfloat16), gy_all[...], preferred_element_type=jnp.float32)
    mix = mix + jnp.dot(q_own.astype(jnp.bfloat16), x_all[...], preferred_element_type=jnp.float32)
    gp_ref[...] = (rowterm + (mix - q_sum * x_own.astype(jnp.float32)) * scale).astype(jnp.bfloat16)

    for c in zx + zg + pot_copies + sum_copies:
        c.wait_send()
    for sent in plane_x + plane_g:
        for c in sent:
            c.wait_send()


def local_fused(ncol, particles, cotangent, row_potential, col_potential, weights):
    own, width = particles.shape
    blocks = 4 * ncol
    total = own * blocks
    pot = jnp.pad(
        jnp.stack([row_potential, col_potential, weights]).astype(jnp.float32), ((0, 0), (0, LANES - own))
    ).reshape(1, 3 * LANES)
    pack = jnp.concatenate([particles, cotangent], axis=0)
    column = pltpu.VMEM((total, LANES), jnp.float32)
    strip = pltpu.VMEM((own, total), jnp.float32)
    line = pltpu.VMEM((1, total), jnp.float32)
    dma = pltpu.SemaphoreType.DMA
    vmem = pl.BlockSpec(memory_space=pltpu.VMEM)
    gp, gw = pl.pallas_call(
        functools.partial(fused_kernel, ncol, own),
        out_shape=(
            jax.ShapeDtypeStruct((own, width), jnp.bfloat16),
            jax.ShapeDtypeStruct((1, own), jnp.float32),
        ),
        in_specs=[vmem, vmem],
        out_specs=[vmem, vmem],
        scratch_shapes=[
            pltpu.VMEM((total, width), jnp.bfloat16),
            pltpu.VMEM((total, width), jnp.bfloat16),
            pltpu.VMEM((blocks, 1, 3 * LANES), jnp.float32),
            pltpu.VMEM((total, total), jnp.float32),
            column, column, column, column, column,
            line, line, line,
            pltpu.VMEM((SUBL, total), jnp.float32),
            pltpu.VMEM((blocks, 1, total + LANES), jnp.float32),
            strip, strip, strip,
            dma((2,)),
            dma((4 * (ncol - 1),)), dma((4 * (ncol - 1),)),
            dma((6 * ncol,)), dma((6 * ncol,)),
            dma((blocks - 1,)), dma((blocks - 1,)),
            dma((blocks - 1,)), dma((blocks - 1,)),
        ],
        compiler_params=pltpu.CompilerParams(
            collective_id=0, has_side_effects=True, vmem_limit_bytes=48 * 1024 * 1024
        ),
        cost_estimate=pl.CostEstimate(
            flops=3 * total * total * width, bytes_accessed=4 * own * width, transcendentals=total * total
        ),
    )(pack, pot)
    return gp, gw.reshape(own)


def solution(mesh):
    nrow, ncol = mesh.shape["row"], mesh.shape["col"]

    def local(particles, cotangent, row_potential, col_potential, weights):
        args = (particles, cotangent, row_potential, col_potential, weights)
        own = particles.shape[0]
        total = own * nrow * ncol
        fits = own % 32 == 0 and own <= LANES and own * ncol % LANES == 0
        if nrow == 4 and ncol > 1 and fits and 4 * total * total <= PLAN_BYTES:
            return local_fused(ncol, *args)
        return local_general(*args)

    return jax.shard_map(
        local,
        mesh=mesh,
        in_specs=(
            P(("filt", "row", "col"), None),
            P(("filt", "row", "col"), None),
            P(("filt", "row", "col")),
            P(("filt", "row", "col")),
            P(("filt", "row", "col")),
        ),
        out_specs=(P(("filt", "row", "col"), None), P(("filt", "row", "col"))),
        check_vma=False,
    )
```
